32 devices in a mesh: section: 2 (over core), dp: 4 (over z), ctx: 4 (over y, x).
Axes of the slice: x: 2, y: 2, z: 4, core: 2. Of those that a mesh axis runs over, the one named last changes fastest.
Arguments:
- tokens: bfloat16 [2, 4, 1024, 1536], P(None, 'dp', 'ctx'), may hold values from -6 to 6
- cotangent: bfloat16 [2, 4, 1024, 1536], P(None, 'dp', 'ctx'), may hold values from -6 to 6
- doc_lengths: int32 [2, 4, 4], P(None, 'dp'), may hold values from 1 to 896, 1024 in all within a row
- norm_gain: float32 [2, 1536], P('section'), may hold values from 0.5 to 1.5
- w_in: bfloat16 [2, 1536, 6448], P('section', ('dp', 'ctx')), may hold values from -0.15625 to 0.15625
- conv_weight: float32 [2, 4, 3328], P('section'), may hold values from -3 to 3
- conv_bias: float32 [2, 3328], P('section'), may hold values from -0.5 to 0.5
- dt_bias: float32 [2, 48], P('section'), may hold values from -6 to -1
- a_log: float32 [2, 48], P('section'), may hold values from -4 to 1.5
- d_skip: float32 [2, 48], P('section'), may hold values from 0.5 to 1.5
- inner_gain: float32 [2, 3072], P('section'), may hold values from 0.5 to 1.5
- w_out: bfloat16 [2, 3072, 1536], P('section', ('dp', 'ctx')), may hold values from -0.109375 to 0.109375
Outputs:
- hidden_states: bfloat16 [2, 2, 4, 1024, 1536], P('section', None, 'dp', 'ctx')
- input_grads: bfloat16 [2, 2, 4, 1024, 1536], P('section', None, 'dp', 'ctx')
- grad_norm_gain: float32 [2, 1536], P('section')
- grad_w_in: float32 [2, 1536, 6448], P('section', ('dp', 'ctx'))
- grad_conv_weight: float32 [2, 4, 3328], P('section')
- grad_conv_bias: float32 [2, 3328], P('section')
- grad_dt_bias: float32 [2, 48], P('section')
- grad_a_log: float32 [2, 48], P('section')
- grad_d_skip: float32 [2, 48], P('section')
- grad_inner_gain: float32 [2, 3072], P('section')
- grad_w_out: float32 [2, 3072, 1536], P('section', ('dp', 'ctx'))
The draws below stay inside these ranges and needn't reach their ends.
Inputs may be any that keep to these rules, and one draw needn't show every extreme that they name: `doc_lengths`: the 4 lengths of a row sum to 1024; in every row the longest is exactly 896.
All inputs are finite; a program needn't handle non-finite values.
Results may differ from the reference program's by a relative error of at most 0.013.
Values may be sent and summed in bfloat16 or wider, within the bound.
No kernel may reach another device: no remote copies, remote signals or barrier semaphores. Data moves between devices by JAX's collectives and lax.ppermute only.
A program may use at most 320 MiB of HBM per device.

```python
import math
import jax
import jax.numpy as jnp
import numpy as np
from jax import lax

D = 1536
HEADS = 48
HEAD = 64
STATE = 128
CONV = 4
GROUP = 256
MB = 2
DOCS = 4
INNER = 3072
CONV_DIM = 3328
PROJ = 6448
ROW_LEN = 1024
ROWS = 4
MOST = 896


def block_levels(key, shape, cuts, low, top_value):
    def one(axis_at, blocks):
        heights = jax.random.uniform(jax.random.fold_in(jax.random.fold_in(key, 6), axis_at), (blocks,), jnp.float32, low / len(cuts), top_value / len(cuts))
        return jnp.repeat(jnp.exp(heights), shape[axis_at] // blocks).reshape((-1,) + (1,) * (len(shape) - axis_at - 1))

    loudness = one(*cuts[0])
    for cut in cuts[1:]:
        loudness = loudness * one(*cut)
    return loudness


def split_up(amount, total, reach, lean):
    loads = [(1 << 20) // math.isqrt(standing ** lean) + 1 for standing in range(2, amount + 1)]
    rest, given = total - reach - (amount - 1), [1] * (amount - 1)
    while rest > 0:
        movable = [i for i in range(amount - 1) if given[i] < reach]
        pool, left = sum([loads[i] for i in movable]), rest
        for i in movable:
            extra = min(reach - given[i], max(1, left * loads[i] // pool), rest)
            given[i] = given[i] + extra
            rest = rest - extra
    return np.array([reach] + given)


def uneven_parts(own_key, number_of, total, bound, skew):
    if number_of == 2:
        one = jax.random.randint(own_key, (), max(1, total - bound), min(bound, total - 1) + 1)
        return jnp.stack([one, total - one])
    sizes = jnp.asarray(split_up(number_of, total, bound, skew), jnp.int32)
    twos = (number_of - 1) // 2
    giver, taker = sizes[1:1 + 2 * twos:2], sizes[2:2 + 2 * twos:2]
    margin = jnp.minimum(giver - 1, bound - taker)
    moved = jax.random.randint(jax.random.fold_in(own_key, 1), (twos,), 0, 1 << 20) % (margin + 1)
    sizes = sizes.at[1:1 + 2 * twos:2].set(giver - moved).at[2:2 + 2 * twos:2].set(taker + moved)
    return sizes[jax.random.permutation(jax.random.fold_in(own_key, 2), number_of)]


def bell_draw(key, extent, scale, limit, cuts=(), kind=jnp.bfloat16):
    entries = jax.random.normal(key, extent, jnp.float32) * scale
    if len(cuts) > 0:
        entries = block_levels(key, extent, cuts, -0.22, 0.18) * entries
    return jnp.clip(entries, min=-limit, max=limit).astype(kind)


def setup_inputs(seed: int = 0) -> dict:
    key_of = jax.random.split(jax.random.key(seed), 13)
    return {
        "tokens": bell_draw(key_of[0], (MB, ROWS, ROW_LEN, D), 1.0, 6.0, ((1, 4), (2, 4))),
        "cotangent": bell_draw(key_of[1], (MB, ROWS, ROW_LEN, D), 1.0, 6.0, ((1, 4), (2, 4))),
        "doc_lengths": jax.vmap(lambda own: uneven_parts(own, DOCS, ROW_LEN, MOST, 2))(jax.random.split(key_of[2], MB * ROWS)).reshape((MB, ROWS, DOCS)).astype(jnp.int32),
        "norm_gain": jnp.clip(1.0 + 0.1 * jax.random.normal(key_of[3], (2, D), jnp.float32), 0.5, 1.5),
        "w_in": bell_draw(key_of[4], (2, D, PROJ), D ** -0.5, 0.15625, ((0, 2), (1, 16))),
        "conv_weight": bell_draw(key_of[5], (2, CONV, CONV_DIM), 0.5, 3.0, ((0, 2),), jnp.float32),
        "conv_bias": jnp.clip(jax.random.uniform(key_of[6], (2, CONV_DIM), jnp.float32, -0.5, 0.5) * block_levels(key_of[6], (2, CONV_DIM), ((0, 2),), -0.4, 0.0), -0.5, 0.5),
        "dt_bias": jnp.clip(-6.0 + 5.0 * jax.random.uniform(key_of[7], (2, HEADS), jnp.float32) ** block_levels(key_of[7], (2, HEADS), ((0, 2),), -0.2, 0.2), -6.0, -1.0),
        "a_log": jnp.clip(-4.0 + 5.5 * jax.random.uniform(key_of[8], (2, HEADS), jnp.float32) ** block_levels(key_of[8], (2, HEADS), ((0, 2),), -0.2, 0.2), -4.0, 1.5),
        "d_skip": jnp.clip(0.5 + 1.0 * jax.random.uniform(key_of[9], (2, HEADS), jnp.float32) ** block_levels(key_of[9], (2, HEADS), ((0, 2),), -0.2, 0.2), 0.5, 1.5),
        "inner_gain": jnp.clip(1.0 + 0.1 * jax.random.normal(key_of[10], (2, INNER), jnp.float32), 0.5, 1.5),
        "w_out": bell_draw(key_of[11], (2, INNER, D), INNER ** -0.5, 0.109375, ((0, 2), (1, 16))),
    }


NORM_EPS = 1e-05
PRECISE = lax.Precision.HIGHEST

@jax.custom_vjp
def low(v):
    return lax.optimization_barrier(v.astype(jnp.bfloat16)).astype(jnp.float32)

@jax.custom_vjp
def low_back(v):
    return v

def low_keep(v):
    return (low(v), None)

def low_pass(kept, grad):
    return (grad,)

def back_keep(v):
    return (v, None)

def back_low(kept, grad):
    return (low(grad),)
low.defvjp(low_keep, low_pass)
low_back.defvjp(back_keep, back_low)

def norm_rows(rows_in, gain):
    return rows_in * lax.rsqrt(lax.optimization_barrier(jnp.mean(rows_in * rows_in, axis=-1, keepdims=True)) + NORM_EPS) * gain

def gate_norm(output, gate_in, inner_gain):
    return norm_rows(output * jax.nn.silu(gate_in), inner_gain)

def conv_mix(extended, flag_ext, conv_weight, conv_bias):
    length = extended.shape[0] - CONV + 1
    counts = jnp.cumsum(flag_ext)
    latest = counts[CONV - 1:]
    summed = jnp.zeros((length, extended.shape[1]), jnp.float32) + conv_bias[None, :]
    for offset in range(CONV):
        usable = jnp.where(counts[offset:offset + length] == latest, 1.0, 0.0)
        summed = summed + conv_weight[offset][None, :] * extended[offset:offset + length] * usable[:, None]
    return jax.nn.silu(summed)

def scan_block(states, pieces):
    values, key_rows, queries, stepsize, decay_log, flag_rows = pieces
    cumulative = jnp.cumsum(decay_log, axis=0)
    segment = jnp.cumsum(flag_rows)
    positions = jnp.arange(flag_rows.shape[0])
    inside = (segment[:, None] == segment[None, :]) & (positions[:, None] >= positions[None, :])
    spread = cumulative[:, None, :] - cumulative[None, :, :]
    damping = jnp.where(inside[:, :, None], jnp.exp(jnp.where(inside[:, :, None], spread, 0.0)), 0.0)
    scores = jnp.dot(queries, key_rows.T, precision=PRECISE)
    mixing = scores[:, :, None] * damping * stepsize[None, :, :]
    output = jnp.einsum('ijh,jhp->ihp', mixing, values, precision=PRECISE)
    carry_in = jnp.where((segment == 0.0)[:, None], jnp.exp(cumulative), 0.0)
    output = output + carry_in[:, :, None] * jnp.einsum('in,hpn->ihp', queries, states, precision=PRECISE)
    at_last = (segment == segment[-1])[:, None]
    tail_weight = jnp.where(at_last, jnp.exp(jnp.where(at_last, cumulative[-1][None, :] - cumulative, 0.0)), 0.0) * stepsize
    passed = jnp.where(segment[-1] == 0.0, jnp.exp(cumulative[-1]), 0.0)
    states = passed[:, None, None] * states + jnp.einsum('jh,jhp,jn->hpn', tail_weight, values, key_rows, precision=PRECISE)
    return (states, output)

def core_from_mixed(mixed_rows, step_raw, dt_bias, a_log, d_skip, flag_rows, start_state):
    length = mixed_rows.shape[0]
    values = mixed_rows[:, :INNER].reshape(length, HEADS, HEAD)
    key_rows = mixed_rows[:, INNER:INNER + STATE]
    queries = mixed_rows[:, INNER + STATE:]
    stepsize = jax.nn.softplus(step_raw + dt_bias)
    decay_log = -stepsize * jnp.exp(a_log)
    group_count = length // GROUP

    def shaped(tensor):
        return tensor.reshape((group_count, GROUP) + tensor.shape[1:])
    end_state, output = lax.scan(jax.checkpoint(scan_block), start_state, (shaped(values), shaped(key_rows), shaped(queries), shaped(stepsize), shaped(decay_log), shaped(flag_rows)))
    output = output.reshape(length, HEADS, HEAD) + d_skip[None, :, None] * values
    return (output.reshape(length, INNER), end_state)

def layer_row(hidden, flag_row, params):
    norm_gain, w_in, conv_weight, conv_bias, dt_bias, a_log, d_skip, inner_gain, w_out = params
    residual = low_back(hidden)
    normed = low(norm_rows(residual, norm_gain))
    project = low_back(jnp.dot(normed, w_in, precision=PRECISE))
    gate_in = project[:, :INNER]
    conv_in = low(project[:, INNER:INNER + CONV_DIM])
    step_raw = project[:, INNER + CONV_DIM:]
    extended = jnp.concatenate([jnp.zeros((CONV - 1, CONV_DIM), jnp.float32), conv_in], axis=0)
    flag_ext = jnp.concatenate([jnp.zeros((CONV - 1,), jnp.float32), flag_row])
    mixed_rows = conv_mix(extended, flag_ext, conv_weight, conv_bias)
    start_state = jnp.zeros((HEADS, HEAD, STATE), jnp.float32)
    output, end_state = core_from_mixed(mixed_rows, step_raw, dt_bias, a_log, d_skip, flag_row, start_state)
    gated_rows = low(gate_norm(output, gate_in, inner_gain))
    return low(residual + jnp.dot(gated_rows, w_out, precision=PRECISE))

def section_layer(hidden, flag_all, params):
    flat_rows = hidden.reshape(MB * ROWS, ROW_LEN, D)
    flat_flags = flag_all.reshape(MB * ROWS, ROW_LEN)

    def one_row(row_pair):
        return jax.checkpoint(layer_row)(row_pair[0], row_pair[1], params)
    return lax.map(one_row, (flat_rows, flat_flags)).reshape(hidden.shape)

def reference(tokens, cotangent, doc_lengths, norm_gain, w_in, conv_weight, conv_bias, dt_bias, a_log, d_skip, inner_gain, w_out):
    bounds = (jnp.cumsum(doc_lengths, axis=-1) - doc_lengths).astype(jnp.int32)
    positions = jnp.arange(ROW_LEN, dtype=jnp.int32)
    flag_all = jnp.where(jnp.any(positions[None, None, :, None] == bounds[:, :, None, :], axis=-1), 1.0, 0.0).astype(jnp.float32)
    weights = (norm_gain, w_in, conv_weight, conv_bias, dt_bias, a_log, d_skip, inner_gain, w_out)
    first_params = tuple((tensor[0].astype(jnp.float32) for tensor in weights))
    second_params = tuple((tensor[1].astype(jnp.float32) for tensor in weights))

    def run_section(hidden, params):
        return section_layer(hidden, flag_all, params)
    middle, back_first = jax.vjp(run_section, tokens.astype(jnp.float32), first_params)
    last_hidden, back_second = jax.vjp(run_section, middle, second_params)
    grad_middle, grads_second = back_second(cotangent.astype(jnp.float32))
    grad_tokens, grads_first = back_first(grad_middle)
    hidden_states = jnp.stack([middle, last_hidden]).astype(jnp.bfloat16)
    input_grads = jnp.stack([grad_tokens, grad_middle]).astype(jnp.bfloat16)
    stacked = tuple((jnp.stack([from_first, from_second]).astype(jnp.float32) for from_first, from_second in zip(grads_first, grads_second)))
    return (hidden_states, input_grads, stacked[0], stacked[1], stacked[2], stacked[3], stacked[4], stacked[5], stacked[6], stacked[7], stacked[8])
```

```python
import functools

import jax
import jax.numpy as jnp
from jax import lax
from jax.experimental import pallas as pl
from jax.experimental.pallas import tpu as pltpu
from jax.sharding import PartitionSpec as P

HEADS = 48
HEAD = 64
STATE = 128
CONV = 4
INNER = 3072
CONV_DIM = 3328
NORM_EPS = 1e-05

F32 = jnp.float32
BF16 = jnp.bfloat16
HIGH = lax.Precision.HIGHEST
CTX = 4
SEGS = 2
LOCAL = HEADS // CTX
WIDE = LOCAL * HEAD
MIX = WIDE + 2 * STATE
FULL = MIX + 128
HALF = WIDE // 2
LOAD = HALF + STATE + 128
PACK = 24
MIB = 1024 * 1024


def swap_core(x):
    return lax.ppermute(x, "section", [(0, 1), (1, 0)])


def flip(x, bits):
    return lax.ppermute(x, "ctx", [(i, i ^ bits) for i in range(CTX)])


def gather_slots(order, own, extra=0):
    half = (own.shape[0] - extra) // 2
    x, y = flip(own, 1), flip(own, 2)

    def forward():
        order.after((x, y))
        first, second = order.now(y[: extra + half]), order.now(x[extra + half :])
        return [own, x, y, flip(first, 1), flip(second, 2)]

    return forward


def scatter_start(own, to_x, to_y, late_x, late_y):
    return own, flip(to_x, 1), flip(to_y, 2), late_x, late_y


def scatter_slots(order, own, from_x, from_y, late_x, late_y):
    extra = from_x.shape[0] - 2 * late_x.shape[0]
    outs = [shape((late_x.shape[0] + extra, late_x.shape[1]), BF16), late_y]
    late_x, late_y = order(call_with("turn", turn_kernel, [from_x, from_y, late_x, late_y], outs))
    return [own, from_x, from_y, flip(late_x, 1), flip(late_y, 2)]


def from_all(x):
    return [x] + [flip(x, m) for m in range(1, CTX)]


def dot(a, b, dims, precision=None):
    return lax.dot_general(a, b, (dims, ((), ())), precision=precision, preferred_element_type=F32)


AB = ((1,), (0,))
ABT = ((1,), (1,))
ATB = ((0,), (0,))


def call_with(name, kernel, ins, outs):
    return lambda sp: call(name, kernel, sp, ins, outs)


def whole(x):
    zeros = (0,) * len(x.shape)
    return pl.BlockSpec(tuple(x.shape), lambda i, sp: zeros)


def shape(dims, dtype):
    return jax.ShapeDtypeStruct(dims, dtype)


def call(name, kernel, sp, ins, outs, vmem=20, grid=1, scratch=()):
    ins = [x if isinstance(x, tuple) else (x, whole(x)) for x in ins]
    outs = [x if isinstance(x, tuple) else (x, whole(x)) for x in outs]
    return pl.pallas_call(
        kernel,
        grid_spec=pltpu.PrefetchScalarGridSpec(
            num_scalar_prefetch=1,
            grid=(grid,),
            in_specs=[spec for _, spec in ins],
            out_specs=[spec for _, spec in outs],
            scratch_shapes=list(scratch),
        ),
        out_shape=[x for x, _ in outs],
        compiler_params=pltpu.CompilerParams(
            dimension_semantics=("arbitrary",), vmem_limit_bytes=vmem * MIB
        ),
        cost_estimate=pl.CostEstimate(flops=1, bytes_accessed=1, transcendentals=0),
        name=name,
    )(sp, *[x for x, _ in ins])


def natural_spec(x, seg, slot):
    def at(i, sp):
        inside = slot ^ sp[0]
        return (2 * seg + (inside >> 1)) ^ sp[0], inside & 1, 0, 0

    return pl.BlockSpec((1, 1) + x.shape[2:], at)


def natural_slots(x, seg):
    return [(x, natural_spec(x, seg, m)) for m in range(CTX)]


def load_rows(refs, extra=0):
    first = 0
    for n, ref in enumerate(refs):
        value = ref[...]
        value = value.reshape(value.shape[-2:])
        if extra and n < 4:
            value = value[extra:]
        yield first, value
        first += value.shape[0]


def row_scale(x):
    return lax.rsqrt(jnp.mean(x * x, axis=-1, keepdims=True) + NORM_EPS)


def project_kernel(count, sp, *refs):
    cw_ref, wc_ref, normed_ref, conv_ref, step_ref = refs[count:]
    gain = cw_ref[8:9, :]
    for first, x in load_rows(refs[:count]):
        x = x.astype(F32)
        rows = pl.ds(first, x.shape[0])
        normed_ref[rows, :] = (x * row_scale(x) * gain).astype(BF16)
    normed = normed_ref[...]
    conv_ref[...] = dot(normed, wc_ref[:, :MIX], AB).astype(BF16)
    step_ref[...] = dot(normed, wc_ref[:, MIX:], AB)


def project(sp, pieces, cw, wc, tokens):
    return call(
        "project",
        functools.partial(project_kernel, len(pieces)),
        sp,
        pieces + [cw, wc],
        [
            shape((tokens, wc.shape[0]), BF16),
            shape((tokens, MIX), BF16),
            shape((tokens, 128), F32),
        ],
    )


def bounds_of(sp):
    return [sp[3 + d] for d in range(sp.shape[0] - 3)]


def distances(sp, first, rows):
    at = lax.broadcasted_iota(jnp.int32, (rows, 1), 0) + first
    since = at
    for bound in bounds_of(sp):
        gap = at - bound
        since = jnp.where(gap >= 0, jnp.minimum(since, gap), since)
    return since


def segment(sp, at):
    total = jnp.zeros_like(at)
    for bound in bounds_of(sp):
        total = total + jnp.where(at >= bound, 1, 0)
    return total


def pair_lanes(a, pair):
    rows = a.shape[0]
    low = lax.broadcasted_iota(jnp.int32, (rows, 2 * HEAD), 1) < HEAD
    first = jnp.broadcast_to(a[:, 2 * pair : 2 * pair + 1], (rows, 2 * HEAD))
    second = jnp.broadcast_to(a[:, 2 * pair + 1 : 2 * pair + 2], (rows, 2 * HEAD))
    return jnp.where(low, first, second)


def conv_forward(ext, cw_ref, since, cols, q):
    total = cw_ref[4:5, cols] + cw_ref[3:4, cols] * ext[8 : 8 + q, cols]
    for shift in range(1, CONV):
        tap = cw_ref[3 - shift : 4 - shift, cols]
        rows = ext[8 - shift : 8 - shift + q, cols]
        total = total + jnp.where(since >= shift, tap * rows, 0.0)
    return total


def block_terms(sp, first, q, raw, cw_ref):
    row = lax.broadcasted_iota(jnp.int32, (q, 1), 0)
    col = lax.broadcasted_iota(jnp.int32, (1, q), 1)
    seg_col, seg_row = segment(sp, row + first), segment(sp, col + first)
    seg_before, seg_last = jnp.int32(0), jnp.int32(0)
    for bound in bounds_of(sp):
        seg_before = seg_before + jnp.where(first - 1 >= bound, 1, 0)
        seg_last = seg_last + jnp.where(first + q - 1 >= bound, 1, 0)
    same = seg_col == seg_row
    shifted = raw + cw_ref[10:11, 0:128]
    stepsize = jax.nn.softplus(shifted)
    decay = -stepsize * cw_ref[11:12, 0:128]
    lower = jnp.where(row >= col, 1.0, 0.0)
    cum = dot(lower, decay, AB, HIGH)
    last = cum[q - 1 : q, :]
    open_w = jnp.where(seg_col == seg_before, jnp.exp(cum), 0.0)
    tail = jnp.where(seg_col == seg_last, jnp.exp(jnp.minimum(last - cum, 0.0)), 0.0)
    passed = jnp.where(seg_last == seg_before, jnp.exp(last), 0.0)
    return row, col, same, shifted, stepsize, decay, cum, open_w, tail, passed


def pair_cols(pair):
    return slice(2 * HEAD * pair, 2 * HEAD * (pair + 1))


def scan_kernel(
    seg,
    sp,
    ci_ref,
    raw_ref,
    cw_ref,
    st_in_ref,
    tail_in_ref,
    y_ref,
    st_ref,
    st_out_ref,
    tail_out_ref,
    ext,
    mix,
    state,
    flow,
    fresh,
):
    k = pl.program_id(0)
    q = ci_ref.shape[0]
    first = (CTX * seg + k) * q

    @pl.when(k == 0)
    def _():
        state[...] = st_in_ref[...]
        ext[0:8, :] = tail_in_ref[...].astype(F32)[8:16, :]

    ci = ci_ref[...]
    tail_out_ref[...] = ci[q - 16 : q, :]
    ext[8 : 8 + q, :] = ci.astype(F32)
    since = distances(sp, first, q)
    for c in range(0, MIX, 128):
        cols = slice(c, c + 128)
        pre = conv_forward(ext, cw_ref, since, cols, q)
        mix[:, cols] = pre * jax.nn.sigmoid(pre)
    ext[0:8, :] = ext[q : q + 8, :]

    row, col, same, _, stepsize, _, cum, open_w, tail, passed = block_terms(
        sp, first, q, raw_ref[...], cw_ref
    )
    cum_t = cum.T
    keys = mix[:, WIDE : WIDE + STATE]
    kb = keys.astype(BF16)
    kt = keys.T.astype(BF16)
    qb = mix[:, WIDE + STATE :].astype(BF16)
    scores = jnp.where(same & (row >= col), dot(qb, kb, ABT), 0.0)
    st_ref[...] = state[...]
    flow[...] = dot(qb, state[...].astype(BF16), AB)
    low = lax.broadcasted_iota(jnp.int32, (q, 2 * HEAD), 1) < HEAD
    tail = tail * stepsize
    for pair in range(LOCAL // 2):
        cols = pair_cols(pair)
        v = mix[:, cols]
        vs = (v * pair_lanes(stepsize, pair)).astype(BF16)
        outs = []
        for h in (2 * pair, 2 * pair + 1):
            damp = jnp.exp(jnp.minimum(cum[:, h : h + 1] - cum_t[h : h + 1, :], 0.0))
            outs.append(dot((scores * damp).astype(BF16), vs, AB))
        inflow = flow[:, cols] * pair_lanes(open_w, pair)
        y = jnp.where(low, outs[0], outs[1]) + inflow + cw_ref[5:6, cols] * v
        y_ref[:, cols] = y.astype(BF16)
        fresh[:, cols] = (v * pair_lanes(tail, pair)).astype(BF16)
    update = dot(kt, fresh[...], AB)
    for pair in range(LOCAL // 2):
        cols = pair_cols(pair)
        state[:, cols] = state[:, cols] * pair_lanes(passed, pair) + update[:, cols]
    st_out_ref[...] = state[...]


def scan_rows(sp, seg, conv_in, step_raw, cw, state, tail):
    q = conv_in.shape[0] // CTX

    def here(x):
        return x, pl.BlockSpec((q, x.shape[1]), lambda k, sp: (k ^ sp[0], 0))

    tokens = conv_in.shape[0]
    states = shape((CTX * STATE, WIDE), F32)
    return call(
        "scan_rows",
        functools.partial(scan_kernel, seg),
        sp,
        [here(conv_in), here(step_raw), cw, state, tail],
        [
            here(shape((tokens, WIDE), BF16)),
            (states, pl.BlockSpec((STATE, WIDE), lambda k, sp: (k, 0))),
            shape((STATE, WIDE), F32),
            shape((16, MIX), BF16),
        ],
        16,
        grid=CTX,
        scratch=[
            pltpu.VMEM((q + 8, MIX), F32),
            pltpu.VMEM((q, MIX), F32),
            pltpu.VMEM((STATE, WIDE), F32),
            pltpu.VMEM((q, WIDE), F32),
            pltpu.VMEM((q, WIDE), BF16),
        ],
    )


def stat_rows(columns):
    rows = columns[0].shape[0]
    lane = lax.broadcasted_iota(jnp.int32, (rows, 128), 1)
    table = jnp.zeros((rows, 128), F32)
    for i, column in enumerate(columns):
        table = jnp.where(lane == i, column, table)
    return table.T[0:8, :]


def stat_columns(rows):
    return jnp.concatenate([rows, jnp.zeros((120, rows.shape[1]), F32)]).T


def split_rows(row, cols):
    high = row.astype(BF16).astype(F32)
    middle = (row - high).astype(BF16).astype(F32)
    low = row - high - middle
    sub = lax.broadcasted_iota(jnp.int32, (16, row.shape[1]), 0)
    tile = jnp.where(sub == 0, high, jnp.where(sub == 1, middle, jnp.where(sub == 2, low, 0.0)))
    spare = jnp.zeros((16, cols - row.shape[1]), F32)
    return jnp.concatenate([tile, spare], axis=1).astype(BF16)


def stat_row(ref, row, count):
    if ref.dtype == F32:
        return ref[row : row + 1, :count]
    tile = ref[...].astype(F32)
    return tile[0:1, :count] + tile[1:2, :count] + tile[2:3, :count]


def store_slots(part, stat, part_refs):
    own_ref, x_ref, y_ref, late_x_ref, late_y_ref = part_refs
    q = own_ref.shape[0]
    half = q // 2
    part = part.astype(BF16)
    own_ref[...] = part[:q]
    x_ref[:half, :] = part[3 * q : 3 * q + half]
    x_ref[half:q, :] = part[q : q + half]
    y_ref[:half, :] = part[3 * q + half :]
    y_ref[half:q, :] = part[2 * q + half : 3 * q]
    late_x_ref[...] = part[q + half : 2 * q]
    late_y_ref[...] = part[2 * q : 2 * q + half]
    if stat is not None:
        tile = split_rows(stat, part.shape[1])
        x_ref[q:, :] = tile
        y_ref[q:, :] = tile


def store_part(part, stat, part_refs):
    if len(part_refs) == 1:
        part_refs[0][...] = part.astype(BF16)
    else:
        store_slots(part, stat, part_refs)


def part_shapes(slots, tokens, d, extra=0):
    if not slots:
        return [shape((tokens, d), BF16)]
    q = tokens // CTX
    sent = shape((q + extra, d), BF16)
    return [shape((q, d), BF16), sent, sent] + [shape((q // 2, d), BF16)] * 2


def tail_tile(x):
    return x, pl.BlockSpec((16, x.shape[1]), lambda i, sp: (x.shape[0] // 16 - 1, 0))


def head_tile(x):
    return x, pl.BlockSpec((16, x.shape[1]), lambda i, sp: (0, 0))


def turn_kernel(sp, from_x_ref, from_y_ref, late_x_ref, late_y_ref, x_ref, y_ref):
    half = y_ref.shape[0]
    x_ref[:half, :] = (late_x_ref[...].astype(F32) + from_y_ref[:half, :].astype(F32)).astype(BF16)
    y_ref[...] = (late_y_ref[...].astype(F32) + from_x_ref[:half, :].astype(F32)).astype(BF16)
    if x_ref.shape[0] > half:
        x_ref[half:, :] = from_y_ref[2 * half :, :]


def out_kernel(count, before, sp, *refs):
    if before:
        before_ref, refs = refs[0], refs[1:]
    normed_ref, y_ref, cw_ref, wg_ref, wo_ref = refs[count : count + 5]
    gate_ref, stat_ref = refs[count + 5 : count + 7]
    gate = dot(normed_ref[...], wg_ref[...], AB)
    gate_ref[...] = gate.astype(BF16)
    g = y_ref[...].astype(F32) * gate * jax.nn.sigmoid(gate)
    part = dot((g * cw_ref[9:10, :WIDE]).astype(BF16), wo_ref[...], AB)
    square = jnp.sum(g * g, axis=-1, keepdims=True)
    inner = [
        jnp.sum(part[first : first + u.shape[0]] * u.astype(F32), axis=-1, keepdims=True)
        for first, u in load_rows(refs[:count])
    ]
    rows = stat_rows([square] + ([jnp.concatenate(inner)] if inner else []))
    store_part(part, rows[0:1, :], refs[count + 7 :])
    if before:
        rows = jnp.concatenate([before_ref[...], rows])
    stat_ref[...] = rows


def out_rows(sp, slots, before, pieces, normed, y, cw, wg, wo):
    tokens, d = normed.shape
    return call(
        "out_rows",
        functools.partial(out_kernel, len(pieces), len(before)),
        sp,
        before + pieces + [normed, y, cw, wg, wo],
        [shape((tokens, WIDE), BF16), shape((8 + 8 * len(before), tokens), F32)] + part_shapes(slots, tokens, d, 16),
        28,
    )


def slot_sums(stat_refs, row, q):
    out = []
    for slot in range(CTX):
        total = 0.0
        for m, ref in enumerate(stat_refs):
            total = total + stat_row(ref, row, CTX * q)[:, (slot ^ m) * q : (slot ^ m) * q + q]
        out.append(total)
    return jnp.concatenate(out, axis=1)


def own_sum(refs):
    own, from_x, from_y, late_x, late_y = [ref[...].astype(F32) for ref in refs]
    half = late_y.shape[0]
    x = jnp.concatenate([from_x[half : 2 * half], late_x[:half]])
    return own + x + jnp.concatenate([late_y, from_y[half : 2 * half]])


def own_squares(stats, sp, natural, q):
    if not natural:
        rows = [stat_row(ref, 0, CTX * q) for ref in stats]
        return sum(row[:, m * q : m * q + q] for m, row in enumerate(rows))
    place, out = sp[0], []
    block = q // 2
    for half in range(2):
        total = jnp.zeros((1, block), F32)
        for s in range(SEGS):
            for slot in range(CTX):
                here = ((place >> 1) == s) & ((slot ^ place) == 2 * (place & 1) + half)
                for m, ref in enumerate(stats):
                    value = ref[8 * s : 8 * s + 1, pl.ds((slot ^ m) * block, block)]
                    total = total + jnp.where(here, value, 0.0)
        out.append(total)
    return jnp.concatenate(out, axis=1)


def own_kernel(count, natural, sp, *refs):
    stats, partial = refs[:CTX], refs[CTX : CTX + 5]
    residual = jnp.concatenate([x for _, x in load_rows(refs[CTX + 5 : CTX + 5 + count])])
    own_ref, branch_ref = refs[CTX + 5 + count :]
    square = own_squares(stats, sp, natural, own_ref.shape[0])
    square = jnp.concatenate([square, jnp.zeros((7, square.shape[1]), F32)])
    scale = lax.rsqrt(stat_columns(square)[:, 0:1] / INNER + NORM_EPS)
    branch = own_sum(partial) * scale
    branch_ref[...] = branch
    own_ref[...] = (residual.astype(F32) + branch).astype(BF16)


def own_rows(sp, natural, stats, partial, residual):
    q, d = partial[0].shape
    return call(
        "own_rows",
        functools.partial(own_kernel, len(residual), natural),
        sp,
        stats + partial + residual,
        [shape((q, d), BF16), shape((q, d), F32)],
        16,
    )


def collect_kernel(sp, part0_ref, part1_ref, own_ref, x_ref, y_ref, late_x_ref, late_y_ref):
    place = sp[0]
    q = late_x_ref.shape[0]
    goals = [
        [own_ref.at[pl.ds(0, q)], own_ref.at[pl.ds(q, q)]],
        [x_ref.at[pl.ds(q, q)], late_x_ref],
        [late_y_ref, y_ref.at[pl.ds(q, q)]],
        [x_ref.at[pl.ds(0, q)], y_ref.at[pl.ds(0, q)]],
    ]
    for m in range(CTX):
        owner = place ^ m
        for half in range(2):
            slot = (2 * (owner & 1) + half) ^ place
            rows = pl.ds(pl.multiple_of(slot * q, q), q)
            goals[m][half][...] = choose((owner >> 1) == 0, part0_ref[rows, :], part1_ref[rows, :])


def collect(sp, parts):
    tokens, d = parts[0].shape
    return call("collect", collect_kernel, sp, list(parts), part_shapes(True, 2 * tokens, d), 20)


def natural_kernel(extra, sp, *refs):
    out_ref = refs[-1]
    q = out_ref.shape[0] // 2
    for place in range(CTX):
        s = place >> 1
        own, x, y, first, second = refs[5 * s : 5 * s + 5]

        @pl.when(sp[0] == place)
        def _():
            for half in range(2):
                slot = (2 * (place & 1) + half) ^ place
                at = half * q
                if slot < 3:
                    out_ref[at : at + q, :] = (own, x, y)[slot][extra:, :]
                else:
                    out_ref[at : at + q // 2, :] = first[extra:, :]
                    out_ref[at + q // 2 : at + q, :] = second[...]


def natural_rows(sp, pieces, extra=0):
    q, d = pieces[0][0].shape
    ins = [x for one in pieces for x in one]
    kernel = functools.partial(natural_kernel, extra)
    return call("natural_rows", kernel, sp, ins, [shape((2 * (q - extra), d), BF16)])[0]


def gate_back_kernel(count, inners, first_stat, sp, *refs):
    pieces, stats = refs[:count], refs[count : count + CTX]
    inner_refs = refs[count + CTX : count + CTX + inners]
    rest = refs[count + CTX + inners :]
    y_ref, gate_ref, cw_ref, wo_ref, dy_ref, dgate_ref, gated_ref, u_ref, dgain_ref = rest
    gain = cw_ref[9:10, :WIDE]
    tokens = y_ref.shape[0]
    q = tokens // CTX
    for first, u in load_rows(pieces, 16 if inners else 0):
        u_ref[pl.ds(first, u.shape[0]), :] = u
    back = dot(u_ref[...], wo_ref[...], ABT)
    scale = lax.rsqrt(slot_sums(stats, first_stat, q) / INNER + NORM_EPS)
    if inners:
        inner = jnp.concatenate([stat_row(ref, 0, q) for ref in inner_refs], axis=1)
    else:
        inner = slot_sums(stats, first_stat + 1, q) * scale
    pull = scale * scale * inner / INNER
    table = stat_columns(jnp.concatenate([scale, pull, jnp.zeros((6, tokens), F32)]))
    scale, pull = table[:, 0:1], table[:, 1:2]
    gate = gate_ref[...].astype(F32)
    y = y_ref[...].astype(F32)
    sig = jax.nn.sigmoid(gate)
    act = gate * sig
    g = y * act
    unit = g * scale
    gated_ref[...] = (unit * gain).astype(BF16)
    dg = back * gain * scale - g * pull
    dy_ref[...] = (dg * act).astype(BF16)
    dgate_ref[...] = (dg * y * (sig + act * (1.0 - sig))).astype(BF16)
    dgain_ref[...] = jnp.broadcast_to(jnp.sum(back * unit, axis=0, keepdims=True), (8, WIDE))


def gate_back(sp, pieces, stats, first_stat, inners, y, gate, cw, wo):
    tokens, d = y.shape[0], wo.shape[1]
    return call(
        "gate_back",
        functools.partial(gate_back_kernel, len(pieces), len(inners), first_stat),
        sp,
        pieces + stats + inners + [y, gate, cw, wo],
        [shape((tokens, WIDE), BF16)] * 3 + [shape((tokens, d), BF16), shape((8, WIDE), F32)],
        28,
    )


def scan_back_kernel(
    seg,
    sp,
    ci_ref,
    prev_ref,
    raw_ref,
    dy_ref,
    st_ref,
    tail_in_ref,
    cw_ref,
    dst_in_ref,
    next_in_ref,
    dci_ref,
    dcw_ref,
    dhp_ref,
    dst_out_ref,
    next_out_ref,
    ext,
    mix,
    slope,
    dext,
    dstate,
    tails,
    dyw,
    flow,
    kept_all,
    ends,
):
    i = pl.program_id(0)
    k = CTX - 1 - i
    q = ci_ref.shape[0]
    first = (CTX * seg + k) * q

    @pl.when(i == 0)
    def _():
        dstate[...] = dst_in_ref[...]
        dext[q : q + 8, :] = next_in_ref[...]
        ends[...] = jnp.zeros_like(ends)
        dcw_ref[...] = jnp.zeros_like(dcw_ref)
        dhp_ref[...] = jnp.zeros_like(dhp_ref)

    @pl.when(k == 0)
    def _():
        ext[0:8, :] = tail_in_ref[...].astype(F32)[8:16, :]

    @pl.when(k > 0)
    def _():
        ext[0:8, :] = prev_ref[...].astype(F32)[8:16, :]

    ext[8 : 8 + q, :] = ci_ref[...].astype(F32)
    since = distances(sp, first, q + 8)
    for c in range(0, MIX, 128):
        cols = slice(c, c + 128)
        pre = conv_forward(ext, cw_ref, since[0:q], cols, q)
        sig = jax.nn.sigmoid(pre)
        act = pre * sig
        mix[:, cols] = act
        slope[:, cols] = sig + act * (1.0 - sig)

    row, col, same, shifted, stepsize, decay, cum, open_w, tail, passed = block_terms(
        sp, first, q, raw_ref[...], cw_ref
    )
    cum_t = cum.T
    kb = mix[:, WIDE : WIDE + STATE].astype(BF16)
    queries = mix[:, WIDE + STATE :]
    qb = queries.astype(BF16)
    qt = queries.T.astype(BF16)
    inside = same & (col >= row)
    scores = jnp.where(inside, dot(kb, qb, ABT), 0.0)
    stb, dstb = st_ref[...].astype(BF16), dstate[...].astype(BF16)
    flow[...] = dot(qb, stb, AB)
    kept_all[...] = dot(kb, dstb, AB)
    low = lax.broadcasted_iota(jnp.int32, (q, 2 * HEAD), 1) < HEAD
    lane = lax.broadcasted_iota(jnp.int32, (q, 128), 1)
    sub = lax.broadcasted_iota(jnp.int32, (16, q), 0)
    dscores = jnp.zeros((q, q), F32)
    plus_t = jnp.zeros((16, q), F32)
    dstep = jnp.zeros((q, 128), F32)
    dcum = jnp.zeros((q, 128), F32)
    for pair in range(LOCAL // 2):
        cols = pair_cols(pair)
        v = mix[:, cols]
        step_e = pair_lanes(stepsize, pair)
        vs = v * step_e
        vsb = vs.astype(BF16)
        dyb = dy_ref[:, cols]
        dyf = dyb.astype(F32)
        dvs = []
        for side, h in ((0, 2 * pair), (1, 2 * pair + 1)):
            mine = low if side == 0 else ~low
            damp = jnp.exp(jnp.minimum(cum_t[h : h + 1, :] - cum[:, h : h + 1], 0.0))
            raw = dot(jnp.where(mine, vs, 0.0).astype(BF16), dyb, ABT)
            mixing = (scores * damp).astype(BF16)
            dscores = dscores + raw * damp
            both = raw * mixing.astype(F32)
            plus_t = plus_t + jnp.where(sub == h, jnp.sum(both, axis=0, keepdims=True), 0.0)
            dvs.append(dot(mixing, dyb, AB))
        dv = jnp.where(low, dvs[0], dvs[1])
        weighted = dyf * pair_lanes(open_w, pair)
        dyw[:, cols] = weighted.astype(BF16)
        tail_e = pair_lanes(tail, pair)
        kept = kept_all[:, cols] * tail_e
        tails[:, cols] = (vs * tail_e).astype(BF16)
        u = dv + kept
        dext[0:q, cols] = (u * step_e + cw_ref[5:6, cols] * dyf) * slope[:, cols]
        from_tail = kept * vs
        dcw_ref[5:6, cols] += jnp.sum(dyf * v, axis=0, keepdims=True)
        ends[1:2, cols] = jnp.sum(from_tail, axis=0, keepdims=True)
        uv = u * v
        change = weighted * flow[:, cols] - dv * vsb.astype(F32) - from_tail
        for side, h in ((0, 2 * pair), (1, 2 * pair + 1)):
            mine = low if side == 0 else ~low

            def per_row(x):
                return jnp.sum(jnp.where(mine, x, 0.0), axis=1, keepdims=True)

            dstep = jnp.where(lane == h, per_row(uv), dstep)
            dcum = jnp.where(lane == h, per_row(change), dcum)

    dcum = dcum + jnp.concatenate([plus_t, jnp.zeros((112, q), F32)]).T
    ends[0:1, :] = jnp.sum(st_ref[...] * dstate[...], axis=0, keepdims=True)
    by_head = dot(ends[...], channel_map(), AB, HIGH)
    at_end = by_head[0:1, :] * passed + by_head[1:2, :]
    dcum = dcum + jnp.where(row == q - 1, at_end, 0.0)
    upper = jnp.where(col >= row, 1.0, 0.0)
    ddecay = dot(upper, dcum, AB, HIGH)
    draw = (dstep - ddecay * cw_ref[11:12, 0:128]) * jax.nn.sigmoid(shifted)
    dci_ref[:, MIX:] = draw.astype(BF16)
    dhp_ref[0:1, :] += jnp.sum(draw, axis=0, keepdims=True)
    dhp_ref[1:2, :] += jnp.sum(ddecay * decay, axis=0, keepdims=True)

    dsb = jnp.where(inside, dscores, 0.0).astype(BF16)
    dkeys = dot(dsb, qb, AB) + dot(tails[...], dstb, ABT)
    dqueries = dot(dsb, kb, ATB) + dot(dyw[...], stb, ABT)
    kcols, qcols = slice(WIDE, WIDE + STATE), slice(WIDE + STATE, MIX)
    dext[0:q, kcols] = dkeys * slope[:, kcols]
    dext[0:q, qcols] = dqueries * slope[:, qcols]
    update = dot(qt, dyw[...], AB)
    for pair in range(LOCAL // 2):
        cols = pair_cols(pair)
        dstate[:, cols] = dstate[:, cols] * pair_lanes(passed, pair) + update[:, cols]
    dst_out_ref[...] = dstate[...]

    for c in range(0, MIX, 128):
        cols = slice(c, c + 128)
        here = dext[0:q, cols]
        total = cw_ref[3:4, cols] * here
        dcw_ref[3:4, cols] += jnp.sum(here * ext[8 : 8 + q, cols], axis=0, keepdims=True)
        dcw_ref[4:5, cols] += jnp.sum(here, axis=0, keepdims=True)
        for shift in range(1, CONV):
            later = jnp.where(since[shift : shift + q] >= shift, dext[shift : shift + q, cols], 0.0)
            total = total + cw_ref[3 - shift : 4 - shift, cols] * later
            used = jnp.where(since[0:q] >= shift, ext[8 - shift : 8 - shift + q, cols], 0.0)
            dcw_ref[3 - shift : 4 - shift, cols] += jnp.sum(here * used, axis=0, keepdims=True)
        dci_ref[:, cols] = total.astype(BF16)
    head_rows = dext[0:8, :]
    dext[q : q + 8, :] = head_rows
    next_out_ref[...] = head_rows


def scan_back(sp, seg, conv_in, step_raw, dy, states, tail, cw, dstate, following):
    tokens = conv_in.shape[0]
    q = tokens // CTX

    def here(x):
        return x, pl.BlockSpec((q, x.shape[1]), lambda i, sp: ((CTX - 1 - i) ^ sp[0], 0))

    def before(i, sp):
        return (jnp.maximum(CTX - 2 - i, 0) ^ sp[0]) * (q // 16) + q // 16 - 1, 0

    return call(
        "scan_back",
        functools.partial(scan_back_kernel, seg),
        sp,
        [
            here(conv_in),
            (conv_in, pl.BlockSpec((16, MIX), before)),
            here(step_raw),
            here(dy),
            (states, pl.BlockSpec((STATE, WIDE), lambda i, sp: (CTX - 1 - i, 0))),
            tail,
            cw,
            dstate,
            following,
        ],
        [
            here(shape((tokens, FULL), BF16)),
            shape((8, MIX), F32),
            shape((8, 128), F32),
            shape((STATE, WIDE), F32),
            shape((8, MIX), F32),
        ],
        24,
        grid=CTX,
        scratch=[
            pltpu.VMEM((q + 8, MIX), F32),
            pltpu.VMEM((q, MIX), F32),
            pltpu.VMEM((q, MIX), F32),
            pltpu.VMEM((q + 8, MIX), F32),
            pltpu.VMEM((STATE, WIDE), F32),
            pltpu.VMEM((q, WIDE), BF16),
            pltpu.VMEM((q, WIDE), BF16),
            pltpu.VMEM((q, WIDE), F32),
            pltpu.VMEM((q, WIDE), F32),
            pltpu.VMEM((8, WIDE), F32),
        ],
    )


def input_back_kernel(sp, dc_ref, dg_ref, wc_ref, wg_ref, *part_refs):
    part = dot(dc_ref[...], wc_ref[...], ABT) + dot(dg_ref[...], wg_ref[...], ABT)
    store_part(part, None, part_refs)


def input_back(sp, slots, dconv, dgate, wc, wg):
    outs = part_shapes(slots, dconv.shape[0], wc.shape[0])
    return call("input_back", input_back_kernel, sp, [dconv, dgate, wc, wg], outs, 24)


def own_back_kernel(count, sp, *refs):
    partial, rest = refs[:5], refs[5:]
    x = jnp.concatenate([v for _, v in load_rows(rest[:count])]).astype(F32)
    u = jnp.concatenate([v for _, v in load_rows(rest[count : 2 * count])]).astype(F32)
    cw_ref, branch_ref, up_ref, dnorm_ref = rest[2 * count :]
    grad = own_sum(partial)
    scale = row_scale(x)
    gained = grad * cw_ref[8:9, :]
    centre = jnp.mean(gained * x, axis=-1, keepdims=True)
    up = (u + scale * (gained - x * (scale * scale * centre))).astype(BF16)
    extra = up_ref.shape[0] - up.shape[0]
    up_ref[extra:, :] = up
    if extra:
        inner = jnp.sum(up.astype(F32) * branch_ref[...], axis=-1, keepdims=True)
        up_ref[:extra, :] = split_rows(stat_rows([inner])[0:1, :], up.shape[1])
    dnorm_ref[...] = jnp.broadcast_to(
        jnp.sum(grad * x * scale, axis=0, keepdims=True), dnorm_ref.shape
    )


def own_back(sp, extra, partial, x, u, cw, branch):
    q, d = partial[0].shape
    return call(
        "own_back",
        functools.partial(own_back_kernel, len(x)),
        sp,
        partial + x + u + [cw, branch],
        [shape((q + extra, d), BF16), shape((8, d), F32)],
    )


def head_map(group, block, flipped=False):
    here = lax.broadcasted_iota(jnp.int32, (128, 128), 1 if flipped else 0)
    there = lax.broadcasted_iota(jnp.int32, (128, 128), 0 if flipped else 1)
    turn = jnp.zeros_like(here)
    for edge in range(block, LOCAL, block):
        turn = turn + jnp.where(here >= edge, 1, 0)
    goal = here + (turn * (CTX - 1) + group) * block
    return jnp.where((here < LOCAL) & (there == goal), 1.0, 0.0)


def channel_map(flipped=False):
    dims = (128, WIDE) if flipped else (WIDE, 128)
    chan = lax.broadcasted_iota(jnp.int32, dims, 1 if flipped else 0)
    head = lax.broadcasted_iota(jnp.int32, dims, 0 if flipped else 1)
    return jnp.where((chan >= head * HEAD) & (chan < (head + 1) * HEAD), 1.0, 0.0)


def spans(group, block):
    wide = block * HEAD
    return [(z * wide, (z * CTX + group) * wide, wide) for z in range(WIDE // wide)]


def choose(first, a, b):
    return jnp.where(first, a, b)


def pack_kernel(block, sp, w_ref, *refs):
    conv_refs, gate_refs, conv, gate = refs[:CTX], refs[CTX : 2 * CTX], refs[-2], refs[-1]
    place = sp[0]
    keys = w_ref[:, 2 * INNER : 2 * INNER + STATE]
    queries = w_ref[:, 2 * INNER + STATE : 2 * INNER + 2 * STATE]
    steps = w_ref[:, 2 * INNER + 2 * STATE :]
    rows = w_ref.shape[0]
    steps = jnp.concatenate([steps, jnp.zeros((rows, 128 - HEADS), BF16)], axis=1)
    for k in range(CTX):
        values = jnp.concatenate(
            [w_ref[:, INNER + there : INNER + there + n] for _, there, n in spans(k, block)], axis=1
        )
        gates = jnp.concatenate(
            [w_ref[:, there : there + n] for _, there, n in spans(k, block)], axis=1
        )
        step = dot(steps, head_map(k, block, True).astype(BF16), AB).astype(BF16)
        conv[k] = jnp.concatenate(
            [values[:, :HALF], keys, step, values[:, HALF:], queries, step], axis=1
        )
        gate[k] = gates
    for m in range(CTX):
        conv_refs[m][...] = conv[m ^ place]
        gate_refs[m][...] = gate[m ^ place]


def pack(sp, block, w_in):
    rows = w_in.shape[0]
    outs = call(
        "pack",
        functools.partial(pack_kernel, block),
        sp,
        [w_in],
        [shape((rows, 2 * LOAD), BF16)] * CTX + [shape((rows, WIDE), BF16)] * CTX,
        16,
        scratch=[
            pltpu.VMEM((CTX, rows, 2 * LOAD), BF16),
            pltpu.VMEM((CTX, rows, WIDE), BF16),
        ],
    )
    return outs[:CTX], outs[CTX:]


def order_conv_kernel(sp, *refs):
    keep_ref, send_ref = refs[CTX:]
    zero = sp[1] == 0
    for m in range(CTX):
        low, high = refs[m][:, :LOAD], refs[m][:, LOAD:]
        keep_ref[m ^ sp[0]] = choose(zero, low, high)
        send_ref[m ^ sp[0]] = choose(zero, high, low)


def order_conv(sp, slots):
    out = shape((CTX, slots[0].shape[0], LOAD), BF16)
    return call("order_conv", order_conv_kernel, sp, slots, [out, out], 12)


def order_gate_kernel(sp, *refs):
    out_ref, keep_ref, send_ref = refs[CTX:]
    zero = sp[1] == 0
    rows = keep_ref.shape[1]
    for m in range(CTX):
        low, high = refs[m][:, :HALF], refs[m][:, HALF:]
        keep_ref[m ^ sp[0], :, :HALF] = choose(zero, low, high)
        send_ref[m ^ sp[0], :, :HALF] = choose(zero, high, low)
    for r in range(2):
        for c in range(2):
            at = slice(r * rows, (r + 1) * rows)
            low = out_ref[at, c * HALF : (c + 1) * HALF]
            high = out_ref[at, (2 + c) * HALF : (3 + c) * HALF]
            keep_ref[2 * r + c, :, HALF:] = choose(zero, low, high)
            send_ref[2 * r + c, :, HALF:] = choose(zero, high, low)


def order_gate(sp, slots, w_out):
    out = shape((CTX, slots[0].shape[0], WIDE), BF16)
    return call("order_gate", order_gate_kernel, sp, slots + [w_out], [out, out], 12)


def join_conv_kernel(sp, mine_ref, other_ref, wc_ref):
    zero = sp[1] == 0
    rows = mine_ref.shape[2]
    for i in range(CTX):
        a, b = mine_ref[0, i, :, :LOAD], other_ref[0, i, :, :LOAD]
        low, high = choose(zero, a, b), choose(zero, b, a)
        at = slice(i * rows, (i + 1) * rows)
        wc_ref[at, 0:HALF] = low[:, :HALF]
        wc_ref[at, HALF:WIDE] = high[:, :HALF]
        wc_ref[at, WIDE : WIDE + STATE] = low[:, HALF : HALF + STATE]
        wc_ref[at, WIDE + STATE : MIX] = high[:, HALF : HALF + STATE]
        wc_ref[at, MIX:] = low[:, HALF + STATE :]


def by_rows(x, count):
    return x, pl.BlockSpec((x.shape[0] // count, x.shape[1]), lambda z, sp: (z, 0))


def join_conv(sp, mine, other):
    dp, _, rows, _ = mine.shape
    out = by_rows(shape((dp * CTX * rows, FULL), BF16), dp)
    ins = [by_first(mine), by_first(other)]
    return call("join_conv", join_conv_kernel, sp, ins, [out], 12, dp)[0]


def join_gate_kernel(first, sp, mine_ref, other_ref, wg_ref, wo_ref):
    zero = sp[1] == 0
    rows = mine_ref.shape[2]
    for i in range(CTX):
        a, b = mine_ref[0, i, :, first:], other_ref[0, i, :, first:]
        low, high = choose(zero, a, b), choose(zero, b, a)
        at = slice(i * rows, (i + 1) * rows)
        wg_ref[at, :HALF] = low[:, :HALF]
        wg_ref[at, HALF:] = high[:, :HALF]
        r, c = i // 2, i % 2
        at = slice(r * rows, (r + 1) * rows)
        wo_ref[at, c * HALF : (c + 1) * HALF] = low[:, HALF:]
        wo_ref[at, (2 + c) * HALF : (3 + c) * HALF] = high[:, HALF:]


def join_gate(sp, mine, other):
    dp, _, rows, cols = mine.shape
    wg, wo = shape((dp * CTX * rows, WIDE), BF16), shape((dp * 2 * rows, 4 * HALF), BF16)
    outs = [by_rows(wg, dp), by_rows(wo, dp)]
    kernel = functools.partial(join_gate_kernel, cols - WIDE)
    ins = [by_first(mine), by_first(other)]
    return call("join_gate", kernel, sp, ins, outs, 12, dp)


def fold_kernel(direct, sp, keep_ref, came_ref, *out_refs):
    total = (keep_ref[0].astype(F32) + came_ref[0].astype(F32)).astype(BF16)
    if direct:
        for m, ref in enumerate(out_refs):

            @pl.when(pl.program_id(0) == (sp[2] ^ m))
            def _():
                ref[...] = total

    else:
        out_refs[0][0] = total


def fold(sp, direct, keep, came):
    part = shape(keep.shape[1:], BF16)
    outs = [part] * 4 if direct else [by_first(shape(keep.shape, BF16))]
    ins = [by_first(keep), by_first(came)]
    return call("fold", functools.partial(fold_kernel, direct), sp, ins, outs, 24, keep.shape[0])


def total_kernel(counts, sp, *refs):
    sums = []
    for count, cols in counts:
        terms, refs = refs[:count], refs[count:]

        def total(at, terms=terms, cols=cols):
            return sum(ref[at, :, :cols].astype(F32) for ref in terms).astype(BF16)

        sums.append(total)
    for m in range(CTX):
        refs[m][...] = jnp.concatenate([total(m ^ sp[0]) for total in sums], axis=1)


def total_line(sp, groups):
    width = {LOAD: LOAD, WIDE: HALF}
    counts = [(len(terms), width[terms[0].shape[2]]) for terms in groups]
    ins = [x for terms in groups for x in terms]
    rows = ins[0].shape[1]
    cols = sum(cols for _, cols in counts)
    outs = [shape((rows, cols), BF16)] * CTX
    return call("total_line", functools.partial(total_kernel, counts), sp, ins, outs)


def mix_kernel(cols, sp, *refs):
    out_ref = refs[-1]
    zero = sp[1] == 0
    for m in range(CTX):
        if cols == LOAD:
            mine, other = refs[CTX + m][...], refs[m][:, :LOAD]
        else:
            mine, other = refs[m][:, LOAD + HALF :], refs[m][:, LOAD : LOAD + HALF]
            out_ref[m, :, HALF:] = choose(zero, refs[CTX + 1][m, :, HALF:], refs[CTX][m, :, HALF:])
        out_ref[m, :, : mine.shape[1]] = choose(zero, other, mine)


def mix(sp, early, late, cols):
    out = shape((CTX, early[0].shape[0], cols), BF16)
    return call("mix", functools.partial(mix_kernel, cols), sp, early + late, [out])[0]


def grad_conv_kernel(sp, n0_ref, n1_ref, d0_ref, d1_ref, keep_ref, send_ref):
    zero = sp[1] == 0
    rows = keep_ref.shape[2]
    total = dot(n0_ref[...], d0_ref[...], ATB) + dot(n1_ref[...], d1_ref[...], ATB)
    total = total.astype(BF16)
    step = total[:, MIX:]
    low = jnp.concatenate([total[:, :HALF], total[:, WIDE : WIDE + STATE], step], axis=1)
    high = jnp.concatenate([total[:, HALF:WIDE], total[:, WIDE + STATE : MIX], step], axis=1)
    keep, send = choose(zero, low, high), choose(zero, high, low)
    for i in range(CTX):
        keep_ref[0, i] = keep[i * rows : (i + 1) * rows]
        send_ref[0, i] = send[i * rows : (i + 1) * rows]


def by_first(x):
    rest = (0,) * (len(x.shape) - 1)
    return x, pl.BlockSpec((1,) + tuple(x.shape[1:]), lambda z, sp: (z,) + rest)


def by_cols(x, count):
    return x, pl.BlockSpec((x.shape[0], x.shape[1] // count), lambda z, sp: (0, z))


def grad_conv(sp, dp, rows, normed, dconv):
    out = shape((dp, CTX, rows, LOAD), BF16)
    return call(
        "grad_conv",
        grad_conv_kernel,
        sp,
        [by_cols(x, dp) for x in normed] + list(dconv),
        [by_first(out), by_first(out)],
        24,
        dp,
    )


def grad_gate_kernel(sp, *refs):
    n_refs, dg_refs, gated_refs, u_refs = refs[0:2], refs[2:4], refs[4:6], refs[6:8]
    keep_ref, send_ref = refs[8:]
    z = pl.program_id(0)
    dp, _, rows, _ = keep_ref.shape
    zero = sp[1] == 0

    def over_tokens(a, b):
        return dot(a[0][...], b[0][...], ATB) + dot(a[1][...], b[1][...], ATB)

    total = over_tokens(n_refs, dg_refs).astype(BF16)
    keep = choose(zero, total[:, :HALF], total[:, HALF:])
    send = choose(zero, total[:, HALF:], total[:, :HALF])
    for i in range(CTX):
        keep_ref[z, i, :, :HALF] = keep[i * rows : (i + 1) * rows]
        send_ref[z, i, :, :HALF] = send[i * rows : (i + 1) * rows]
    total = over_tokens(gated_refs, u_refs).astype(BF16)
    side, c = z // 2, lax.rem(z, 2)

    def put(ref):
        for there in range(dp):
            for r in range(2):
                first = (2 * there + r) * rows
                ref[there, 2 * r + c, :, HALF:] = total[first : first + rows]

    @pl.when(side == sp[1])
    def _():
        put(keep_ref)

    @pl.when(side != sp[1])
    def _():
        put(send_ref)


def grad_gate(sp, dp, rows, normed, dgate, gated, u):
    out = shape((dp, CTX, rows, WIDE), BF16)
    return call(
        "grad_gate",
        grad_gate_kernel,
        sp,
        [by_cols(x, dp) for x in normed]
        + list(dgate)
        + list(gated)
        + [by_cols(x, dp) for x in u],
        [out, out],
        32,
        dp,
    )


def finish_kernel(block, sp, *refs):
    early, late, (gate0, gate1, came_gate, came_conv) = refs[:4], refs[4:8], refs[8:12]
    in_ref, out_ref, lows, highs, glows, ghighs = refs[12:]
    place, zero = sp[0], sp[1] == 0
    rows = in_ref.shape[0]
    for m in range(CTX):
        mine, came = choose(zero, late[m][...], early[m][:, :LOAD]), came_conv[m]
        lows[m ^ place] = choose(zero, mine, came).astype(F32)
        highs[m ^ place] = choose(zero, came, mine).astype(F32)
        mine = choose(zero, early[m][:, LOAD + HALF :], early[m][:, LOAD : LOAD + HALF])
        came = came_gate[m, :, :HALF]
        glows[m ^ place] = choose(zero, mine, came).astype(F32)
        ghighs[m ^ place] = choose(zero, came, mine).astype(F32)
    keys, queries, steps = 0.0, 0.0, 0.0
    for k in range(CTX):
        keys = keys + lows[k, :, HALF : HALF + STATE]
        queries = queries + highs[k, :, HALF : HALF + STATE]
        steps = steps + dot(lows[k, :, HALF + STATE :], head_map(k, block), AB, HIGH)
    for z in range(WIDE // (block * HEAD)):
        def side_by_side(a, b):
            parts = []
            for k in range(CTX):
                here, _, n = spans(k, block)[z]
                source = a if here < HALF else b
                parts.append(source[k, :, here % HALF : here % HALF + n])
            return jnp.concatenate(parts, axis=1)

        wide = CTX * block * HEAD
        in_ref[:, z * wide : (z + 1) * wide] = side_by_side(glows, ghighs)
        in_ref[:, INNER + z * wide : INNER + (z + 1) * wide] = side_by_side(lows, highs)
    in_ref[:, 2 * INNER : 2 * INNER + STATE] = keys
    in_ref[:, 2 * INNER + STATE : 2 * INNER + 2 * STATE] = queries
    in_ref[:, 2 * INNER + 2 * STATE :] = steps[:, :HEADS]
    for i in range(4):
        r, c = i // 2, i % 2
        mine, came = choose(zero, gate0[i, :, HALF:], gate1[i, :, HALF:]), came_gate[i, :, HALF:]
        at = slice(r * rows, (r + 1) * rows)
        out_ref[at, c * HALF : (c + 1) * HALF] = choose(zero, mine, came).astype(F32)
        out_ref[at, (2 + c) * HALF : (3 + c) * HALF] = choose(zero, came, mine).astype(F32)


def finish(sp, block, early, late, gates, came_gate, came_conv):
    rows = came_conv.shape[1]
    return call(
        "finish",
        functools.partial(finish_kernel, block),
        sp,
        early + late + gates + [came_gate, came_conv],
        [shape((rows, 2 * INNER + 2 * STATE + HEADS), F32), shape((2 * rows, 4 * HALF), F32)],
        24,
        scratch=[pltpu.VMEM((CTX, rows, LOAD), F32)] * 2 + [pltpu.VMEM((CTX, rows, HALF), F32)] * 2,
    )


class Direct:
    def __init__(self, order, mine, dp, block, w_in, w_out):
        self.order, self.mine, self.dp, self.block = order, mine, dp, block
        self.rows = w_in.shape[0]
        conv, gate = order(pack, block, w_in)
        conv = order(order_conv, [flip(x, m) if m else x for m, x in enumerate(conv)])
        self.conv = self.trade(*conv)
        self.first = self.gathered(self.conv[0])
        gate = [order.now(x) for x in gate]
        self.slots = [flip(x, m) if m else x for m, x in enumerate(gate)]
        self.w_out = w_out

    def prepare_gate(self):
        self.gate = self.trade(*self.order(order_gate, self.slots, self.w_out))

    def trade(self, keep, send):
        came = swap_core(send)
        return choose(self.mine == 0, keep, came), choose(self.mine == 0, came, keep)

    def gathered(self, x):
        return lax.all_gather(x, "dp", axis=0)

    def start_conv(self):
        return self.first

    def start_gate(self, after):
        x, _ = lax.optimization_barrier((self.order.now(self.gate[0]), after))
        return self.gathered(x)

    def start_both(self):
        return self.gathered(self.order.now(jnp.concatenate([self.conv[1], self.gate[1]], -1)))

    def trade_weights(self, x):
        x = self.order.now(x)
        return x, swap_core(x)

    def conv_weights(self, sp, both):
        return join_conv(sp, *both)

    def gate_weights(self, sp, both):
        return join_gate(sp, *both)

    def grad_gate(self, sp, layer, normed, dgate, gated, u):
        return grad_gate(sp, self.dp, self.rows, normed, dgate, gated, u)

    def grad_conv(self, sp, layer, normed, dconv):
        return grad_conv(sp, self.dp, self.rows, normed, dconv)

    def trade_grads(self, grads):
        return grads[0], swap_core(grads[1])

    def send(self, sp, direct, traded):
        parts = fold(sp, direct, *traded)
        if not direct:
            return [lax.psum_scatter(parts[0], "dp", scatter_dimension=0, tiled=True)[0]], parts[0]
        pairs = [[(i, i ^ m) for i in range(4)] for m in range(4)]
        terms = [lax.ppermute(x, "dp", pairs[m]) if m else x for m, x in enumerate(parts)]
        return terms, parts[0]

    def early(self, conv1, gate1, gate0):
        self.gates = [gate0[0], gate1[0]]
        slots = self.order(total_line, [conv1, gate1, gate0])
        self.slots = [flip(x, m) if m else x for m, x in enumerate(slots)]

    def early_trade(self):
        self.came = swap_core(self.order(mix, self.slots, self.gates, WIDE))

    def gradients(self, conv0):
        late = self.order(total_line, [conv0])
        late = [flip(x, m) if m else x for m, x in enumerate(late)]
        came = swap_core(self.order(mix, self.slots, late, LOAD))
        return self.order(finish, self.block, self.slots, late, self.gates, self.came, came)


def grouped(columns, block):
    lead = columns.shape[:-1]
    split = jnp.moveaxis(columns.reshape(lead + (-1, CTX, block)), -2, 0)
    return split.reshape((CTX,) + lead + (-1,))


def ungrouped(groups, block):
    lead = groups.shape[1:-1]
    split = groups.reshape((CTX,) + lead + (-1, block))
    return jnp.moveaxis(split, 0, -2).reshape(lead + (-1,))


def pad_to(x, rows, cols):
    room = [(0, 0)] * (x.ndim - 2) + [(0, rows - x.shape[-2]), (0, cols - x.shape[-1])]
    return jnp.pad(x, room)


class Plain:
    def __init__(self, mine, place, block, w_in, w_out):
        self.mine, self.place, self.block = mine, place, block
        full_in = lax.all_gather(w_in, ("dp", "ctx"), axis=0, tiled=True)
        full_out = lax.all_gather(w_out, ("dp", "ctx"), axis=0, tiled=True)
        self.full = [(full_in, full_out), (swap_core(full_in), swap_core(full_out))]
        self.grads = [{}, {}]

    def prepare_gate(self):
        pass

    def start_conv(self):
        return 0

    def start_gate(self, after):
        return 0

    def start_both(self):
        return 1

    def trade_weights(self, layer):
        return layer

    def trade_grads(self, grads):
        return grads

    def send(self, sp, direct, traded):
        return traded, traded[0]

    def early(self, conv1, gate1, gate0):
        pass

    def early_trade(self):
        pass

    def group(self, columns, block):
        return lax.dynamic_index_in_dim(grouped(columns, block), self.place, 0, False)

    def layer(self, layer, which):
        return choose(self.mine == layer, self.full[0][which], self.full[1][which])

    def conv_weights(self, sp, layer):
        one = self.layer(layer, 0)
        values = self.group(one[:, INNER : 2 * INNER], self.block * HEAD)
        step = self.group(one[:, 2 * INNER + 2 * STATE :], self.block)
        shared = one[:, 2 * INNER : 2 * INNER + 2 * STATE]
        return jnp.concatenate([values, shared, pad_to(step, step.shape[0], 128)], 1)

    def gate_weights(self, sp, layer):
        one, out = self.layer(layer, 0), self.layer(layer, 1)
        wide = self.block * HEAD
        return self.group(one[:, :INNER], wide), self.group(out.T, wide).T

    def over_tokens(self, a, b):
        both = [dot(x, y, ATB) for x, y in zip(a, b)]
        return (both[0] + both[1]).astype(BF16)

    def grad_gate(self, sp, layer, normed, dgate, gated, u):
        out = self.over_tokens(gated, u)
        self.grads[layer].update(gate=self.over_tokens(normed, dgate), out=out)
        return [out]

    def grad_conv(self, sp, layer, normed, dconv):
        self.grads[layer].update(conv=self.over_tokens(normed, dconv))
        return [self.grads[layer]["conv"]]

    def spread(self, columns, block):
        at = lax.broadcasted_iota(jnp.int32, (CTX, 1, 1), 0) == self.place
        return ungrouped(jnp.where(at, columns[None], jnp.zeros((), columns.dtype)), block)

    def gradients(self, conv0):
        wide = self.block * HEAD
        fulls = []
        for grads in self.grads:
            gate, conv = grads["gate"], grads["conv"]
            grad_in = jnp.concatenate(
                [
                    self.spread(gate, wide),
                    self.spread(conv[:, :WIDE], wide),
                    conv[:, WIDE:MIX],
                    self.spread(conv[:, MIX : MIX + LOCAL], self.block),
                ],
                -1,
            )
            fulls.append((grad_in, self.spread(grads["out"].T, wide).T))
        sums = []
        for a, b in zip(*fulls):
            zero = self.mine == 0
            total = choose(zero, a, b).astype(F32) + swap_core(choose(zero, b, a)).astype(F32)
            total = total.astype(BF16)
            sums.append(
                lax.psum_scatter(total, ("dp", "ctx"), scatter_dimension=0, tiled=True).astype(F32)
            )
        return sums[0], sums[1]


def prepare_kernel(block, sp, norm_ref, taps_ref, bias_ref, dt_ref, log_ref, skip_ref, gain_ref, out_ref):
    out_ref[...] = jnp.zeros_like(out_ref)
    for k in range(CTX):

        @pl.when(sp[0] == k)
        def _():
            for here, there, n in spans(k, block):
                out_ref[0:CONV, here : here + n] = taps_ref[0, :, there : there + n]
                out_ref[4:5, here : here + n] = bias_ref[:, there : there + n]
                out_ref[9:10, here : here + n] = gain_ref[:, there : there + n]
            spare = jnp.zeros((1, 128 - HEADS), F32)
            rows = [jnp.concatenate([ref[...], spare], axis=1) for ref in (dt_ref, log_ref, skip_ref)]
            rows = jnp.concatenate(rows + [jnp.zeros((5, 128), F32)])
            local = dot(rows, head_map(k, block, True), AB, HIGH)
            out_ref[10:11, 0:128] = local[0:1, :]
            out_ref[11:12, 0:128] = jnp.exp(local[1:2, :])
            out_ref[5:6, :WIDE] = dot(local, channel_map(True), AB, HIGH)[2:3, :]

    out_ref[0:CONV, WIDE:MIX] = taps_ref[0, :, INNER:]
    out_ref[4:5, WIDE:MIX] = bias_ref[:, INNER:]
    out_ref[8:9, :] = norm_ref[...]


def prepare(sp, block, arrays):
    out = shape((16, arrays[0].shape[1]), F32)
    return call("prepare", functools.partial(prepare_kernel, block), sp, arrays, [out], 12)[0]


def gather_small_kernel(counts, sp, *refs):
    keep_ref, send_ref = refs[-2:]
    packed, at = [], 0
    for layer in range(2):
        sums = []
        for count in counts[layer]:
            sums.append(sum(ref[...] for ref in refs[at : at + count]))
            at += count
        dcw, dhp, dgain, dnorm = sums
        tall = lax.broadcasted_iota(jnp.int32, (8, MIX), 0)
        gain = jnp.concatenate([dgain, jnp.zeros((8, MIX - WIDE), F32)], axis=1)
        short = dnorm.shape[1] - MIX
        norm_rest = jnp.concatenate([dnorm[:, MIX:], jnp.zeros((8, MIX - short), F32)], axis=1)
        middle = jnp.where(tall == 0, gain, jnp.where(tall == 1, dnorm[:, :MIX], norm_rest))
        heads = jnp.concatenate([dhp, jnp.zeros((8, MIX - 128), F32)], axis=1)
        packed.append(jnp.concatenate([dcw, middle, heads]))
    zero = sp[1] == 0
    keep_ref[...] = choose(zero, packed[0], packed[1])
    send_ref[...] = choose(zero, packed[1], packed[0])


def gather_small(sp, small):
    counts = [[len(kind) for kind in layer] for layer in small]
    arrays = [x for layer in small for kind in layer for x in kind]
    out = shape((PACK, MIX), F32)
    kernel = functools.partial(gather_small_kernel, counts)
    return call("gather_small", kernel, sp, arrays, [out, out], 12)


def spread_small_kernel(block, sp, *refs):
    slots, all_slots = refs[:CTX], refs[-1]
    norm_ref, taps_ref, bias_ref, dt_ref, log_ref, skip_ref, gain_ref = refs[CTX:-1]
    for m in range(CTX):
        all_slots[m ^ sp[0]] = slots[m][...]
    total = sum(all_slots[k] for k in range(CTX))
    norm_ref[:, :MIX] = total[9:10, :]
    norm_ref[:, MIX:] = total[10:11, : norm_ref.shape[1] - MIX]
    taps_ref[0, :, INNER:] = total[0:CONV, WIDE:]
    bias_ref[:, INNER:] = total[4:5, WIDE:]
    pick = channel_map()
    heads = 0.0
    for k in range(CTX):
        for here, there, n in spans(k, block):
            taps_ref[0, :, there : there + n] = all_slots[k, 0:CONV, here : here + n]
            bias_ref[:, there : there + n] = all_slots[k, 4:5, here : here + n]
            gain_ref[:, there : there + n] = all_slots[k, 8:9, here : here + n]
        skip = dot(all_slots[k, 0:8, :WIDE], pick, AB, HIGH)
        both = jnp.concatenate([all_slots[k, 16:24, :128], skip])
        heads = heads + dot(both, head_map(k, block), AB, HIGH)
    dt_ref[...] = heads[0:1, :HEADS]
    log_ref[...] = heads[1:2, :HEADS]
    skip_ref[...] = heads[13:14, :HEADS]


def spread_small(sp, block, slots, d):
    one = shape((1, HEADS), F32)
    return call(
        "spread_small",
        functools.partial(spread_small_kernel, block),
        sp,
        slots,
        [
            shape((1, d), F32),
            shape((1, CONV, CONV_DIM), F32),
            shape((1, CONV_DIM), F32),
            one,
            one,
            one,
            shape((1, INNER), F32),
        ],
        12,
        scratch=[pltpu.VMEM((CTX, PACK, MIX), F32)],
    )


def sum_over_dp(x, dp):
    if dp & (dp - 1):
        return lax.psum(x, "dp")
    step = 1
    while step < dp:
        x = x + lax.ppermute(x, "dp", [(i, i ^ step) for i in range(dp)])
        step *= 2
    return x


class Order:
    def __init__(self, sp):
        self.sp = sp

    def __call__(self, kernel, *args):
        out = kernel(self.sp, *args)
        self.after(out[0] if isinstance(out, (list, tuple)) else out)
        return out

    def after(self, x):
        self.sp, _ = lax.optimization_barrier((self.sp, x))

    def now(self, x):
        return lax.optimization_barrier((x, self.sp))[0]


def shards(
    tokens,
    cotangent,
    doc_lengths,
    norm_gain,
    w_in,
    conv_weight,
    conv_bias,
    dt_bias,
    a_log,
    d_skip,
    inner_gain,
    w_out,
):
    mine, place = lax.axis_index("section"), lax.axis_index("ctx")
    dp = lax.axis_size("dp")
    piece, d = tokens.shape[2], tokens.shape[3]
    seg_len = piece * CTX // SEGS
    direct = dp == 4 and w_out.shape[1] % HEAD == 0 and w_out.shape[1] * dp == WIDE
    block = w_out.shape[1] // HEAD if direct else LOCAL

    own_x = lax.dynamic_index_in_dim(tokens, mine, 0, False)[0]
    own_u = lax.dynamic_index_in_dim(cotangent, mine, 0, False)[0]
    lengths = lax.dynamic_index_in_dim(doc_lengths, mine, 0, False)[0]
    start = jnp.stack([place, mine, lax.axis_index("dp")]).astype(jnp.int32)
    sp = jnp.concatenate([start, jnp.cumsum(lengths) - lengths])
    run = Order(sp)
    if direct:
        carrier = Direct(run, mine, dp, block, w_in[0], w_out[0])
    else:
        carrier = Plain(mine, place, block, w_in[0], w_out[0])

    def natural(slots):
        return jnp.concatenate(slots).reshape(CTX, 2, piece // 2, d)

    rows_x = gather_slots(run, run.now(own_x))
    arrays = [norm_gain, conv_weight, conv_bias, dt_bias, a_log, d_skip, inner_gain]
    params = run(prepare, block, arrays)
    other = swap_core(params)
    params = [choose(mine == 0, params, other), choose(mine == 0, other, params)]
    carrier.prepare_gate()
    rows_x = natural(rows_x())
    conv0 = carrier.start_conv()
    run.after(rows_x)
    gate0 = carrier.start_gate(conv0)
    conv0 = carrier.trade_weights(conv0)
    rows_u = gather_slots(run, run.now(own_u))
    no_state, no_tail = jnp.zeros((STATE, WIDE), F32), jnp.zeros((16, MIX), BF16)

    def forward(layer, s, pieces, wc, state, tail):
        normed, conv_in, step_raw = run(project, pieces, params[layer], wc, seg_len)
        y, states, state, next_tail = run(
            scan_rows, s, conv_in, step_raw, params[layer], state, tail
        )
        return dict(
            normed=normed, conv_in=conv_in, step_raw=step_raw, y=y, states=states, tail=tail
        ), state, next_tail

    wc0 = run(carrier.conv_weights, conv0)
    both1 = carrier.start_both()
    first, second = [None, None], [None, None]
    state, tail = no_state, no_tail
    first[0], state, tail = forward(0, 0, natural_slots(rows_x, 0), wc0, state, tail)
    first[1], state, tail = forward(0, 1, natural_slots(rows_x, 1), wc0, state, tail)
    rows_u = rows_u()
    gate0 = carrier.trade_weights(gate0)
    wg0, wo0 = run(carrier.gate_weights, gate0)
    sums, middle = [], []
    for s in range(SEGS):
        saved = first[s]
        saved["gate"], stat, *part = run(
            out_rows, True, [], [], saved["normed"], saved["y"], params[0], wg0, wo0
        )
        sums.append((stat, scatter_start(*part)))
    for s in range(SEGS):
        stat, part = sums[s]
        part = scatter_slots(run, *part)
        first[s]["stats"] = [stat] + [tail_tile(x) for x in part[1:4]]
        sums[s] = part
    for s in range(SEGS):
        residual = natural_slots(rows_x, s)[:1]
        own, first[s]["branch"] = run(own_rows, False, first[s]["stats"], sums[s], residual)
        first[s]["own"] = own
        middle.append(gather_slots(run, own))
    middle[0] = middle[0]()
    rows_u = natural(rows_u)
    run.after(rows_u)

    both1 = carrier.trade_weights(both1)
    wc1 = run(carrier.conv_weights, both1)
    wg1, wo1 = run(carrier.gate_weights, both1)
    state, tail = no_state, no_tail
    parts, before = [], []
    for s in range(SEGS):
        second[s], state, tail = forward(1, s, middle[s], wc1, state, tail)
        saved = second[s]
        if s == 0:
            middle[1] = middle[1]()
        saved["gate"], stats, part = run(
            out_rows,
            False,
            before,
            natural_slots(rows_u, s),
            saved["normed"],
            saved["y"],
            params[1],
            wg1,
            wo1,
        )
        before = [stats]
        parts.append(part)
    stats = from_all(stats)
    part1 = run(collect, parts)
    hidden0 = run(natural_rows, middle)

    def gate_step(layer, s, saved, pieces, stats, first_stat, inners, wo):
        out = run(
            gate_back, pieces, stats, first_stat, inners, saved["y"], saved["gate"], params[layer], wo
        )
        saved.update(zip(("dy", "dgate", "gated", "u", "dgain"), out))

    def scan_step(layer, s, saved, dstate, later):
        saved["dconv"], saved["dcw"], saved["dhp"], dstate, later = run(
            scan_back,
            s,
            saved["conv_in"],
            saved["step_raw"],
            saved["dy"],
            saved["states"],
            saved["tail"],
            params[layer],
            dstate,
            later,
        )
        return dstate, later

    def of(saved, *names):
        return [[one[name] for one in saved] for name in names]

    def send(traded, direct=False):
        terms, first_part = carrier.send(run.sp, direct, traded)
        run.after(first_part)
        return terms

    def back_start(s):
        saved = second[s]
        return scatter_start(*run(input_back, True, saved["dconv"], saved["dgate"], wc1, wg1))

    def back_end(s, part):
        up, second[s]["dnorm"] = run(
            own_back,
            16,
            part,
            [first[s]["own"]],
            natural_slots(rows_u, s)[:1],
            params[1],
            first[s]["branch"],
        )
        return gather_slots(run, up, 16)

    upper = [None, None]

    def lower_gate(s):
        inners = [head_tile(x) for x in upper[s][:4]]
        gate_step(0, s, first[s], upper[s], first[s]["stats"], 0, inners, wo0)

    for s in (1, 0):
        gate_step(1, s, second[s], natural_slots(rows_u, s), stats, 8 * s, [], wo1)
    gate1 = carrier.trade_grads(run(carrier.grad_gate, 1, *of(second, "normed", "dgate", "gated", "u")))
    part1 = scatter_start(*part1)
    gate1 = send(gate1)
    dstate, later = no_state, jnp.zeros((8, MIX), F32)
    dstate, later = scan_step(1, 1, second[1], dstate, later)
    upper[1] = back_start(1)
    part1 = scatter_slots(run, *part1)
    dstate, later = scan_step(1, 0, second[0], dstate, later)
    upper[1] = scatter_slots(run, *upper[1])
    upper[0] = back_start(0)
    upper[1] = back_end(1, upper[1])
    conv1 = carrier.trade_grads(run(carrier.grad_conv, 1, *of(second, "normed", "dconv")))
    upper[0] = scatter_slots(run, *upper[0])
    upper[1] = upper[1]()
    conv1 = send(conv1)
    hidden1, _ = run(own_rows, True, stats, part1, [hidden0])
    upper[0] = back_end(0, upper[0])
    lower_gate(1)
    dstate, later = no_state, jnp.zeros((8, MIX), F32)
    dstate, later = scan_step(0, 1, first[1], dstate, later)
    upper[0] = upper[0]()
    (part_1,) = run(input_back, False, first[1]["dconv"], first[1]["dgate"], wc0, wg0)
    lower_gate(0)
    gate0 = carrier.trade_grads(run(carrier.grad_gate, 0, *of(first, "normed", "dgate", "gated", "u")))
    grads1 = run(natural_rows, upper, 16)
    gate0 = send(gate0)
    dstate, later = scan_step(0, 0, first[0], dstate, later)
    conv0 = carrier.trade_grads(run(carrier.grad_conv, 0, *of(first, "normed", "dconv")))
    (part_0,) = run(input_back, False, first[0]["dconv"], first[0]["dgate"], wc0, wg0)
    conv0 = send(conv0, True)
    part = scatter_start(*run(collect, [part_0, part_1]))
    carrier.early(conv1, gate1, gate0)
    part = scatter_slots(run, *part)
    carrier.early_trade()
    branch = jnp.zeros((piece, d), F32)
    grads0, dnorm0 = run(own_back, 0, part, [own_x], [grads1], params[0], branch)
    small = [
        of(first, "dcw", "dhp", "dgain") + [[dnorm0]],
        of(second, "dcw", "dhp", "dgain", "dnorm"),
    ]
    keep, small_sent = run(gather_small, small)
    total = from_all(sum_over_dp(keep + swap_core(small_sent), dp))
    shard_in, shard_out = carrier.gradients(conv0)
    norm, taps, bias, dt, log, skip, gain = spread_small(sp, block, total, d)

    def to_layers(a, b):
        here, there = choose(mine == 0, a, b), swap_core(choose(mine == 0, b, a))
        both = jnp.stack([choose(mine == 0, here, there), choose(mine == 0, there, here)])
        return both[None, :, None]

    return (
        to_layers(hidden0, hidden1),
        to_layers(grads0, grads1),
        norm,
        shard_in[None],
        taps,
        bias,
        dt,
        log,
        skip,
        gain,
        shard_out[None],
    )


def solution(mesh):
    in_specs = (
        P(None, "dp", "ctx", None),
        P(None, "dp", "ctx", None),
        P(None, "dp", None),
        P("section", None),
        P("section", ("dp", "ctx"), None),
        P("section", None, None),
        P("section", None),
        P("section", None),
        P("section", None),
        P("section", None),
        P("section", None),
        P("section", ("dp", "ctx"), None),
    )
    out_specs = (
        P("section", None, "dp", "ctx", None),
        P("section", None, "dp", "ctx", None),
        P("section", None),
        P("section", ("dp", "ctx"), None),
        P("section", None, None),
        P("section", None),
        P("section", None),
        P("section", None),
        P("section", None),
        P("section", None),
        P("section", ("dp", "ctx"), None),
    )
    return jax.shard_map(shards, mesh=mesh, in_specs=in_specs, out_specs=out_specs, check_vma=False)
```

```python
import functools

import jax
import jax.numpy as jnp
from jax import lax
from jax.experimental import pallas as pl
from jax.experimental.pallas import tpu as pltpu
from jax.sharding import PartitionSpec as P

HEADS = 48
HEAD = 64
STATE = 128
CONV = 4
INNER = 3072
CONV_DIM = 3328
NORM_EPS = 1e-05

F32 = jnp.float32
BF16 = jnp.bfloat16
HIGH = lax.Precision.HIGHEST
CTX = 4
SEGS = 2
LOCAL = HEADS // CTX
WIDE = LOCAL * HEAD
MIX = WIDE + 2 * STATE
FULL = MIX + 128
HALF = WIDE // 2
LOAD = HALF + STATE + 128
PACK = 24
MIB = 1024 * 1024
MICROS = {
    "project": 3,
    "scan_rows": 8,
    "out_rows": 4,
    "gate_back": 3,
    "scan_back": 16,
    "input_back": 4,
    "grad_gate": 8,
    "grad_conv": 6,
}


def swap_core(x):
    return lax.ppermute(x, "section", [(0, 1), (1, 0)])


def flip(x, bits):
    return lax.ppermute(x, "ctx", [(i, i ^ bits) for i in range(CTX)])


def gather_slots(order, own, extra=0):
    half = (own.shape[0] - extra) // 2
    x, y = flip(own, 1), flip(own, 2)

    def forward():
        order.after((x, y))
        first, second = order.now(y[: extra + half]), order.now(x[extra + half :])
        return [own, x, y, flip(first, 1), flip(second, 2)]

    return forward


def scatter_start(own, to_x, to_y, late_x, late_y):
    return own, flip(to_x, 1), flip(to_y, 2), late_x, late_y


def scatter_slots(order, own, from_x, from_y, late_x, late_y):
    extra = from_x.shape[0] - 2 * late_x.shape[0]
    outs = [shape((late_x.shape[0] + extra, late_x.shape[1]), BF16), late_y]
    late_x, late_y = order(call_with("turn", turn_kernel, [from_x, from_y, late_x, late_y], outs))
    return [own, from_x, from_y, flip(late_x, 1), flip(late_y, 2)]


def from_all(x):
    return [x] + [flip(x, m) for m in range(1, CTX)]


def dot(a, b, dims, precision=None):
    return lax.dot_general(a, b, (dims, ((), ())), precision=precision, preferred_element_type=F32)


AB = ((1,), (0,))
ABT = ((1,), (1,))
ATB = ((0,), (0,))


def call_with(name, kernel, ins, outs):
    return lambda sp: call(name, kernel, sp, ins, outs)


def split_dot(a, b, dims):
    a_high, b_high = a.astype(BF16), b.astype(BF16)
    a_low = (a - a_high.astype(F32)).astype(BF16)
    b_low = (b - b_high.astype(F32)).astype(BF16)
    return dot(a_high, b_high, dims) + dot(a_low, b_high, dims) + dot(a_high, b_low, dims)


def whole(x):
    zeros = (0,) * len(x.shape)
    return pl.BlockSpec(tuple(x.shape), lambda i, sp: zeros)


def shape(dims, dtype):
    return jax.ShapeDtypeStruct(dims, dtype)


def call(name, kernel, sp, ins, outs, vmem=20, grid=1, scratch=()):
    ins = [x if isinstance(x, tuple) else (x, whole(x)) for x in ins]
    outs = [x if isinstance(x, tuple) else (x, whole(x)) for x in outs]
    return pl.pallas_call(
        kernel,
        grid_spec=pltpu.PrefetchScalarGridSpec(
            num_scalar_prefetch=1,
            grid=(grid,),
            in_specs=[spec for _, spec in ins],
            out_specs=[spec for _, spec in outs],
            scratch_shapes=list(scratch),
        ),
        out_shape=[x for x, _ in outs],
        compiler_params=pltpu.CompilerParams(
            dimension_semantics=("arbitrary",), vmem_limit_bytes=vmem * MIB
        ),
        cost_estimate=pl.CostEstimate(
            flops=int(MICROS.get(name, 1) * 1e9), bytes_accessed=1, transcendentals=0
        ),
        name=name,
    )(sp, *[x for x, _ in ins])


def natural_spec(x, seg, slot):
    def at(i, sp):
        inside = slot ^ sp[0]
        return (2 * seg + (inside >> 1)) ^ sp[0], inside & 1, 0, 0

    return pl.BlockSpec((1, 1) + x.shape[2:], at)


def natural_slots(x, seg):
    return [(x, natural_spec(x, seg, m)) for m in range(CTX)]


def load_rows(refs, extra=0):
    first = 0
    for n, ref in enumerate(refs):
        value = ref[...]
        value = value.reshape(value.shape[-2:])
        if extra and n < 4:
            value = value[extra:]
        yield first, value
        first += value.shape[0]


def row_scale(x):
    return lax.rsqrt(jnp.mean(x * x, axis=-1, keepdims=True) + NORM_EPS)


def project_kernel(count, sp, *refs):
    cw_ref, wc_ref, normed_ref, conv_ref, step_ref = refs[count:]
    gain = cw_ref[8:9, :]
    for first, x in load_rows(refs[:count]):
        x = x.astype(F32)
        rows = pl.ds(first, x.shape[0])
        normed_ref[rows, :] = (x * row_scale(x) * gain).astype(BF16)
    normed = normed_ref[...]
    conv_ref[...] = dot(normed, wc_ref[:, :MIX], AB).astype(BF16)
    step_ref[...] = dot(normed, wc_ref[:, MIX:], AB)


def project(sp, pieces, cw, wc, tokens):
    return call(
        "project",
        functools.partial(project_kernel, len(pieces)),
        sp,
        pieces + [cw, wc],
        [
            shape((tokens, wc.shape[0]), BF16),
            shape((tokens, MIX), BF16),
            shape((tokens, 128), F32),
        ],
    )


def bounds_of(sp):
    return [sp[3 + d] for d in range(sp.shape[0] - 3)]


def distances(sp, first, rows):
    at = lax.broadcasted_iota(jnp.int32, (rows, 1), 0) + first
    since = at
    for bound in bounds_of(sp):
        gap = at - bound
        since = jnp.where(gap >= 0, jnp.minimum(since, gap), since)
    return since


def segment(sp, at):
    total = jnp.zeros_like(at)
    for bound in bounds_of(sp):
        total = total + jnp.where(at >= bound, 1, 0)
    return total


def pair_lanes(a, pair):
    rows = a.shape[0]
    low = lax.broadcasted_iota(jnp.int32, (rows, 2 * HEAD), 1) < HEAD
    first = jnp.broadcast_to(a[:, 2 * pair : 2 * pair + 1], (rows, 2 * HEAD))
    second = jnp.broadcast_to(a[:, 2 * pair + 1 : 2 * pair + 2], (rows, 2 * HEAD))
    return jnp.where(low, first, second)


def conv_forward(ext, cw_ref, since, cols, q):
    total = cw_ref[4:5, cols] + cw_ref[3:4, cols] * ext[8 : 8 + q, cols]
    for shift in range(1, CONV):
        tap = cw_ref[3 - shift : 4 - shift, cols]
        rows = ext[8 - shift : 8 - shift + q, cols]
        total = total + jnp.where(since >= shift, tap * rows, 0.0)
    return total


def block_terms(sp, first, q, raw, cw_ref):
    row = lax.broadcasted_iota(jnp.int32, (q, 1), 0)
    col = lax.broadcasted_iota(jnp.int32, (1, q), 1)
    seg_col, seg_row = segment(sp, row + first), segment(sp, col + first)
    seg_before, seg_last = jnp.int32(0), jnp.int32(0)
    for bound in bounds_of(sp):
        seg_before = seg_before + jnp.where(first - 1 >= bound, 1, 0)
        seg_last = seg_last + jnp.where(first + q - 1 >= bound, 1, 0)
    same = seg_col == seg_row
    shifted = raw + cw_ref[10:11, 0:128]
    stepsize = jax.nn.softplus(shifted)
    decay = -stepsize * cw_ref[11:12, 0:128]
    lower = jnp.where(row >= col, 1.0, 0.0)
    cum = dot(lower, decay, AB, HIGH)
    last = cum[q - 1 : q, :]
    open_w = jnp.where(seg_col == seg_before, jnp.exp(cum), 0.0)
    tail = jnp.where(seg_col == seg_last, jnp.exp(jnp.minimum(last - cum, 0.0)), 0.0)
    passed = jnp.where(seg_last == seg_before, jnp.exp(last), 0.0)
    return row, col, same, shifted, stepsize, decay, cum, open_w, tail, passed


def pair_cols(pair):
    return slice(2 * HEAD * pair, 2 * HEAD * (pair + 1))


def scan_kernel(
    seg,
    sp,
    ci_ref,
    raw_ref,
    cw_ref,
    st_in_ref,
    tail_in_ref,
    y_ref,
    st_ref,
    st_out_ref,
    tail_out_ref,
    ext,
    mix,
    state,
    flow,
    fresh,
):
    k = pl.program_id(0)
    q = ci_ref.shape[0]
    first = (CTX * seg + k) * q

    @pl.when(k == 0)
    def _():
        state[...] = st_in_ref[...]
        ext[0:8, :] = tail_in_ref[...].astype(F32)[8:16, :]

    ci = ci_ref[...]
    tail_out_ref[...] = ci[q - 16 : q, :]
    ext[8 : 8 + q, :] = ci.astype(F32)
    since = distances(sp, first, q)
    for c in range(0, MIX, 128):
        cols = slice(c, c + 128)
        pre = conv_forward(ext, cw_ref, since, cols, q)
        mix[:, cols] = pre * jax.nn.sigmoid(pre)
    ext[0:8, :] = ext[q : q + 8, :]

    row, col, same, _, stepsize, _, cum, open_w, tail, passed = block_terms(
        sp, first, q, raw_ref[...], cw_ref
    )
    cum_t = cum.T
    keys = mix[:, WIDE : WIDE + STATE]
    kt = keys.T.astype(BF16)
    queries = mix[:, WIDE + STATE :]
    qb = queries.astype(BF16)
    scores = jnp.where(same & (row >= col), split_dot(queries, keys, ABT), 0.0)
    st_ref[...] = state[...]
    flow[...] = split_dot(queries, state[...], AB)
    low = lax.broadcasted_iota(jnp.int32, (q, 2 * HEAD), 1) < HEAD
    tail = tail * stepsize
    for pair in range(LOCAL // 2):
        cols = pair_cols(pair)
        v = mix[:, cols]
        vs = v * pair_lanes(stepsize, pair)
        outs = []
        for h in (2 * pair, 2 * pair + 1):
            damp = jnp.exp(jnp.minimum(cum[:, h : h + 1] - cum_t[h : h + 1, :], 0.0))
            outs.append(split_dot(scores * damp, vs, AB))
        inflow = flow[:, cols] * pair_lanes(open_w, pair)
        y = jnp.where(low, outs[0], outs[1]) + inflow + cw_ref[5:6, cols] * v
        y_ref[:, cols] = y
        fresh[:, cols] = (v * pair_lanes(tail, pair)).astype(BF16)
    update = dot(kt, fresh[...], AB)
    for pair in range(LOCAL // 2):
        cols = pair_cols(pair)
        state[:, cols] = state[:, cols] * pair_lanes(passed, pair) + update[:, cols]
    st_out_ref[...] = state[...]


def scan_rows(sp, seg, conv_in, step_raw, cw, state, tail):
    q = conv_in.shape[0] // CTX

    def here(x):
        return x, pl.BlockSpec((q, x.shape[1]), lambda k, sp: (k ^ sp[0], 0))

    tokens = conv_in.shape[0]
    states = shape((CTX * STATE, WIDE), F32)
    return call(
        "scan_rows",
        functools.partial(scan_kernel, seg),
        sp,
        [here(conv_in), here(step_raw), cw, state, tail],
        [
            here(shape((tokens, WIDE), F32)),
            (states, pl.BlockSpec((STATE, WIDE), lambda k, sp: (k, 0))),
            shape((STATE, WIDE), F32),
            shape((16, MIX), BF16),
        ],
        16,
        grid=CTX,
        scratch=[
            pltpu.VMEM((q + 8, MIX), F32),
            pltpu.VMEM((q, MIX), F32),
            pltpu.VMEM((STATE, WIDE), F32),
            pltpu.VMEM((q, WIDE), F32),
            pltpu.VMEM((q, WIDE), BF16),
        ],
    )


def stat_rows(columns):
    rows = columns[0].shape[0]
    lane = lax.broadcasted_iota(jnp.int32, (rows, 128), 1)
    table = jnp.zeros((rows, 128), F32)
    for i, column in enumerate(columns):
        table = jnp.where(lane == i, column, table)
    return table.T[0:8, :]


def stat_columns(rows):
    return jnp.concatenate([rows, jnp.zeros((120, rows.shape[1]), F32)]).T


def split_rows(row, cols):
    high = row.astype(BF16).astype(F32)
    middle = (row - high).astype(BF16).astype(F32)
    low = row - high - middle
    sub = lax.broadcasted_iota(jnp.int32, (16, row.shape[1]), 0)
    tile = jnp.where(sub == 0, high, jnp.where(sub == 1, middle, jnp.where(sub == 2, low, 0.0)))
    spare = jnp.zeros((16, cols - row.shape[1]), F32)
    return jnp.concatenate([tile, spare], axis=1).astype(BF16)


def stat_row(ref, row, count):
    if ref.dtype == F32:
        return ref[row : row + 1, :count]
    tile = ref[...].astype(F32)
    return tile[0:1, :count] + tile[1:2, :count] + tile[2:3, :count]


def store_slots(part, stat, part_refs):
    own_ref, x_ref, y_ref, late_x_ref, late_y_ref = part_refs
    q = own_ref.shape[0]
    half = q // 2
    part = part.astype(BF16)
    own_ref[...] = part[:q]
    x_ref[:half, :] = part[3 * q : 3 * q + half]
    x_ref[half:q, :] = part[q : q + half]
    y_ref[:half, :] = part[3 * q + half :]
    y_ref[half:q, :] = part[2 * q + half : 3 * q]
    late_x_ref[...] = part[q + half : 2 * q]
    late_y_ref[...] = part[2 * q : 2 * q + half]
    if stat is not None:
        tile = split_rows(stat, part.shape[1])
        x_ref[q:, :] = tile
        y_ref[q:, :] = tile


def store_part(part, stat, part_refs):
    if len(part_refs) == 1:
        part_refs[0][...] = part.astype(BF16)
    else:
        store_slots(part, stat, part_refs)


def part_shapes(slots, tokens, d, extra=0):
    if not slots:
        return [shape((tokens, d), BF16)]
    q = tokens // CTX
    sent = shape((q + extra, d), BF16)
    return [shape((q, d), BF16), sent, sent] + [shape((q // 2, d), BF16)] * 2


def tail_tile(x):
    return x, pl.BlockSpec((16, x.shape[1]), lambda i, sp: (x.shape[0] // 16 - 1, 0))


def head_tile(x):
    return x, pl.BlockSpec((16, x.shape[1]), lambda i, sp: (0, 0))


def turn_kernel(sp, from_x_ref, from_y_ref, late_x_ref, late_y_ref, x_ref, y_ref):
    half = y_ref.shape[0]
    x_ref[:half, :] = (late_x_ref[...].astype(F32) + from_y_ref[:half, :].astype(F32)).astype(BF16)
    y_ref[...] = (late_y_ref[...].astype(F32) + from_x_ref[:half, :].astype(F32)).astype(BF16)
    if x_ref.shape[0] > half:
        x_ref[half:, :] = from_y_ref[2 * half :, :]


def out_kernel(count, before, sp, *refs):
    if before:
        before_ref, refs = refs[0], refs[1:]
    normed_ref, y_ref, cw_ref, wg_ref, wo_ref = refs[count : count + 5]
    gate_ref, stat_ref = refs[count + 5 : count + 7]
    gate = dot(normed_ref[...], wg_ref[...], AB)
    gate_ref[...] = gate
    g = y_ref[...] * gate * jax.nn.sigmoid(gate)
    part = dot((g * cw_ref[9:10, :WIDE]).astype(BF16), wo_ref[...], AB)
    square = jnp.sum(g * g, axis=-1, keepdims=True)
    inner = [
        jnp.sum(part[first : first + u.shape[0]] * u.astype(F32), axis=-1, keepdims=True)
        for first, u in load_rows(refs[:count])
    ]
    rows = stat_rows([square] + ([jnp.concatenate(inner)] if inner else []))
    store_part(part, rows[0:1, :], refs[count + 7 :])
    if before:
        rows = jnp.concatenate([before_ref[...], rows])
    stat_ref[...] = rows


def out_rows(sp, slots, before, pieces, normed, y, cw, wg, wo):
    tokens, d = normed.shape
    return call(
        "out_rows",
        functools.partial(out_kernel, len(pieces), len(before)),
        sp,
        before + pieces + [normed, y, cw, wg, wo],
        [shape((tokens, WIDE), F32), shape((8 + 8 * len(before), tokens), F32)] + part_shapes(slots, tokens, d, 16),
        28,
    )


def slot_sums(stat_refs, row, q):
    out = []
    for slot in range(CTX):
        total = 0.0
        for m, ref in enumerate(stat_refs):
            total = total + stat_row(ref, row, CTX * q)[:, (slot ^ m) * q : (slot ^ m) * q + q]
        out.append(total)
    return jnp.concatenate(out, axis=1)


def own_sum(refs):
    own, from_x, from_y, late_x, late_y = [ref[...].astype(F32) for ref in refs]
    half = late_y.shape[0]
    x = jnp.concatenate([from_x[half : 2 * half], late_x[:half]])
    return own + x + jnp.concatenate([late_y, from_y[half : 2 * half]])


def own_squares(stats, sp, natural, q):
    if not natural:
        rows = [stat_row(ref, 0, CTX * q) for ref in stats]
        return sum(row[:, m * q : m * q + q] for m, row in enumerate(rows))
    place, out = sp[0], []
    block = q // 2
    for half in range(2):
        total = jnp.zeros((1, block), F32)
        for s in range(SEGS):
            for slot in range(CTX):
                here = ((place >> 1) == s) & ((slot ^ place) == 2 * (place & 1) + half)
                for m, ref in enumerate(stats):
                    value = ref[8 * s : 8 * s + 1, pl.ds((slot ^ m) * block, block)]
                    total = total + jnp.where(here, value, 0.0)
        out.append(total)
    return jnp.concatenate(out, axis=1)


def own_kernel(count, natural, sp, *refs):
    stats, partial = refs[:CTX], refs[CTX : CTX + 5]
    residual = jnp.concatenate([x for _, x in load_rows(refs[CTX + 5 : CTX + 5 + count])])
    own_ref, branch_ref = refs[CTX + 5 + count :]
    square = own_squares(stats, sp, natural, own_ref.shape[0])
    square = jnp.concatenate([square, jnp.zeros((7, square.shape[1]), F32)])
    scale = lax.rsqrt(stat_columns(square)[:, 0:1] / INNER + NORM_EPS)
    branch = own_sum(partial) * scale
    branch_ref[...] = branch
    own_ref[...] = (residual.astype(F32) + branch).astype(BF16)


def own_rows(sp, natural, stats, partial, residual):
    q, d = partial[0].shape
    return call(
        "own_rows",
        functools.partial(own_kernel, len(residual), natural),
        sp,
        stats + partial + residual,
        [shape((q, d), BF16), shape((q, d), F32)],
        16,
    )


def collect_kernel(sp, part0_ref, part1_ref, own_ref, x_ref, y_ref, late_x_ref, late_y_ref):
    place = sp[0]
    q = late_x_ref.shape[0]
    goals = [
        [own_ref.at[pl.ds(0, q)], own_ref.at[pl.ds(q, q)]],
        [x_ref.at[pl.ds(q, q)], late_x_ref],
        [late_y_ref, y_ref.at[pl.ds(q, q)]],
        [x_ref.at[pl.ds(0, q)], y_ref.at[pl.ds(0, q)]],
    ]
    for m in range(CTX):
        owner = place ^ m
        for half in range(2):
            slot = (2 * (owner & 1) + half) ^ place
            rows = pl.ds(pl.multiple_of(slot * q, q), q)
            goals[m][half][...] = choose((owner >> 1) == 0, part0_ref[rows, :], part1_ref[rows, :])


def collect(sp, parts):
    tokens, d = parts[0].shape
    return call("collect", collect_kernel, sp, list(parts), part_shapes(True, 2 * tokens, d), 20)


def natural_kernel(extra, sp, *refs):
    out_ref = refs[-1]
    q = out_ref.shape[0] // 2
    for place in range(CTX):
        s = place >> 1
        own, x, y, first, second = refs[5 * s : 5 * s + 5]

        @pl.when(sp[0] == place)
        def _():
            for half in range(2):
                slot = (2 * (place & 1) + half) ^ place
                at = half * q
                if slot < 3:
                    out_ref[at : at + q, :] = (own, x, y)[slot][extra:, :]
                else:
                    out_ref[at : at + q // 2, :] = first[extra:, :]
                    out_ref[at + q // 2 : at + q, :] = second[...]


def natural_rows(sp, pieces, extra=0):
    q, d = pieces[0][0].shape
    ins = [x for one in pieces for x in one]
    kernel = functools.partial(natural_kernel, extra)
    return call("natural_rows", kernel, sp, ins, [shape((2 * (q - extra), d), BF16)])[0]


def gate_back_kernel(count, inners, first_stat, sp, *refs):
    pieces, stats = refs[:count], refs[count : count + CTX]
    inner_refs = refs[count + CTX : count + CTX + inners]
    rest = refs[count + CTX + inners :]
    y_ref, gate_ref, cw_ref, wo_ref, dy_ref, dgate_ref, gated_ref, u_ref, dgain_ref = rest
    gain = cw_ref[9:10, :WIDE]
    tokens = y_ref.shape[0]
    q = tokens // CTX
    for first, u in load_rows(pieces, 16 if inners else 0):
        u_ref[pl.ds(first, u.shape[0]), :] = u
    back = dot(u_ref[...], wo_ref[...], ABT)
    scale = lax.rsqrt(slot_sums(stats, first_stat, q) / INNER + NORM_EPS)
    if inners:
        inner = jnp.concatenate([stat_row(ref, 0, q) for ref in inner_refs], axis=1)
    else:
        inner = slot_sums(stats, first_stat + 1, q) * scale
    pull = scale * scale * inner / INNER
    table = stat_columns(jnp.concatenate([scale, pull, jnp.zeros((6, tokens), F32)]))
    scale, pull = table[:, 0:1], table[:, 1:2]
    gate = gate_ref[...]
    y = y_ref[...]
    sig = jax.nn.sigmoid(gate)
    act = gate * sig
    g = y * act
    unit = g * scale
    gated_ref[...] = (unit * gain).astype(BF16)
    dg = back * gain * scale - g * pull
    dy_ref[...] = (dg * act).astype(BF16)
    dgate_ref[...] = (dg * y * (sig + act * (1.0 - sig))).astype(BF16)
    dgain_ref[...] = jnp.broadcast_to(jnp.sum(back * unit, axis=0, keepdims=True), (8, WIDE))


def gate_back(sp, pieces, stats, first_stat, inners, y, gate, cw, wo):
    tokens, d = y.shape[0], wo.shape[1]
    return call(
        "gate_back",
        functools.partial(gate_back_kernel, len(pieces), len(inners), first_stat),
        sp,
        pieces + stats + inners + [y, gate, cw, wo],
        [shape((tokens, WIDE), BF16)] * 3 + [shape((tokens, d), BF16), shape((8, WIDE), F32)],
        28,
    )


def scan_back_kernel(
    seg,
    sp,
    ci_ref,
    prev_ref,
    raw_ref,
    dy_ref,
    st_ref,
    tail_in_ref,
    cw_ref,
    dst_in_ref,
    next_in_ref,
    dci_ref,
    dcw_ref,
    dhp_ref,
    dst_out_ref,
    next_out_ref,
    ext,
    mix,
    slope,
    dext,
    dstate,
    tails,
    dyw,
    flow,
    kept_all,
    ends,
):
    i = pl.program_id(0)
    k = CTX - 1 - i
    q = ci_ref.shape[0]
    first = (CTX * seg + k) * q

    @pl.when(i == 0)
    def _():
        dstate[...] = dst_in_ref[...]
        dext[q : q + 8, :] = next_in_ref[...]
        ends[...] = jnp.zeros_like(ends)
        dcw_ref[...] = jnp.zeros_like(dcw_ref)
        dhp_ref[...] = jnp.zeros_like(dhp_ref)

    @pl.when(k == 0)
    def _():
        ext[0:8, :] = tail_in_ref[...].astype(F32)[8:16, :]

    @pl.when(k > 0)
    def _():
        ext[0:8, :] = prev_ref[...].astype(F32)[8:16, :]

    ext[8 : 8 + q, :] = ci_ref[...].astype(F32)
    since = distances(sp, first, q + 8)
    for c in range(0, MIX, 128):
        cols = slice(c, c + 128)
        pre = conv_forward(ext, cw_ref, since[0:q], cols, q)
        sig = jax.nn.sigmoid(pre)
        act = pre * sig
        mix[:, cols] = act
        slope[:, cols] = sig + act * (1.0 - sig)

    row, col, same, shifted, stepsize, decay, cum, open_w, tail, passed = block_terms(
        sp, first, q, raw_ref[...], cw_ref
    )
    cum_t = cum.T
    keys = mix[:, WIDE : WIDE + STATE]
    kb = keys.astype(BF16)
    queries = mix[:, WIDE + STATE :]
    qb = queries.astype(BF16)
    qt = queries.T.astype(BF16)
    inside = same & (col >= row)
    scores = jnp.where(inside, split_dot(keys, queries, ABT), 0.0)
    stb, dstb = st_ref[...].astype(BF16), dstate[...].astype(BF16)
    flow[...] = dot(qb, stb, AB)
    kept_all[...] = dot(kb, dstb, AB)
    low = lax.broadcasted_iota(jnp.int32, (q, 2 * HEAD), 1) < HEAD
    lane = lax.broadcasted_iota(jnp.int32, (q, 128), 1)
    sub = lax.broadcasted_iota(jnp.int32, (16, q), 0)
    dscores = jnp.zeros((q, q), F32)
    plus_t = jnp.zeros((16, q), F32)
    dstep = jnp.zeros((q, 128), F32)
    dcum = jnp.zeros((q, 128), F32)
    for pair in range(LOCAL // 2):
        cols = pair_cols(pair)
        v = mix[:, cols]
        step_e = pair_lanes(stepsize, pair)
        vs = v * step_e
        vsb = vs.astype(BF16)
        dyb = dy_ref[:, cols]
        dyf = dyb.astype(F32)
        dvs = []
        for side, h in ((0, 2 * pair), (1, 2 * pair + 1)):
            mine = low if side == 0 else ~low
            damp = jnp.exp(jnp.minimum(cum_t[h : h + 1, :] - cum[:, h : h + 1], 0.0))
            raw = dot(jnp.where(mine, vs, 0.0).astype(BF16), dyb, ABT)
            mixing = (scores * damp).astype(BF16)
            dscores = dscores + raw * damp
            both = raw * mixing.astype(F32)
            plus_t = plus_t + jnp.where(sub == h, jnp.sum(both, axis=0, keepdims=True), 0.0)
            dvs.append(dot(mixing, dyb, AB))
        dv = jnp.where(low, dvs[0], dvs[1])
        weighted = dyf * pair_lanes(open_w, pair)
        dyw[:, cols] = weighted.astype(BF16)
        tail_e = pair_lanes(tail, pair)
        kept = kept_all[:, cols] * tail_e
        tails[:, cols] = (vs * tail_e).astype(BF16)
        u = dv + kept
        dext[0:q, cols] = (u * step_e + cw_ref[5:6, cols] * dyf) * slope[:, cols]
        from_tail = kept * vs
        dcw_ref[5:6, cols] += jnp.sum(dyf * v, axis=0, keepdims=True)
        ends[1:2, cols] = jnp.sum(from_tail, axis=0, keepdims=True)
        uv = u * v
        change = weighted * flow[:, cols] - dv * vsb.astype(F32) - from_tail
        for side, h in ((0, 2 * pair), (1, 2 * pair + 1)):
            mine = low if side == 0 else ~low

            def per_row(x):
                return jnp.sum(jnp.where(mine, x, 0.0), axis=1, keepdims=True)

            dstep = jnp.where(lane == h, per_row(uv), dstep)
            dcum = jnp.where(lane == h, per_row(change), dcum)

    dcum = dcum + jnp.concatenate([plus_t, jnp.zeros((112, q), F32)]).T
    ends[0:1, :] = jnp.sum(st_ref[...] * dstate[...], axis=0, keepdims=True)
    by_head = dot(ends[...], channel_map(), AB, HIGH)
    at_end = by_head[0:1, :] * passed + by_head[1:2, :]
    dcum = dcum + jnp.where(row == q - 1, at_end, 0.0)
    upper = jnp.where(col >= row, 1.0, 0.0)
    ddecay = dot(upper, dcum, AB, HIGH)
    draw = (dstep - ddecay * cw_ref[11:12, 0:128]) * jax.nn.sigmoid(shifted)
    dci_ref[:, MIX:] = draw.astype(BF16)
    dhp_ref[0:1, :] += jnp.sum(draw, axis=0, keepdims=True)
    dhp_ref[1:2, :] += jnp.sum(ddecay * decay, axis=0, keepdims=True)

    dsb = jnp.where(inside, dscores, 0.0).astype(BF16)
    dkeys = dot(dsb, qb, AB) + dot(tails[...], dstb, ABT)
    dqueries = dot(dsb, kb, ATB) + dot(dyw[...], stb, ABT)
    kcols, qcols = slice(WIDE, WIDE + STATE), slice(WIDE + STATE, MIX)
    dext[0:q, kcols] = dkeys * slope[:, kcols]
    dext[0:q, qcols] = dqueries * slope[:, qcols]
    update = dot(qt, dyw[...], AB)
    for pair in range(LOCAL // 2):
        cols = pair_cols(pair)
        dstate[:, cols] = dstate[:, cols] * pair_lanes(passed, pair) + update[:, cols]
    dst_out_ref[...] = dstate[...]

    for c in range(0, MIX, 128):
        cols = slice(c, c + 128)
        here = dext[0:q, cols]
        total = cw_ref[3:4, cols] * here
        dcw_ref[3:4, cols] += jnp.sum(here * ext[8 : 8 + q, cols], axis=0, keepdims=True)
        dcw_ref[4:5, cols] += jnp.sum(here, axis=0, keepdims=True)
        for shift in range(1, CONV):
            later = jnp.where(since[shift : shift + q] >= shift, dext[shift : shift + q, cols], 0.0)
            total = total + cw_ref[3 - shift : 4 - shift, cols] * later
            used = jnp.where(since[0:q] >= shift, ext[8 - shift : 8 - shift + q, cols], 0.0)
            dcw_ref[3 - shift : 4 - shift, cols] += jnp.sum(here * used, axis=0, keepdims=True)
        dci_ref[:, cols] = total.astype(BF16)
    head_rows = dext[0:8, :]
    dext[q : q + 8, :] = head_rows
    next_out_ref[...] = head_rows


def scan_back(sp, seg, conv_in, step_raw, dy, states, tail, cw, dstate, following):
    tokens = conv_in.shape[0]
    q = tokens // CTX

    def here(x):
        return x, pl.BlockSpec((q, x.shape[1]), lambda i, sp: ((CTX - 1 - i) ^ sp[0], 0))

    def before(i, sp):
        return (jnp.maximum(CTX - 2 - i, 0) ^ sp[0]) * (q // 16) + q // 16 - 1, 0

    return call(
        "scan_back",
        functools.partial(scan_back_kernel, seg),
        sp,
        [
            here(conv_in),
            (conv_in, pl.BlockSpec((16, MIX), before)),
            here(step_raw),
            here(dy),
            (states, pl.BlockSpec((STATE, WIDE), lambda i, sp: (CTX - 1 - i, 0))),
            tail,
            cw,
            dstate,
            following,
        ],
        [
            here(shape((tokens, FULL), BF16)),
            shape((8, MIX), F32),
            shape((8, 128), F32),
            shape((STATE, WIDE), F32),
            shape((8, MIX), F32),
        ],
        24,
        grid=CTX,
        scratch=[
            pltpu.VMEM((q + 8, MIX), F32),
            pltpu.VMEM((q, MIX), F32),
            pltpu.VMEM((q, MIX), F32),
            pltpu.VMEM((q + 8, MIX), F32),
            pltpu.VMEM((STATE, WIDE), F32),
            pltpu.VMEM((q, WIDE), BF16),
            pltpu.VMEM((q, WIDE), BF16),
            pltpu.VMEM((q, WIDE), F32),
            pltpu.VMEM((q, WIDE), F32),
            pltpu.VMEM((8, WIDE), F32),
        ],
    )


def input_back_kernel(sp, dc_ref, dg_ref, wc_ref, wg_ref, *part_refs):
    part = dot(dc_ref[...], wc_ref[...], ABT) + dot(dg_ref[...], wg_ref[...], ABT)
    store_part(part, None, part_refs)


def input_back(sp, slots, dconv, dgate, wc, wg):
    outs = part_shapes(slots, dconv.shape[0], wc.shape[0])
    return call("input_back", input_back_kernel, sp, [dconv, dgate, wc, wg], outs, 24)


def own_back_kernel(count, sp, *refs):
    partial, rest = refs[:5], refs[5:]
    x = jnp.concatenate([v for _, v in load_rows(rest[:count])]).astype(F32)
    u = jnp.concatenate([v for _, v in load_rows(rest[count : 2 * count])]).astype(F32)
    cw_ref, branch_ref, up_ref, dnorm_ref = rest[2 * count :]
    grad = own_sum(partial)
    scale = row_scale(x)
    gained = grad * cw_ref[8:9, :]
    centre = jnp.mean(gained * x, axis=-1, keepdims=True)
    up = (u + scale * (gained - x * (scale * scale * centre))).astype(BF16)
    extra = up_ref.shape[0] - up.shape[0]
    up_ref[extra:, :] = up
    if extra:
        inner = jnp.sum(up.astype(F32) * branch_ref[...], axis=-1, keepdims=True)
        up_ref[:extra, :] = split_rows(stat_rows([inner])[0:1, :], up.shape[1])
    dnorm_ref[...] = jnp.broadcast_to(
        jnp.sum(grad * x * scale, axis=0, keepdims=True), dnorm_ref.shape
    )


def own_back(sp, extra, partial, x, u, cw, branch):
    q, d = partial[0].shape
    return call(
        "own_back",
        functools.partial(own_back_kernel, len(x)),
        sp,
        partial + x + u + [cw, branch],
        [shape((q + extra, d), BF16), shape((8, d), F32)],
    )


def head_map(group, block, flipped=False):
    here = lax.broadcasted_iota(jnp.int32, (128, 128), 1 if flipped else 0)
    there = lax.broadcasted_iota(jnp.int32, (128, 128), 0 if flipped else 1)
    turn = jnp.zeros_like(here)
    for edge in range(block, LOCAL, block):
        turn = turn + jnp.where(here >= edge, 1, 0)
    goal = here + (turn * (CTX - 1) + group) * block
    return jnp.where((here < LOCAL) & (there == goal), 1.0, 0.0)


def channel_map(flipped=False):
    dims = (128, WIDE) if flipped else (WIDE, 128)
    chan = lax.broadcasted_iota(jnp.int32, dims, 1 if flipped else 0)
    head = lax.broadcasted_iota(jnp.int32, dims, 0 if flipped else 1)
    return jnp.where((chan >= head * HEAD) & (chan < (head + 1) * HEAD), 1.0, 0.0)


def spans(group, block):
    wide = block * HEAD
    return [(z * wide, (z * CTX + group) * wide, wide) for z in range(WIDE // wide)]


def choose(first, a, b):
    return jnp.where(first, a, b)


def pack_kernel(block, sp, w_ref, *refs):
    conv_refs, gate_refs, conv, gate = refs[:CTX], refs[CTX : 2 * CTX], refs[-2], refs[-1]
    place = sp[0]
    keys = w_ref[:, 2 * INNER : 2 * INNER + STATE]
    queries = w_ref[:, 2 * INNER + STATE : 2 * INNER + 2 * STATE]
    steps = w_ref[:, 2 * INNER + 2 * STATE :]
    rows = w_ref.shape[0]
    steps = jnp.concatenate([steps, jnp.zeros((rows, 128 - HEADS), BF16)], axis=1)
    for k in range(CTX):
        values = jnp.concatenate(
            [w_ref[:, INNER + there : INNER + there + n] for _, there, n in spans(k, block)], axis=1
        )
        gates = jnp.concatenate(
            [w_ref[:, there : there + n] for _, there, n in spans(k, block)], axis=1
        )
        step = dot(steps, head_map(k, block, True).astype(BF16), AB).astype(BF16)
        conv[k] = jnp.concatenate(
            [values[:, :HALF], keys, step, values[:, HALF:], queries, step], axis=1
        )
        gate[k] = gates
    for m in range(CTX):
        conv_refs[m][...] = conv[m ^ place]
        gate_refs[m][...] = gate[m ^ place]


def pack(sp, block, w_in):
    rows = w_in.shape[0]
    outs = call(
        "pack",
        functools.partial(pack_kernel, block),
        sp,
        [w_in],
        [shape((rows, 2 * LOAD), BF16)] * CTX + [shape((rows, WIDE), BF16)] * CTX,
        16,
        scratch=[
            pltpu.VMEM((CTX, rows, 2 * LOAD), BF16),
            pltpu.VMEM((CTX, rows, WIDE), BF16),
        ],
    )
    return outs[:CTX], outs[CTX:]


def order_conv_kernel(sp, *refs):
    keep_ref, send_ref = refs[CTX:]
    zero = sp[1] == 0
    for m in range(CTX):
        low, high = refs[m][:, :LOAD], refs[m][:, LOAD:]
        keep_ref[m ^ sp[0]] = choose(zero, low, high)
        send_ref[m ^ sp[0]] = choose(zero, high, low)


def order_conv(sp, slots):
    out = shape((CTX, slots[0].shape[0], LOAD), BF16)
    return call("order_conv", order_conv_kernel, sp, slots, [out, out], 12)


def order_gate_kernel(sp, *refs):
    out_ref, keep_ref, send_ref = refs[CTX:]
    zero = sp[1] == 0
    rows = keep_ref.shape[1]
    for m in range(CTX):
        low, high = refs[m][:, :HALF], refs[m][:, HALF:]
        keep_ref[m ^ sp[0], :, :HALF] = choose(zero, low, high)
        send_ref[m ^ sp[0], :, :HALF] = choose(zero, high, low)
    for r in range(2):
        for c in range(2):
            at = slice(r * rows, (r + 1) * rows)
            low = out_ref[at, c * HALF : (c + 1) * HALF]
            high = out_ref[at, (2 + c) * HALF : (3 + c) * HALF]
            keep_ref[2 * r + c, :, HALF:] = choose(zero, low, high)
            send_ref[2 * r + c, :, HALF:] = choose(zero, high, low)


def order_gate(sp, slots, w_out):
    out = shape((CTX, slots[0].shape[0], WIDE), BF16)
    return call("order_gate", order_gate_kernel, sp, slots + [w_out], [out, out], 12)


def join_conv_kernel(sp, mine_ref, other_ref, wc_ref):
    zero = sp[1] == 0
    rows = mine_ref.shape[2]
    for i in range(CTX):
        a, b = mine_ref[0, i, :, :LOAD], other_ref[0, i, :, :LOAD]
        low, high = choose(zero, a, b), choose(zero, b, a)
        at = slice(i * rows, (i + 1) * rows)
        wc_ref[at, 0:HALF] = low[:, :HALF]
        wc_ref[at, HALF:WIDE] = high[:, :HALF]
        wc_ref[at, WIDE : WIDE + STATE] = low[:, HALF : HALF + STATE]
        wc_ref[at, WIDE + STATE : MIX] = high[:, HALF : HALF + STATE]
        wc_ref[at, MIX:] = low[:, HALF + STATE :]


def by_rows(x, count):
    return x, pl.BlockSpec((x.shape[0] // count, x.shape[1]), lambda z, sp: (z, 0))


def join_conv(sp, mine, other):
    dp, _, rows, _ = mine.shape
    out = by_rows(shape((dp * CTX * rows, FULL), BF16), dp)
    ins = [by_first(mine), by_first(other)]
    return call("join_conv", join_conv_kernel, sp, ins, [out], 12, dp)[0]


def join_gate_kernel(first, sp, mine_ref, other_ref, wg_ref, wo_ref):
    zero = sp[1] == 0
    rows = mine_ref.shape[2]
    for i in range(CTX):
        a, b = mine_ref[0, i, :, first:], other_ref[0, i, :, first:]
        low, high = choose(zero, a, b), choose(zero, b, a)
        at = slice(i * rows, (i + 1) * rows)
        wg_ref[at, :HALF] = low[:, :HALF]
        wg_ref[at, HALF:] = high[:, :HALF]
        r, c = i // 2, i % 2
        at = slice(r * rows, (r + 1) * rows)
        wo_ref[at, c * HALF : (c + 1) * HALF] = low[:, HALF:]
        wo_ref[at, (2 + c) * HALF : (3 + c) * HALF] = high[:, HALF:]


def join_gate(sp, mine, other):
    dp, _, rows, cols = mine.shape
    wg, wo = shape((dp * CTX * rows, WIDE), BF16), shape((dp * 2 * rows, 4 * HALF), BF16)
    outs = [by_rows(wg, dp), by_rows(wo, dp)]
    kernel = functools.partial(join_gate_kernel, cols - WIDE)
    ins = [by_first(mine), by_first(other)]
    return call("join_gate", kernel, sp, ins, outs, 12, dp)


def fold_kernel(sp, keep_ref, came_ref, out_ref):
    out_ref[...] = (keep_ref[...].astype(F32) + came_ref[...].astype(F32)).astype(BF16)


def fold(sp, keep, came):
    ins = [by_first(keep), by_first(came)]
    return call("fold", fold_kernel, sp, ins, [by_first(shape(keep.shape, BF16))], 24, keep.shape[0])


def total_kernel(counts, sp, *refs):
    for m in range(CTX):
        parts = [ref[m ^ sp[0], :, :cols] for ref, cols in zip(refs, counts)]
        refs[len(counts) + m][...] = jnp.concatenate(parts, axis=1)


def total_line(sp, sums):
    width = {LOAD: LOAD, WIDE: HALF}
    counts = [width[x.shape[2]] for x in sums]
    outs = [shape((sums[0].shape[1], sum(counts)), BF16)] * CTX
    return call("total_line", functools.partial(total_kernel, counts), sp, sums, outs)


def mix_kernel(cols, sp, *refs):
    out_ref = refs[-1]
    zero = sp[1] == 0
    for m in range(CTX):
        if cols == LOAD:
            mine, other = refs[CTX + m][...], refs[m][:, :LOAD]
        else:
            mine, other = refs[m][:, LOAD + HALF :], refs[m][:, LOAD : LOAD + HALF]
            out_ref[m, :, HALF:] = choose(zero, refs[CTX + 1][m, :, HALF:], refs[CTX][m, :, HALF:])
        out_ref[m, :, : mine.shape[1]] = choose(zero, other, mine)


def mix(sp, early, late, cols):
    out = shape((CTX, early[0].shape[0], cols), BF16)
    return call("mix", functools.partial(mix_kernel, cols), sp, early + late, [out])[0]


def grad_conv_kernel(sp, n0_ref, n1_ref, d0_ref, d1_ref, keep_ref, send_ref):
    zero = sp[1] == 0
    rows = keep_ref.shape[2]
    total = dot(n0_ref[...], d0_ref[...], ATB) + dot(n1_ref[...], d1_ref[...], ATB)
    total = total.astype(BF16)
    step = total[:, MIX:]
    low = jnp.concatenate([total[:, :HALF], total[:, WIDE : WIDE + STATE], step], axis=1)
    high = jnp.concatenate([total[:, HALF:WIDE], total[:, WIDE + STATE : MIX], step], axis=1)
    keep, send = choose(zero, low, high), choose(zero, high, low)
    for i in range(CTX):
        keep_ref[0, i] = keep[i * rows : (i + 1) * rows]
        send_ref[0, i] = send[i * rows : (i + 1) * rows]


def by_first(x):
    rest = (0,) * (len(x.shape) - 1)
    return x, pl.BlockSpec((1,) + tuple(x.shape[1:]), lambda z, sp: (z,) + rest)


def by_cols(x, count):
    return x, pl.BlockSpec((x.shape[0], x.shape[1] // count), lambda z, sp: (0, z))


def grad_conv(sp, dp, rows, normed, dconv):
    out = shape((dp, CTX, rows, LOAD), BF16)
    return call(
        "grad_conv",
        grad_conv_kernel,
        sp,
        [by_cols(x, dp) for x in normed] + list(dconv),
        [by_first(out), by_first(out)],
        24,
        dp,
    )


def grad_gate_kernel(sp, *refs):
    n_refs, dg_refs, gated_refs, u_refs = refs[0:2], refs[2:4], refs[4:6], refs[6:8]
    keep_ref, send_ref = refs[8:]
    z = pl.program_id(0)
    dp, _, rows, _ = keep_ref.shape
    zero = sp[1] == 0

    def over_tokens(a, b):
        return dot(a[0][...], b[0][...], ATB) + dot(a[1][...], b[1][...], ATB)

    total = over_tokens(n_refs, dg_refs).astype(BF16)
    keep = choose(zero, total[:, :HALF], total[:, HALF:])
    send = choose(zero, total[:, HALF:], total[:, :HALF])
    for i in range(CTX):
        keep_ref[z, i, :, :HALF] = keep[i * rows : (i + 1) * rows]
        send_ref[z, i, :, :HALF] = send[i * rows : (i + 1) * rows]
    total = over_tokens(gated_refs, u_refs).astype(BF16)
    side, c = z // 2, lax.rem(z, 2)

    def put(ref):
        for there in range(dp):
            for r in range(2):
                first = (2 * there + r) * rows
                ref[there, 2 * r + c, :, HALF:] = total[first : first + rows]

    @pl.when(side == sp[1])
    def _():
        put(keep_ref)

    @pl.when(side != sp[1])
    def _():
        put(send_ref)


def grad_gate(sp, dp, rows, normed, dgate, gated, u):
    out = shape((dp, CTX, rows, WIDE), BF16)
    return call(
        "grad_gate",
        grad_gate_kernel,
        sp,
        [by_cols(x, dp) for x in normed]
        + list(dgate)
        + list(gated)
        + [by_cols(x, dp) for x in u],
        [out, out],
        32,
        dp,
    )


def finish_kernel(block, sp, *refs):
    early, late, (gate0, gate1, came_gate, came_conv) = refs[:4], refs[4:8], refs[8:12]
    in_ref, out_ref, lows, highs, glows, ghighs = refs[12:]
    place, zero = sp[0], sp[1] == 0
    rows = in_ref.shape[0]
    for m in range(CTX):
        mine, came = choose(zero, late[m][...], early[m][:, :LOAD]), came_conv[m]
        lows[m ^ place] = choose(zero, mine, came).astype(F32)
        highs[m ^ place] = choose(zero, came, mine).astype(F32)
        mine = choose(zero, early[m][:, LOAD + HALF :], early[m][:, LOAD : LOAD + HALF])
        came = came_gate[m, :, :HALF]
        glows[m ^ place] = choose(zero, mine, came).astype(F32)
        ghighs[m ^ place] = choose(zero, came, mine).astype(F32)
    keys, queries, steps = 0.0, 0.0, 0.0
    for k in range(CTX):
        keys = keys + lows[k, :, HALF : HALF + STATE]
        queries = queries + highs[k, :, HALF : HALF + STATE]
        steps = steps + dot(lows[k, :, HALF + STATE :], head_map(k, block), AB, HIGH)
    for z in range(WIDE // (block * HEAD)):
        def side_by_side(a, b):
            parts = []
            for k in range(CTX):
                here, _, n = spans(k, block)[z]
                source = a if here < HALF else b
                parts.append(source[k, :, here % HALF : here % HALF + n])
            return jnp.concatenate(parts, axis=1)

        wide = CTX * block * HEAD
        in_ref[:, z * wide : (z + 1) * wide] = side_by_side(glows, ghighs)
        in_ref[:, INNER + z * wide : INNER + (z + 1) * wide] = side_by_side(lows, highs)
    in_ref[:, 2 * INNER : 2 * INNER + STATE] = keys
    in_ref[:, 2 * INNER + STATE : 2 * INNER + 2 * STATE] = queries
    in_ref[:, 2 * INNER + 2 * STATE :] = steps[:, :HEADS]
    for i in range(4):
        r, c = i // 2, i % 2
        mine, came = choose(zero, gate0[i, :, HALF:], gate1[i, :, HALF:]), came_gate[i, :, HALF:]
        at = slice(r * rows, (r + 1) * rows)
        out_ref[at, c * HALF : (c + 1) * HALF] = choose(zero, mine, came).astype(F32)
        out_ref[at, (2 + c) * HALF : (3 + c) * HALF] = choose(zero, came, mine).astype(F32)


def finish(sp, block, early, late, gates, came_gate, came_conv):
    rows = came_conv.shape[1]
    return call(
        "finish",
        functools.partial(finish_kernel, block),
        sp,
        early + late + gates + [came_gate, came_conv],
        [shape((rows, 2 * INNER + 2 * STATE + HEADS), F32), shape((2 * rows, 4 * HALF), F32)],
        24,
        scratch=[pltpu.VMEM((CTX, rows, LOAD), F32)] * 2 + [pltpu.VMEM((CTX, rows, HALF), F32)] * 2,
    )


class Direct:
    def __init__(self, order, mine, dp, block, w_in, w_out):
        self.order, self.mine, self.dp, self.block = order, mine, dp, block
        self.rows = w_in.shape[0]
        conv, gate = order(pack, block, w_in)
        conv = order(order_conv, [flip(x, m) if m else x for m, x in enumerate(conv)])
        self.conv = self.trade(*conv)
        self.first = self.gathered(self.conv[0])
        gate = [order.now(x) for x in gate]
        self.slots = [flip(x, m) if m else x for m, x in enumerate(gate)]
        self.w_out = w_out

    def prepare_gate(self):
        self.gate = self.trade(*self.order(order_gate, self.slots, self.w_out))

    def trade(self, keep, send):
        came = swap_core(send)
        return choose(self.mine == 0, keep, came), choose(self.mine == 0, came, keep)

    def gathered(self, x):
        return lax.all_gather(x, "dp", axis=0)

    def start_conv(self):
        return self.first

    def start_gate(self, after):
        x, _ = lax.optimization_barrier((self.order.now(self.gate[0]), after))
        return self.gathered(x)

    def start_second(self):
        return self.gathered(self.order.now(self.conv[1])), self.gathered(self.order.now(self.gate[1]))

    def trade_weights(self, x):
        x = self.order.now(x)
        return x, swap_core(x)

    def conv_weights(self, sp, both):
        return join_conv(sp, *both)

    def gate_weights(self, sp, both):
        return join_gate(sp, *both)

    def grad_gate(self, sp, layer, normed, dgate, gated, u):
        return grad_gate(sp, self.dp, self.rows, normed, dgate, gated, u)

    def grad_conv(self, sp, layer, normed, dconv):
        return grad_conv(sp, self.dp, self.rows, normed, dconv)

    def trade_grads(self, grads):
        return grads[0], swap_core(grads[1])

    def send(self, traded):
        (total,) = self.order(fold, *traded)
        return lax.psum_scatter(total, "dp", scatter_dimension=0, tiled=True)[0]

    def early(self, conv1, gate1, gate0):
        self.gates = [gate0, gate1]
        slots = self.order(total_line, [conv1, gate1, gate0])
        self.slots = [flip(x, m) if m else x for m, x in enumerate(slots)]

    def early_trade(self):
        self.came = swap_core(self.order(mix, self.slots, self.gates, WIDE))

    def gradients(self, conv0):
        late = self.order(total_line, [conv0])
        late = [flip(x, m) if m else x for m, x in enumerate(late)]
        came = swap_core(self.order(mix, self.slots, late, LOAD))
        return self.order(finish, self.block, self.slots, late, self.gates, self.came, came)


def grouped(columns, block):
    lead = columns.shape[:-1]
    split = jnp.moveaxis(columns.reshape(lead + (-1, CTX, block)), -2, 0)
    return split.reshape((CTX,) + lead + (-1,))


def ungrouped(groups, block):
    lead = groups.shape[1:-1]
    split = groups.reshape((CTX,) + lead + (-1, block))
    return jnp.moveaxis(split, 0, -2).reshape(lead + (-1,))


def pad_to(x, rows, cols):
    room = [(0, 0)] * (x.ndim - 2) + [(0, rows - x.shape[-2]), (0, cols - x.shape[-1])]
    return jnp.pad(x, room)


class Plain:
    def __init__(self, mine, place, block, w_in, w_out):
        self.mine, self.place, self.block = mine, place, block
        full_in = lax.all_gather(w_in, ("dp", "ctx"), axis=0, tiled=True)
        full_out = lax.all_gather(w_out, ("dp", "ctx"), axis=0, tiled=True)
        self.full = [(full_in, full_out), (swap_core(full_in), swap_core(full_out))]
        self.grads = [{}, {}]

    def prepare_gate(self):
        pass

    def start_conv(self):
        return 0

    def start_gate(self, after):
        return 0

    def start_second(self):
        return 1, 1

    def trade_weights(self, layer):
        return layer

    def trade_grads(self, grads):
        return grads

    def send(self, traded):
        return traded

    def early(self, conv1, gate1, gate0):
        pass

    def early_trade(self):
        pass

    def group(self, columns, block):
        return lax.dynamic_index_in_dim(grouped(columns, block), self.place, 0, False)

    def layer(self, layer, which):
        return choose(self.mine == layer, self.full[0][which], self.full[1][which])

    def conv_weights(self, sp, layer):
        one = self.layer(layer, 0)
        values = self.group(one[:, INNER : 2 * INNER], self.block * HEAD)
        step = self.group(one[:, 2 * INNER + 2 * STATE :], self.block)
        shared = one[:, 2 * INNER : 2 * INNER + 2 * STATE]
        return jnp.concatenate([values, shared, pad_to(step, step.shape[0], 128)], 1)

    def gate_weights(self, sp, layer):
        one, out = self.layer(layer, 0), self.layer(layer, 1)
        wide = self.block * HEAD
        return self.group(one[:, :INNER], wide), self.group(out.T, wide).T

    def over_tokens(self, a, b):
        both = [dot(x, y, ATB) for x, y in zip(a, b)]
        return (both[0] + both[1]).astype(BF16)

    def grad_gate(self, sp, layer, normed, dgate, gated, u):
        out = self.over_tokens(gated, u)
        self.grads[layer].update(gate=self.over_tokens(normed, dgate), out=out)
        return [out]

    def grad_conv(self, sp, layer, normed, dconv):
        self.grads[layer].update(conv=self.over_tokens(normed, dconv))
        return [self.grads[layer]["conv"]]

    def spread(self, columns, block):
        at = lax.broadcasted_iota(jnp.int32, (CTX, 1, 1), 0) == self.place
        return ungrouped(jnp.where(at, columns[None], jnp.zeros((), columns.dtype)), block)

    def gradients(self, conv0):
        wide = self.block * HEAD
        fulls = []
        for grads in self.grads:
            gate, conv = grads["gate"], grads["conv"]
            grad_in = jnp.concatenate(
                [
                    self.spread(gate, wide),
                    self.spread(conv[:, :WIDE], wide),
                    conv[:, WIDE:MIX],
                    self.spread(conv[:, MIX : MIX + LOCAL], self.block),
                ],
                -1,
            )
            fulls.append((grad_in, self.spread(grads["out"].T, wide).T))
        sums = []
        for a, b in zip(*fulls):
            zero = self.mine == 0
            total = choose(zero, a, b).astype(F32) + swap_core(choose(zero, b, a)).astype(F32)
            total = total.astype(BF16)
            sums.append(
                lax.psum_scatter(total, ("dp", "ctx"), scatter_dimension=0, tiled=True).astype(F32)
            )
        return sums[0], sums[1]


def prepare_kernel(block, sp, norm_ref, taps_ref, bias_ref, dt_ref, log_ref, skip_ref, gain_ref, out_ref):
    out_ref[...] = jnp.zeros_like(out_ref)
    for k in range(CTX):

        @pl.when(sp[0] == k)
        def _():
            for here, there, n in spans(k, block):
                out_ref[0:CONV, here : here + n] = taps_ref[0, :, there : there + n]
                out_ref[4:5, here : here + n] = bias_ref[:, there : there + n]
                out_ref[9:10, here : here + n] = gain_ref[:, there : there + n]
            spare = jnp.zeros((1, 128 - HEADS), F32)
            rows = [jnp.concatenate([ref[...], spare], axis=1) for ref in (dt_ref, log_ref, skip_ref)]
            rows = jnp.concatenate(rows + [jnp.zeros((5, 128), F32)])
            local = dot(rows, head_map(k, block, True), AB, HIGH)
            out_ref[10:11, 0:128] = local[0:1, :]
            out_ref[11:12, 0:128] = jnp.exp(local[1:2, :])
            out_ref[5:6, :WIDE] = dot(local, channel_map(True), AB, HIGH)[2:3, :]

    out_ref[0:CONV, WIDE:MIX] = taps_ref[0, :, INNER:]
    out_ref[4:5, WIDE:MIX] = bias_ref[:, INNER:]
    out_ref[8:9, :] = norm_ref[...]


def prepare(sp, block, arrays):
    out = shape((16, arrays[0].shape[1]), F32)
    return call("prepare", functools.partial(prepare_kernel, block), sp, arrays, [out], 12)[0]


def gather_small_kernel(counts, sp, *refs):
    keep_ref, send_ref = refs[-2:]
    packed, at = [], 0
    for layer in range(2):
        sums = []
        for count in counts[layer]:
            sums.append(sum(ref[...] for ref in refs[at : at + count]))
            at += count
        dcw, dhp, dgain, dnorm = sums
        tall = lax.broadcasted_iota(jnp.int32, (8, MIX), 0)
        gain = jnp.concatenate([dgain, jnp.zeros((8, MIX - WIDE), F32)], axis=1)
        short = dnorm.shape[1] - MIX
        norm_rest = jnp.concatenate([dnorm[:, MIX:], jnp.zeros((8, MIX - short), F32)], axis=1)
        middle = jnp.where(tall == 0, gain, jnp.where(tall == 1, dnorm[:, :MIX], norm_rest))
        heads = jnp.concatenate([dhp, jnp.zeros((8, MIX - 128), F32)], axis=1)
        packed.append(jnp.concatenate([dcw, middle, heads]))
    zero = sp[1] == 0
    keep_ref[...] = choose(zero, packed[0], packed[1])
    send_ref[...] = choose(zero, packed[1], packed[0])


def gather_small(sp, small):
    counts = [[len(kind) for kind in layer] for layer in small]
    arrays = [x for layer in small for kind in layer for x in kind]
    out = shape((PACK, MIX), F32)
    kernel = functools.partial(gather_small_kernel, counts)
    return call("gather_small", kernel, sp, arrays, [out, out], 12)


def spread_small_kernel(block, sp, *refs):
    slots, all_slots = refs[:CTX], refs[-1]
    norm_ref, taps_ref, bias_ref, dt_ref, log_ref, skip_ref, gain_ref = refs[CTX:-1]
    for m in range(CTX):
        all_slots[m ^ sp[0]] = slots[m][...]
    total = sum(all_slots[k] for k in range(CTX))
    norm_ref[:, :MIX] = total[9:10, :]
    norm_ref[:, MIX:] = total[10:11, : norm_ref.shape[1] - MIX]
    taps_ref[0, :, INNER:] = total[0:CONV, WIDE:]
    bias_ref[:, INNER:] = total[4:5, WIDE:]
    pick = channel_map()
    heads = 0.0
    for k in range(CTX):
        for here, there, n in spans(k, block):
            taps_ref[0, :, there : there + n] = all_slots[k, 0:CONV, here : here + n]
            bias_ref[:, there : there + n] = all_slots[k, 4:5, here : here + n]
            gain_ref[:, there : there + n] = all_slots[k, 8:9, here : here + n]
        skip = dot(all_slots[k, 0:8, :WIDE], pick, AB, HIGH)
        both = jnp.concatenate([all_slots[k, 16:24, :128], skip])
        heads = heads + dot(both, head_map(k, block), AB, HIGH)
    dt_ref[...] = heads[0:1, :HEADS]
    log_ref[...] = heads[1:2, :HEADS]
    skip_ref[...] = heads[13:14, :HEADS]


def spread_small(sp, block, slots, d):
    one = shape((1, HEADS), F32)
    return call(
        "spread_small",
        functools.partial(spread_small_kernel, block),
        sp,
        slots,
        [
            shape((1, d), F32),
            shape((1, CONV, CONV_DIM), F32),
            shape((1, CONV_DIM), F32),
            one,
            one,
            one,
            shape((1, INNER), F32),
        ],
        12,
        scratch=[pltpu.VMEM((CTX, PACK, MIX), F32)],
    )


def sum_over_dp(x, dp):
    if dp & (dp - 1):
        return lax.psum(x, "dp")
    step = 1
    while step < dp:
        x = x + lax.ppermute(x, "dp", [(i, i ^ step) for i in range(dp)])
        step *= 2
    return x


class Order:
    def __init__(self, sp):
        self.sp = sp

    def __call__(self, kernel, *args):
        out = kernel(self.sp, *args)
        self.after(out[0] if isinstance(out, (list, tuple)) else out)
        return out

    def after(self, x):
        self.sp, _ = lax.optimization_barrier((self.sp, x))

    def now(self, x):
        return lax.optimization_barrier((x, self.sp))[0]


def shards(
    tokens,
    cotangent,
    doc_lengths,
    norm_gain,
    w_in,
    conv_weight,
    conv_bias,
    dt_bias,
    a_log,
    d_skip,
    inner_gain,
    w_out,
):
    mine, place = lax.axis_index("section"), lax.axis_index("ctx")
    dp = lax.axis_size("dp")
    piece, d = tokens.shape[2], tokens.shape[3]
    seg_len = piece * CTX // SEGS
    direct = dp == 4 and w_out.shape[1] % HEAD == 0 and w_out.shape[1] * dp == WIDE
    block = w_out.shape[1] // HEAD if direct else LOCAL

    own_x = lax.dynamic_index_in_dim(tokens, mine, 0, False)[0]
    own_u = lax.dynamic_index_in_dim(cotangent, mine, 0, False)[0]
    lengths = lax.dynamic_index_in_dim(doc_lengths, mine, 0, False)[0]
    start = jnp.stack([place, mine, lax.axis_index("dp")]).astype(jnp.int32)
    sp = jnp.concatenate([start, jnp.cumsum(lengths) - lengths])
    run = Order(sp)
    if direct:
        carrier = Direct(run, mine, dp, block, w_in[0], w_out[0])
    else:
        carrier = Plain(mine, place, block, w_in[0], w_out[0])

    def natural(slots):
        return jnp.concatenate(slots).reshape(CTX, 2, piece // 2, d)

    rows_x = gather_slots(run, run.now(own_x))
    arrays = [norm_gain, conv_weight, conv_bias, dt_bias, a_log, d_skip, inner_gain]
    params = run(prepare, block, arrays)
    other = swap_core(params)
    params = [choose(mine == 0, params, other), choose(mine == 0, other, params)]
    carrier.prepare_gate()
    rows_x = natural(rows_x())
    conv0 = carrier.start_conv()
    run.after(rows_x)
    gate0 = carrier.start_gate(conv0)
    conv0 = carrier.trade_weights(conv0)
    rows_u = gather_slots(run, run.now(own_u))
    no_state, no_tail = jnp.zeros((STATE, WIDE), F32), jnp.zeros((16, MIX), BF16)

    def forward(layer, s, pieces, wc, state, tail, between=None):
        normed, conv_in, step_raw = run(project, pieces, params[layer], wc, seg_len)
        if between is not None:
            middle[1] = between()
        y, states, state, next_tail = run(
            scan_rows, s, conv_in, step_raw, params[layer], state, tail
        )
        return dict(
            normed=normed, conv_in=conv_in, step_raw=step_raw, y=y, states=states, tail=tail
        ), state, next_tail

    wc0 = run(carrier.conv_weights, conv0)
    conv1, gate1 = carrier.start_second()
    first, second = [None, None], [None, None]
    state, tail = no_state, no_tail
    first[0], state, tail = forward(0, 0, natural_slots(rows_x, 0), wc0, state, tail)
    first[1], state, tail = forward(0, 1, natural_slots(rows_x, 1), wc0, state, tail)
    rows_u = rows_u()
    gate0 = carrier.trade_weights(gate0)
    wg0, wo0 = run(carrier.gate_weights, gate0)
    stats, sums = [None, None], [None, None]
    for s in range(SEGS):
        saved = first[s]
        saved["gate"], stats[s], *sums[s] = run(
            out_rows, True, [], [], saved["normed"], saved["y"], params[0], wg0, wo0
        )
        if s == 0:
            sums[0] = scatter_start(*sums[0])

    def own_step(s):
        residual = natural_slots(rows_x, s)[:1]
        first[s]["stats"] = [stats[s]] + [tail_tile(x) for x in sums[s][1:4]]
        own, first[s]["branch"] = run(own_rows, False, first[s]["stats"], sums[s], residual)
        first[s]["own"] = own
        return gather_slots(run, own)

    sums[0] = scatter_slots(run, *sums[0])
    sums[1] = scatter_start(*[run.now(x) for x in sums[1]])
    middle = [own_step(0), None]
    sums[1] = scatter_slots(run, *sums[1])
    middle[0] = middle[0]()
    rows_u = natural(rows_u)
    run.after(rows_u)

    conv1 = carrier.trade_weights(conv1)
    wc1 = run(carrier.conv_weights, conv1)
    middle[1] = own_step(1)
    state, tail = no_state, no_tail
    parts, before = [], []
    for s in range(SEGS):
        between = middle[1] if s == 0 else None
        second[s], state, tail = forward(1, s, middle[s], wc1, state, tail, between)
        if s == 0:
            gate1 = carrier.trade_weights(gate1)
    wg1, wo1 = run(carrier.gate_weights, gate1)
    for s in range(SEGS):
        saved = second[s]
        saved["gate"], stats, part = run(
            out_rows,
            False,
            before,
            natural_slots(rows_u, s),
            saved["normed"],
            saved["y"],
            params[1],
            wg1,
            wo1,
        )
        before = [stats]
        parts.append(part)
    stats = from_all(stats)
    part1 = run(collect, parts)
    hidden0 = run(natural_rows, middle)

    def gate_step(layer, s, saved, pieces, stats, first_stat, inners, wo):
        out = run(
            gate_back, pieces, stats, first_stat, inners, saved["y"], saved["gate"], params[layer], wo
        )
        saved.update(zip(("dy", "dgate", "gated", "u", "dgain"), out))

    def scan_step(layer, s, saved, dstate, later):
        saved["dconv"], saved["dcw"], saved["dhp"], dstate, later = run(
            scan_back,
            s,
            saved["conv_in"],
            saved["step_raw"],
            saved["dy"],
            saved["states"],
            saved["tail"],
            params[layer],
            dstate,
            later,
        )
        return dstate, later

    def of(saved, *names):
        return [[one[name] for one in saved] for name in names]

    def back_start(s):
        saved = second[s]
        return scatter_start(*run(input_back, True, saved["dconv"], saved["dgate"], wc1, wg1))

    def back_end(s, part):
        up, second[s]["dnorm"] = run(
            own_back,
            16,
            part,
            [first[s]["own"]],
            natural_slots(rows_u, s)[:1],
            params[1],
            first[s]["branch"],
        )
        return gather_slots(run, up, 16)

    upper = [None, None]

    def lower_gate(s):
        inners = [head_tile(x) for x in upper[s][:4]]
        gate_step(0, s, first[s], upper[s], first[s]["stats"], 0, inners, wo0)

    for s in (1, 0):
        gate_step(1, s, second[s], natural_slots(rows_u, s), stats, 8 * s, [], wo1)
    gate1 = carrier.trade_grads(run(carrier.grad_gate, 1, *of(second, "normed", "dgate", "gated", "u")))
    part1 = scatter_start(*part1)
    dstate, later = no_state, jnp.zeros((8, MIX), F32)
    dstate, later = scan_step(1, 1, second[1], dstate, later)
    part1 = scatter_slots(run, *part1)
    gate1 = carrier.send(gate1)
    upper[1] = back_start(1)
    dstate, later = scan_step(1, 0, second[0], dstate, later)
    hidden1, _ = run(own_rows, True, stats, part1, [hidden0])
    upper[1] = scatter_slots(run, *upper[1])
    upper[0] = back_start(0)
    upper[1] = back_end(1, upper[1])
    upper[1] = upper[1]()
    upper[0] = scatter_slots(run, *upper[0])
    conv1 = carrier.trade_grads(run(carrier.grad_conv, 1, *of(second, "normed", "dconv")))
    lower_gate(1)
    conv1 = carrier.send(conv1)
    upper[0] = back_end(0, upper[0])
    dstate, later = no_state, jnp.zeros((8, MIX), F32)
    dstate, later = scan_step(0, 1, first[1], dstate, later)
    upper[0] = upper[0]()
    (part_1,) = run(input_back, False, first[1]["dconv"], first[1]["dgate"], wc0, wg0)
    lower_gate(0)
    gate0 = carrier.trade_grads(run(carrier.grad_gate, 0, *of(first, "normed", "dgate", "gated", "u")))
    grads1 = run(natural_rows, upper, 16)
    gate0 = carrier.send(gate0)
    dstate, later = scan_step(0, 0, first[0], dstate, later)
    conv0 = carrier.trade_grads(run(carrier.grad_conv, 0, *of(first, "normed", "dconv")))
    (part_0,) = run(input_back, False, first[0]["dconv"], first[0]["dgate"], wc0, wg0)
    conv0 = carrier.send(conv0)
    part = scatter_start(*run(collect, [part_0, part_1]))
    carrier.early(conv1, gate1, gate0)
    part = scatter_slots(run, *part)
    carrier.early_trade()
    branch = jnp.zeros((piece, d), F32)
    grads0, dnorm0 = run(own_back, 0, part, [own_x], [grads1], params[0], branch)
    small = [
        of(first, "dcw", "dhp", "dgain") + [[dnorm0]],
        of(second, "dcw", "dhp", "dgain", "dnorm"),
    ]
    keep, small_sent = run(gather_small, small)
    total = from_all(sum_over_dp(keep + swap_core(small_sent), dp))
    shard_in, shard_out = carrier.gradients(conv0)
    norm, taps, bias, dt, log, skip, gain = spread_small(sp, block, total, d)

    def to_layers(a, b):
        here, there = choose(mine == 0, a, b), swap_core(choose(mine == 0, b, a))
        both = jnp.stack([choose(mine == 0, here, there), choose(mine == 0, there, here)])
        return both[None, :, None]

    return (
        to_layers(hidden0, hidden1),
        to_layers(grads0, grads1),
        norm,
        shard_in[None],
        taps,
        bias,
        dt,
        log,
        skip,
        gain,
        shard_out[None],
    )


def solution(mesh):
    in_specs = (
        P(None, "dp", "ctx", None),
        P(None, "dp", "ctx", None),
        P(None, "dp", None),
        P("section", None),
        P("section", ("dp", "ctx"), None),
        P("section", None, None),
        P("section", None),
        P("section", None),
        P("section", None),
        P("section", None),
        P("section", None),
        P("section", ("dp", "ctx"), None),
    )
    out_specs = (
        P("section", None, "dp", "ctx", None),
        P("section", None, "dp", "ctx", None),
        P("section", None),
        P("section", ("dp", "ctx"), None),
        P("section", None, None),
        P("section", None),
        P("section", None),
        P("section", None),
        P("section", None),
        P("section", None),
        P("section", ("dp", "ctx"), None),
    )
    return jax.shard_map(shards, mesh=mesh, in_specs=in_specs, out_specs=out_specs, check_vma=False)
```

```python
import functools

import jax
import jax.numpy as jnp
from jax import lax
from jax.experimental import pallas as pl
from jax.experimental.pallas import tpu as pltpu
from jax.sharding import PartitionSpec as P

HEADS = 48
HEAD = 64
STATE = 128
CONV = 4
INNER = 3072
CONV_DIM = 3328
NORM_EPS = 1e-05

F32 = jnp.float32
BF16 = jnp.bfloat16
HIGH = lax.Precision.HIGHEST
CTX = 4
SEGS = 2
LOCAL = HEADS // CTX
WIDE = LOCAL * HEAD
MIX = WIDE + 2 * STATE
FULL = MIX + 128
HALF = WIDE // 2
LOAD = HALF + STATE + 128
PACK = 24
MIB = 1024 * 1024
MICROS = {
    "project": 3,
    "scan_rows": 8,
    "out_rows": 4,
    "gate_back": 3,
    "scan_back": 16,
    "input_back": 4,
    "grad_gate": 8,
    "grad_conv": 6,
}


def swap_core(x):
    return lax.ppermute(x, "section", [(0, 1), (1, 0)])


def flip(x, bits):
    return lax.ppermute(x, "ctx", [(i, i ^ bits) for i in range(CTX)])


def gather_slots(order, own, extra=0):
    half = (own.shape[0] - extra) // 2
    x, y = flip(own, 1), flip(own, 2)

    def forward():
        order.after((x, y))
        first, second = order.now(y[: extra + half]), order.now(x[extra + half :])
        return [own, x, y, flip(first, 1), flip(second, 2)]

    return forward


def scatter_start(own, to_x, to_y, late_x, late_y):
    return own, flip(to_x, 1), flip(to_y, 2), late_x, late_y


def scatter_slots(order, own, from_x, from_y, late_x, late_y):
    extra = from_x.shape[0] - 2 * late_x.shape[0]
    outs = [shape((late_x.shape[0] + extra, late_x.shape[1]), BF16), late_y]
    late_x, late_y = order(call_with("turn", turn_kernel, [from_x, from_y, late_x, late_y], outs))
    return [own, from_x, from_y, flip(late_x, 1), flip(late_y, 2)]


def from_all(x):
    return [x] + [flip(x, m) for m in range(1, CTX)]


def dot(a, b, dims, precision=None):
    return lax.dot_general(a, b, (dims, ((), ())), precision=precision, preferred_element_type=F32)


AB = ((1,), (0,))
ABT = ((1,), (1,))
ATB = ((0,), (0,))


def far(x):
    return pltpu.with_memory_space_constraint(x, pltpu.HBM)


def call_with(name, kernel, ins, outs):
    return lambda sp: call(name, kernel, sp, ins, outs)


def split_dot(a, b, dims):
    a_high, b_high = a.astype(BF16), b.astype(BF16)
    a_low = (a - a_high.astype(F32)).astype(BF16)
    b_low = (b - b_high.astype(F32)).astype(BF16)
    return dot(a_high, b_high, dims) + dot(a_low, b_high, dims) + dot(a_high, b_low, dims)


def whole(x):
    zeros = (0,) * len(x.shape)
    return pl.BlockSpec(tuple(x.shape), lambda i, sp: zeros)


def shape(dims, dtype):
    return jax.ShapeDtypeStruct(dims, dtype)


def call(name, kernel, sp, ins, outs, vmem=20, grid=1, scratch=()):
    ins = [x if isinstance(x, tuple) else (x, whole(x)) for x in ins]
    outs = [x if isinstance(x, tuple) else (x, whole(x)) for x in outs]
    return pl.pallas_call(
        kernel,
        grid_spec=pltpu.PrefetchScalarGridSpec(
            num_scalar_prefetch=1,
            grid=(grid,),
            in_specs=[spec for _, spec in ins],
            out_specs=[spec for _, spec in outs],
            scratch_shapes=list(scratch),
        ),
        out_shape=[x for x, _ in outs],
        compiler_params=pltpu.CompilerParams(
            dimension_semantics=("arbitrary",), vmem_limit_bytes=vmem * MIB
        ),
        cost_estimate=pl.CostEstimate(
            flops=int(MICROS.get(name, 1) * 1e9), bytes_accessed=1, transcendentals=0
        ),
        name=name,
    )(sp, *[x for x, _ in ins])


def natural_spec(x, seg, slot):
    def at(i, sp):
        inside = slot ^ sp[0]
        return (2 * seg + (inside >> 1)) ^ sp[0], inside & 1, 0, 0

    return pl.BlockSpec((1, 1) + x.shape[2:], at)


def natural_slots(x, seg):
    x = far(x)
    return [(x, natural_spec(x, seg, m)) for m in range(CTX)]


def load_rows(refs, extra=0):
    first = 0
    for n, ref in enumerate(refs):
        value = ref[...]
        value = value.reshape(value.shape[-2:])
        if extra and n < 4:
            value = value[extra:]
        yield first, value
        first += value.shape[0]


def row_scale(x):
    return lax.rsqrt(jnp.mean(x * x, axis=-1, keepdims=True) + NORM_EPS)


def project_kernel(count, sp, *refs):
    cw_ref, wc_ref, normed_ref, conv_ref, step_ref = refs[count:]
    gain = cw_ref[8:9, :]
    for first, x in load_rows(refs[:count]):
        x = x.astype(F32)
        rows = pl.ds(first, x.shape[0])
        normed_ref[rows, :] = (x * row_scale(x) * gain).astype(BF16)
    normed = normed_ref[...]
    conv_ref[...] = dot(normed, wc_ref[:, :MIX], AB).astype(BF16)
    step_ref[...] = dot(normed, wc_ref[:, MIX:], AB)


def project(sp, pieces, cw, wc, tokens):
    return call(
        "project",
        functools.partial(project_kernel, len(pieces)),
        sp,
        pieces + [cw, wc],
        [
            shape((tokens, wc.shape[0]), BF16),
            shape((tokens, MIX), BF16),
            shape((tokens, 128), F32),
        ],
    )


def bounds_of(sp):
    return [sp[3 + d] for d in range(sp.shape[0] - 3)]


def distances(sp, first, rows):
    at = lax.broadcasted_iota(jnp.int32, (rows, 1), 0) + first
    since = at
    for bound in bounds_of(sp):
        gap = at - bound
        since = jnp.where(gap >= 0, jnp.minimum(since, gap), since)
    return since


def segment(sp, at):
    total = jnp.zeros_like(at)
    for bound in bounds_of(sp):
        total = total + jnp.where(at >= bound, 1, 0)
    return total


def pair_lanes(a, pair):
    rows = a.shape[0]
    low = lax.broadcasted_iota(jnp.int32, (rows, 2 * HEAD), 1) < HEAD
    first = jnp.broadcast_to(a[:, 2 * pair : 2 * pair + 1], (rows, 2 * HEAD))
    second = jnp.broadcast_to(a[:, 2 * pair + 1 : 2 * pair + 2], (rows, 2 * HEAD))
    return jnp.where(low, first, second)


def conv_forward(ext, cw_ref, since, cols, q):
    total = cw_ref[4:5, cols] + cw_ref[3:4, cols] * ext[8 : 8 + q, cols]
    for shift in range(1, CONV):
        tap = cw_ref[3 - shift : 4 - shift, cols]
        rows = ext[8 - shift : 8 - shift + q, cols]
        total = total + jnp.where(since >= shift, tap * rows, 0.0)
    return total


def block_terms(sp, first, q, raw, cw_ref):
    row = lax.broadcasted_iota(jnp.int32, (q, 1), 0)
    col = lax.broadcasted_iota(jnp.int32, (1, q), 1)
    seg_col, seg_row = segment(sp, row + first), segment(sp, col + first)
    seg_before, seg_last = jnp.int32(0), jnp.int32(0)
    for bound in bounds_of(sp):
        seg_before = seg_before + jnp.where(first - 1 >= bound, 1, 0)
        seg_last = seg_last + jnp.where(first + q - 1 >= bound, 1, 0)
    same = seg_col == seg_row
    shifted = raw + cw_ref[10:11, 0:128]
    stepsize = jax.nn.softplus(shifted)
    decay = -stepsize * cw_ref[11:12, 0:128]
    lower = jnp.where(row >= col, 1.0, 0.0)
    cum = dot(lower, decay, AB, HIGH)
    last = cum[q - 1 : q, :]
    open_w = jnp.where(seg_col == seg_before, jnp.exp(cum), 0.0)
    tail = jnp.where(seg_col == seg_last, jnp.exp(jnp.minimum(last - cum, 0.0)), 0.0)
    passed = jnp.where(seg_last == seg_before, jnp.exp(last), 0.0)
    return row, col, same, shifted, stepsize, decay, cum, open_w, tail, passed


def pair_cols(pair):
    return slice(2 * HEAD * pair, 2 * HEAD * (pair + 1))


def scan_kernel(
    seg,
    sp,
    ci_ref,
    raw_ref,
    cw_ref,
    st_in_ref,
    tail_in_ref,
    y_ref,
    st_ref,
    st_out_ref,
    tail_out_ref,
    ext,
    mix,
    state,
    flow,
    fresh,
):
    k = pl.program_id(0)
    q = ci_ref.shape[0]
    first = (CTX * seg + k) * q

    @pl.when(k == 0)
    def _():
        state[...] = st_in_ref[...]
        ext[0:8, :] = tail_in_ref[...].astype(F32)[8:16, :]

    ci = ci_ref[...]
    tail_out_ref[...] = ci[q - 16 : q, :]
    ext[8 : 8 + q, :] = ci.astype(F32)
    since = distances(sp, first, q)
    for c in range(0, MIX, 128):
        cols = slice(c, c + 128)
        pre = conv_forward(ext, cw_ref, since, cols, q)
        mix[:, cols] = pre * jax.nn.sigmoid(pre)
    ext[0:8, :] = ext[q : q + 8, :]

    row, col, same, _, stepsize, _, cum, open_w, tail, passed = block_terms(
        sp, first, q, raw_ref[...], cw_ref
    )
    cum_t = cum.T
    keys = mix[:, WIDE : WIDE + STATE]
    kt = keys.T.astype(BF16)
    queries = mix[:, WIDE + STATE :]
    qb = queries.astype(BF16)
    scores = jnp.where(same & (row >= col), split_dot(queries, keys, ABT), 0.0)
    st_ref[...] = state[...]
    flow[...] = split_dot(queries, state[...], AB)
    low = lax.broadcasted_iota(jnp.int32, (q, 2 * HEAD), 1) < HEAD
    tail = tail * stepsize
    for pair in range(LOCAL // 2):
        cols = pair_cols(pair)
        v = mix[:, cols]
        vs = v * pair_lanes(stepsize, pair)
        outs = []
        for h in (2 * pair, 2 * pair + 1):
            damp = jnp.exp(jnp.minimum(cum[:, h : h + 1] - cum_t[h : h + 1, :], 0.0))
            outs.append(split_dot(scores * damp, vs, AB))
        inflow = flow[:, cols] * pair_lanes(open_w, pair)
        y = jnp.where(low, outs[0], outs[1]) + inflow + cw_ref[5:6, cols] * v
        y_ref[:, cols] = y
        fresh[:, cols] = (v * pair_lanes(tail, pair)).astype(BF16)
    update = dot(kt, fresh[...], AB)
    for pair in range(LOCAL // 2):
        cols = pair_cols(pair)
        state[:, cols] = state[:, cols] * pair_lanes(passed, pair) + update[:, cols]
    st_out_ref[...] = state[...]


def scan_rows(sp, seg, conv_in, step_raw, cw, state, tail):
    q = conv_in.shape[0] // CTX

    def here(x):
        return x, pl.BlockSpec((q, x.shape[1]), lambda k, sp: (k ^ sp[0], 0))

    tokens = conv_in.shape[0]
    states = pltpu.HBM((CTX * STATE, WIDE), F32)
    return call(
        "scan_rows",
        functools.partial(scan_kernel, seg),
        sp,
        [here(conv_in), here(step_raw), cw, state, tail],
        [
            here(shape((tokens, WIDE), F32)),
            (states, pl.BlockSpec((STATE, WIDE), lambda k, sp: (k, 0))),
            shape((STATE, WIDE), F32),
            shape((16, MIX), BF16),
        ],
        16,
        grid=CTX,
        scratch=[
            pltpu.VMEM((q + 8, MIX), F32),
            pltpu.VMEM((q, MIX), F32),
            pltpu.VMEM((STATE, WIDE), F32),
            pltpu.VMEM((q, WIDE), F32),
            pltpu.VMEM((q, WIDE), BF16),
        ],
    )


def stat_rows(columns):
    rows = columns[0].shape[0]
    lane = lax.broadcasted_iota(jnp.int32, (rows, 128), 1)
    table = jnp.zeros((rows, 128), F32)
    for i, column in enumerate(columns):
        table = jnp.where(lane == i, column, table)
    return table.T[0:8, :]


def stat_columns(rows):
    return jnp.concatenate([rows, jnp.zeros((120, rows.shape[1]), F32)]).T


def split_rows(row, cols):
    high = row.astype(BF16).astype(F32)
    middle = (row - high).astype(BF16).astype(F32)
    low = row - high - middle
    sub = lax.broadcasted_iota(jnp.int32, (16, row.shape[1]), 0)
    tile = jnp.where(sub == 0, high, jnp.where(sub == 1, middle, jnp.where(sub == 2, low, 0.0)))
    spare = jnp.zeros((16, cols - row.shape[1]), F32)
    return jnp.concatenate([tile, spare], axis=1).astype(BF16)


def stat_row(ref, row, count):
    if ref.dtype == F32:
        return ref[row : row + 1, :count]
    tile = ref[...].astype(F32)
    return tile[0:1, :count] + tile[1:2, :count] + tile[2:3, :count]


def store_slots(part, stat, part_refs):
    own_ref, x_ref, y_ref, late_x_ref, late_y_ref = part_refs
    q = own_ref.shape[0]
    half = q // 2
    part = part.astype(BF16)
    own_ref[...] = part[:q]
    x_ref[:half, :] = part[3 * q : 3 * q + half]
    x_ref[half:q, :] = part[q : q + half]
    y_ref[:half, :] = part[3 * q + half :]
    y_ref[half:q, :] = part[2 * q + half : 3 * q]
    late_x_ref[...] = part[q + half : 2 * q]
    late_y_ref[...] = part[2 * q : 2 * q + half]
    if stat is not None:
        tile = split_rows(stat, part.shape[1])
        x_ref[q:, :] = tile
        y_ref[q:, :] = tile


def store_part(part, stat, part_refs):
    if len(part_refs) == 1:
        part_refs[0][...] = part.astype(BF16)
    else:
        store_slots(part, stat, part_refs)


def part_shapes(slots, tokens, d, extra=0):
    if not slots:
        return [shape((tokens, d), BF16)]
    q = tokens // CTX
    sent = shape((q + extra, d), BF16)
    return [shape((q, d), BF16), sent, sent] + [shape((q // 2, d), BF16)] * 2


def tail_tile(x):
    return x, pl.BlockSpec((16, x.shape[1]), lambda i, sp: (x.shape[0] // 16 - 1, 0))


def head_tile(x):
    return x, pl.BlockSpec((16, x.shape[1]), lambda i, sp: (0, 0))


def turn_kernel(sp, from_x_ref, from_y_ref, late_x_ref, late_y_ref, x_ref, y_ref):
    half = y_ref.shape[0]
    x_ref[:half, :] = (late_x_ref[...].astype(F32) + from_y_ref[:half, :].astype(F32)).astype(BF16)
    y_ref[...] = (late_y_ref[...].astype(F32) + from_x_ref[:half, :].astype(F32)).astype(BF16)
    if x_ref.shape[0] > half:
        x_ref[half:, :] = from_y_ref[2 * half :, :]


def out_kernel(count, before, sp, *refs):
    if before:
        before_ref, refs = refs[0], refs[1:]
    normed_ref, y_ref, cw_ref, wg_ref, wo_ref = refs[count : count + 5]
    gate_ref, stat_ref = refs[count + 5 : count + 7]
    gate = dot(normed_ref[...], wg_ref[...], AB)
    gate_ref[...] = gate
    g = y_ref[...] * gate * jax.nn.sigmoid(gate)
    part = dot((g * cw_ref[9:10, :WIDE]).astype(BF16), wo_ref[...], AB)
    square = jnp.sum(g * g, axis=-1, keepdims=True)
    inner = [
        jnp.sum(part[first : first + u.shape[0]] * u.astype(F32), axis=-1, keepdims=True)
        for first, u in load_rows(refs[:count])
    ]
    rows = stat_rows([square] + ([jnp.concatenate(inner)] if inner else []))
    store_part(part, rows[0:1, :], refs[count + 7 :])
    if before:
        rows = jnp.concatenate([before_ref[...], rows])
    stat_ref[...] = rows


def out_rows(sp, slots, before, pieces, normed, y, cw, wg, wo):
    tokens, d = normed.shape
    return call(
        "out_rows",
        functools.partial(out_kernel, len(pieces), len(before)),
        sp,
        before + pieces + [normed, y, cw, wg, wo],
        [shape((tokens, WIDE), F32), shape((8 + 8 * len(before), tokens), F32)] + part_shapes(slots, tokens, d, 16),
        28,
    )


def slot_sums(stat_refs, row, q):
    out = []
    for slot in range(CTX):
        total = 0.0
        for m, ref in enumerate(stat_refs):
            total = total + stat_row(ref, row, CTX * q)[:, (slot ^ m) * q : (slot ^ m) * q + q]
        out.append(total)
    return jnp.concatenate(out, axis=1)


def own_sum(refs):
    own, from_x, from_y, late_x, late_y = [ref[...].astype(F32) for ref in refs]
    half = late_y.shape[0]
    x = jnp.concatenate([from_x[half : 2 * half], late_x[:half]])
    return own + x + jnp.concatenate([late_y, from_y[half : 2 * half]])


def own_squares(stats, sp, natural, q):
    if not natural:
        rows = [stat_row(ref, 0, CTX * q) for ref in stats]
        return sum(row[:, m * q : m * q + q] for m, row in enumerate(rows))
    place, out = sp[0], []
    block = q // 2
    for half in range(2):
        total = jnp.zeros((1, block), F32)
        for s in range(SEGS):
            for slot in range(CTX):
                here = ((place >> 1) == s) & ((slot ^ place) == 2 * (place & 1) + half)
                for m, ref in enumerate(stats):
                    value = ref[8 * s : 8 * s + 1, pl.ds((slot ^ m) * block, block)]
                    total = total + jnp.where(here, value, 0.0)
        out.append(total)
    return jnp.concatenate(out, axis=1)


def own_kernel(count, natural, sp, *refs):
    stats, partial = refs[:CTX], refs[CTX : CTX + 5]
    residual = jnp.concatenate([x for _, x in load_rows(refs[CTX + 5 : CTX + 5 + count])])
    own_ref, branch_ref = refs[CTX + 5 + count :]
    square = own_squares(stats, sp, natural, own_ref.shape[0])
    square = jnp.concatenate([square, jnp.zeros((7, square.shape[1]), F32)])
    scale = lax.rsqrt(stat_columns(square)[:, 0:1] / INNER + NORM_EPS)
    branch = own_sum(partial) * scale
    branch_ref[...] = branch
    own_ref[...] = (residual.astype(F32) + branch).astype(BF16)


def own_rows(sp, natural, stats, partial, residual):
    q, d = partial[0].shape
    return call(
        "own_rows",
        functools.partial(own_kernel, len(residual), natural),
        sp,
        stats + partial + residual,
        [shape((q, d), BF16), shape((q, d), F32)],
        16,
    )


def collect_kernel(sp, part0_ref, part1_ref, own_ref, x_ref, y_ref, late_x_ref, late_y_ref):
    place = sp[0]
    q = late_x_ref.shape[0]
    goals = [
        [own_ref.at[pl.ds(0, q)], own_ref.at[pl.ds(q, q)]],
        [x_ref.at[pl.ds(q, q)], late_x_ref],
        [late_y_ref, y_ref.at[pl.ds(q, q)]],
        [x_ref.at[pl.ds(0, q)], y_ref.at[pl.ds(0, q)]],
    ]
    for m in range(CTX):
        owner = place ^ m
        for half in range(2):
            slot = (2 * (owner & 1) + half) ^ place
            rows = pl.ds(pl.multiple_of(slot * q, q), q)
            goals[m][half][...] = choose((owner >> 1) == 0, part0_ref[rows, :], part1_ref[rows, :])


def collect(sp, parts):
    tokens, d = parts[0].shape
    return call("collect", collect_kernel, sp, list(parts), part_shapes(True, 2 * tokens, d), 20)


def natural_kernel(extra, sp, *refs):
    out_ref = refs[-1]
    q = out_ref.shape[0] // 2
    for place in range(CTX):
        s = place >> 1
        own, x, y, first, second = refs[5 * s : 5 * s + 5]

        @pl.when(sp[0] == place)
        def _():
            for half in range(2):
                slot = (2 * (place & 1) + half) ^ place
                at = half * q
                if slot < 3:
                    out_ref[at : at + q, :] = (own, x, y)[slot][extra:, :]
                else:
                    out_ref[at : at + q // 2, :] = first[extra:, :]
                    out_ref[at + q // 2 : at + q, :] = second[...]


def natural_rows(sp, pieces, extra=0):
    q, d = pieces[0][0].shape
    ins = [x for one in pieces for x in one]
    kernel = functools.partial(natural_kernel, extra)
    return call("natural_rows", kernel, sp, ins, [shape((2 * (q - extra), d), BF16)])[0]


def gate_back_kernel(count, inners, first_stat, sp, *refs):
    pieces, stats = refs[:count], refs[count : count + CTX]
    inner_refs = refs[count + CTX : count + CTX + inners]
    rest = refs[count + CTX + inners :]
    y_ref, gate_ref, cw_ref, wo_ref, dy_ref, dgate_ref, gated_ref, u_ref, dgain_ref = rest
    gain = cw_ref[9:10, :WIDE]
    tokens = y_ref.shape[0]
    q = tokens // CTX
    for first, u in load_rows(pieces, 16 if inners else 0):
        u_ref[pl.ds(first, u.shape[0]), :] = u
    back = dot(u_ref[...], wo_ref[...], ABT)
    scale = lax.rsqrt(slot_sums(stats, first_stat, q) / INNER + NORM_EPS)
    if inners:
        inner = jnp.concatenate([stat_row(ref, 0, q) for ref in inner_refs], axis=1)
    else:
        inner = slot_sums(stats, first_stat + 1, q) * scale
    pull = scale * scale * inner / INNER
    table = stat_columns(jnp.concatenate([scale, pull, jnp.zeros((6, tokens), F32)]))
    scale, pull = table[:, 0:1], table[:, 1:2]
    gate = gate_ref[...]
    y = y_ref[...]
    sig = jax.nn.sigmoid(gate)
    act = gate * sig
    g = y * act
    unit = g * scale
    gated_ref[...] = (unit * gain).astype(BF16)
    dg = back * gain * scale - g * pull
    dy_ref[...] = (dg * act).astype(BF16)
    dgate_ref[...] = (dg * y * (sig + act * (1.0 - sig))).astype(BF16)
    dgain_ref[...] = jnp.broadcast_to(jnp.sum(back * unit, axis=0, keepdims=True), (8, WIDE))


def gate_back(sp, pieces, stats, first_stat, inners, y, gate, cw, wo):
    tokens, d = y.shape[0], wo.shape[1]
    return call(
        "gate_back",
        functools.partial(gate_back_kernel, len(pieces), len(inners), first_stat),
        sp,
        pieces + stats + inners + [y, gate, cw, wo],
        [shape((tokens, WIDE), BF16)] * 3 + [shape((tokens, d), BF16), shape((8, WIDE), F32)],
        28,
    )


def scan_back_kernel(
    seg,
    sp,
    ci_ref,
    prev_ref,
    raw_ref,
    dy_ref,
    st_ref,
    tail_in_ref,
    cw_ref,
    dst_in_ref,
    next_in_ref,
    dci_ref,
    dcw_ref,
    dhp_ref,
    dst_out_ref,
    next_out_ref,
    ext,
    mix,
    slope,
    dext,
    dstate,
    tails,
    dyw,
    flow,
    kept_all,
    ends,
):
    i = pl.program_id(0)
    k = CTX - 1 - i
    q = ci_ref.shape[0]
    first = (CTX * seg + k) * q

    @pl.when(i == 0)
    def _():
        dstate[...] = dst_in_ref[...]
        dext[q : q + 8, :] = next_in_ref[...]
        ends[...] = jnp.zeros_like(ends)
        dcw_ref[...] = jnp.zeros_like(dcw_ref)
        dhp_ref[...] = jnp.zeros_like(dhp_ref)

    @pl.when(k == 0)
    def _():
        ext[0:8, :] = tail_in_ref[...].astype(F32)[8:16, :]

    @pl.when(k > 0)
    def _():
        ext[0:8, :] = prev_ref[...].astype(F32)[8:16, :]

    ext[8 : 8 + q, :] = ci_ref[...].astype(F32)
    since = distances(sp, first, q + 8)
    for c in range(0, MIX, 128):
        cols = slice(c, c + 128)
        pre = conv_forward(ext, cw_ref, since[0:q], cols, q)
        sig = jax.nn.sigmoid(pre)
        act = pre * sig
        mix[:, cols] = act
        slope[:, cols] = sig + act * (1.0 - sig)

    row, col, same, shifted, stepsize, decay, cum, open_w, tail, passed = block_terms(
        sp, first, q, raw_ref[...], cw_ref
    )
    cum_t = cum.T
    keys = mix[:, WIDE : WIDE + STATE]
    kb = keys.astype(BF16)
    queries = mix[:, WIDE + STATE :]
    qb = queries.astype(BF16)
    qt = queries.T.astype(BF16)
    inside = same & (col >= row)
    scores = jnp.where(inside, split_dot(keys, queries, ABT), 0.0)
    stb, dstb = st_ref[...].astype(BF16), dstate[...].astype(BF16)
    flow[...] = dot(qb, stb, AB)
    kept_all[...] = dot(kb, dstb, AB)
    low = lax.broadcasted_iota(jnp.int32, (q, 2 * HEAD), 1) < HEAD
    lane = lax.broadcasted_iota(jnp.int32, (q, 128), 1)
    sub = lax.broadcasted_iota(jnp.int32, (16, q), 0)
    dscores = jnp.zeros((q, q), F32)
    plus_t = jnp.zeros((16, q), F32)
    dstep = jnp.zeros((q, 128), F32)
    dcum = jnp.zeros((q, 128), F32)
    for pair in range(LOCAL // 2):
        cols = pair_cols(pair)
        v = mix[:, cols]
        step_e = pair_lanes(stepsize, pair)
        vs = v * step_e
        vsb = vs.astype(BF16)
        dyb = dy_ref[:, cols]
        dyf = dyb.astype(F32)
        dvs = []
        for side, h in ((0, 2 * pair), (1, 2 * pair + 1)):
            mine = low if side == 0 else ~low
            damp = jnp.exp(jnp.minimum(cum_t[h : h + 1, :] - cum[:, h : h + 1], 0.0))
            raw = dot(jnp.where(mine, vs, 0.0).astype(BF16), dyb, ABT)
            mixing = (scores * damp).astype(BF16)
            dscores = dscores + raw * damp
            both = raw * mixing.astype(F32)
            plus_t = plus_t + jnp.where(sub == h, jnp.sum(both, axis=0, keepdims=True), 0.0)
            dvs.append(dot(mixing, dyb, AB))
        dv = jnp.where(low, dvs[0], dvs[1])
        weighted = dyf * pair_lanes(open_w, pair)
        dyw[:, cols] = weighted.astype(BF16)
        tail_e = pair_lanes(tail, pair)
        kept = kept_all[:, cols] * tail_e
        tails[:, cols] = (vs * tail_e).astype(BF16)
        u = dv + kept
        dext[0:q, cols] = (u * step_e + cw_ref[5:6, cols] * dyf) * slope[:, cols]
        from_tail = kept * vs
        dcw_ref[5:6, cols] += jnp.sum(dyf * v, axis=0, keepdims=True)
        ends[1:2, cols] = jnp.sum(from_tail, axis=0, keepdims=True)
        uv = u * v
        change = weighted * flow[:, cols] - dv * vsb.astype(F32) - from_tail
        for side, h in ((0, 2 * pair), (1, 2 * pair + 1)):
            mine = low if side == 0 else ~low

            def per_row(x):
                return jnp.sum(jnp.where(mine, x, 0.0), axis=1, keepdims=True)

            dstep = jnp.where(lane == h, per_row(uv), dstep)
            dcum = jnp.where(lane == h, per_row(change), dcum)

    dcum = dcum + jnp.concatenate([plus_t, jnp.zeros((112, q), F32)]).T
    ends[0:1, :] = jnp.sum(st_ref[...] * dstate[...], axis=0, keepdims=True)
    by_head = dot(ends[...], channel_map(), AB, HIGH)
    at_end = by_head[0:1, :] * passed + by_head[1:2, :]
    dcum = dcum + jnp.where(row == q - 1, at_end, 0.0)
    upper = jnp.where(col >= row, 1.0, 0.0)
    ddecay = dot(upper, dcum, AB, HIGH)
    draw = (dstep - ddecay * cw_ref[11:12, 0:128]) * jax.nn.sigmoid(shifted)
    dci_ref[:, MIX:] = draw.astype(BF16)
    dhp_ref[0:1, :] += jnp.sum(draw, axis=0, keepdims=True)
    dhp_ref[1:2, :] += jnp.sum(ddecay * decay, axis=0, keepdims=True)

    dsb = jnp.where(inside, dscores, 0.0).astype(BF16)
    dkeys = dot(dsb, qb, AB) + dot(tails[...], dstb, ABT)
    dqueries = dot(dsb, kb, ATB) + dot(dyw[...], stb, ABT)
    kcols, qcols = slice(WIDE, WIDE + STATE), slice(WIDE + STATE, MIX)
    dext[0:q, kcols] = dkeys * slope[:, kcols]
    dext[0:q, qcols] = dqueries * slope[:, qcols]
    update = dot(qt, dyw[...], AB)
    for pair in range(LOCAL // 2):
        cols = pair_cols(pair)
        dstate[:, cols] = dstate[:, cols] * pair_lanes(passed, pair) + update[:, cols]
    dst_out_ref[...] = dstate[...]

    for c in range(0, MIX, 128):
        cols = slice(c, c + 128)
        here = dext[0:q, cols]
        total = cw_ref[3:4, cols] * here
        dcw_ref[3:4, cols] += jnp.sum(here * ext[8 : 8 + q, cols], axis=0, keepdims=True)
        dcw_ref[4:5, cols] += jnp.sum(here, axis=0, keepdims=True)
        for shift in range(1, CONV):
            later = jnp.where(since[shift : shift + q] >= shift, dext[shift : shift + q, cols], 0.0)
            total = total + cw_ref[3 - shift : 4 - shift, cols] * later
            used = jnp.where(since[0:q] >= shift, ext[8 - shift : 8 - shift + q, cols], 0.0)
            dcw_ref[3 - shift : 4 - shift, cols] += jnp.sum(here * used, axis=0, keepdims=True)
        dci_ref[:, cols] = total.astype(BF16)
    head_rows = dext[0:8, :]
    dext[q : q + 8, :] = head_rows
    next_out_ref[...] = head_rows


def scan_back(sp, stored, seg, conv_in, step_raw, dy, states, tail, cw, dstate, following):
    tokens = conv_in.shape[0]
    q = tokens // CTX

    def here(x):
        return x, pl.BlockSpec((q, x.shape[1]), lambda i, sp: ((CTX - 1 - i) ^ sp[0], 0))

    if stored:
        conv_in, step_raw, dy, states = [far(x) for x in (conv_in, step_raw, dy, states)]
        tail, cw, dstate, following = [far(x) for x in (tail, cw, dstate, following)]

    def before(i, sp):
        return (jnp.maximum(CTX - 2 - i, 0) ^ sp[0]) * (q // 16) + q // 16 - 1, 0

    return call(
        "scan_back",
        functools.partial(scan_back_kernel, seg),
        sp,
        [
            here(conv_in),
            (conv_in, pl.BlockSpec((16, MIX), before)),
            here(step_raw),
            here(dy),
            (states, pl.BlockSpec((STATE, WIDE), lambda i, sp: (CTX - 1 - i, 0))),
            tail,
            cw,
            dstate,
            following,
        ],
        [
            here(shape((tokens, FULL), BF16)),
            shape((8, MIX), F32),
            shape((8, 128), F32),
            shape((STATE, WIDE), F32),
            shape((8, MIX), F32),
        ],
        24,
        grid=CTX,
        scratch=[
            pltpu.VMEM((q + 8, MIX), F32),
            pltpu.VMEM((q, MIX), F32),
            pltpu.VMEM((q, MIX), F32),
            pltpu.VMEM((q + 8, MIX), F32),
            pltpu.VMEM((STATE, WIDE), F32),
            pltpu.VMEM((q, WIDE), BF16),
            pltpu.VMEM((q, WIDE), BF16),
            pltpu.VMEM((q, WIDE), F32),
            pltpu.VMEM((q, WIDE), F32),
            pltpu.VMEM((8, WIDE), F32),
        ],
    )


def input_back_kernel(sp, dc_ref, dg_ref, wc_ref, wg_ref, *part_refs):
    part = dot(dc_ref[...], wc_ref[...], ABT) + dot(dg_ref[...], wg_ref[...], ABT)
    store_part(part, None, part_refs)


def input_back(sp, slots, dconv, dgate, wc, wg):
    outs = part_shapes(slots, dconv.shape[0], wc.shape[0])
    return call("input_back", input_back_kernel, sp, [dconv, dgate, wc, wg], outs, 24)


def own_back_kernel(count, sp, *refs):
    partial, rest = refs[:5], refs[5:]
    x = jnp.concatenate([v for _, v in load_rows(rest[:count])]).astype(F32)
    u = jnp.concatenate([v for _, v in load_rows(rest[count : 2 * count])]).astype(F32)
    cw_ref, branch_ref, up_ref, dnorm_ref = rest[2 * count :]
    grad = own_sum(partial)
    scale = row_scale(x)
    gained = grad * cw_ref[8:9, :]
    centre = jnp.mean(gained * x, axis=-1, keepdims=True)
    up = (u + scale * (gained - x * (scale * scale * centre))).astype(BF16)
    extra = up_ref.shape[0] - up.shape[0]
    up_ref[extra:, :] = up
    if extra:
        inner = jnp.sum(up.astype(F32) * branch_ref[...], axis=-1, keepdims=True)
        up_ref[:extra, :] = split_rows(stat_rows([inner])[0:1, :], up.shape[1])
    dnorm_ref[...] = jnp.broadcast_to(
        jnp.sum(grad * x * scale, axis=0, keepdims=True), dnorm_ref.shape
    )


def own_back(sp, extra, partial, x, u, cw, branch):
    q, d = partial[0].shape
    return call(
        "own_back",
        functools.partial(own_back_kernel, len(x)),
        sp,
        partial + x + u + [cw, branch],
        [shape((q + extra, d), BF16), shape((8, d), F32)],
    )


def head_map(group, block, flipped=False):
    here = lax.broadcasted_iota(jnp.int32, (128, 128), 1 if flipped else 0)
    there = lax.broadcasted_iota(jnp.int32, (128, 128), 0 if flipped else 1)
    turn = jnp.zeros_like(here)
    for edge in range(block, LOCAL, block):
        turn = turn + jnp.where(here >= edge, 1, 0)
    goal = here + (turn * (CTX - 1) + group) * block
    return jnp.where((here < LOCAL) & (there == goal), 1.0, 0.0)


def channel_map(flipped=False):
    dims = (128, WIDE) if flipped else (WIDE, 128)
    chan = lax.broadcasted_iota(jnp.int32, dims, 1 if flipped else 0)
    head = lax.broadcasted_iota(jnp.int32, dims, 0 if flipped else 1)
    return jnp.where((chan >= head * HEAD) & (chan < (head + 1) * HEAD), 1.0, 0.0)


def spans(group, block):
    wide = block * HEAD
    return [(z * wide, (z * CTX + group) * wide, wide) for z in range(WIDE // wide)]


def choose(first, a, b):
    return jnp.where(first, a, b)


def pack_kernel(block, sp, w_ref, *refs):
    conv_refs, gate_refs, conv, gate = refs[:CTX], refs[CTX : 2 * CTX], refs[-2], refs[-1]
    place = sp[0]
    keys = w_ref[:, 2 * INNER : 2 * INNER + STATE]
    queries = w_ref[:, 2 * INNER + STATE : 2 * INNER + 2 * STATE]
    steps = w_ref[:, 2 * INNER + 2 * STATE :]
    rows = w_ref.shape[0]
    steps = jnp.concatenate([steps, jnp.zeros((rows, 128 - HEADS), BF16)], axis=1)
    for k in range(CTX):
        values = jnp.concatenate(
            [w_ref[:, INNER + there : INNER + there + n] for _, there, n in spans(k, block)], axis=1
        )
        gates = jnp.concatenate(
            [w_ref[:, there : there + n] for _, there, n in spans(k, block)], axis=1
        )
        step = dot(steps, head_map(k, block, True).astype(BF16), AB).astype(BF16)
        conv[k] = jnp.concatenate(
            [values[:, :HALF], keys, step, values[:, HALF:], queries, step], axis=1
        )
        gate[k] = gates
    for m in range(CTX):
        conv_refs[m][...] = conv[m ^ place]
        gate_refs[m][...] = gate[m ^ place]


def pack(sp, block, w_in):
    rows = w_in.shape[0]
    outs = call(
        "pack",
        functools.partial(pack_kernel, block),
        sp,
        [w_in],
        [shape((rows, 2 * LOAD), BF16)] * CTX + [shape((rows, WIDE), BF16)] * CTX,
        16,
        scratch=[
            pltpu.VMEM((CTX, rows, 2 * LOAD), BF16),
            pltpu.VMEM((CTX, rows, WIDE), BF16),
        ],
    )
    return outs[:CTX], outs[CTX:]


def order_conv_kernel(sp, *refs):
    keep_ref, send_ref = refs[CTX:]
    zero = sp[1] == 0
    for m in range(CTX):
        low, high = refs[m][:, :LOAD], refs[m][:, LOAD:]
        keep_ref[m ^ sp[0]] = choose(zero, low, high)
        send_ref[m ^ sp[0]] = choose(zero, high, low)


def order_conv(sp, slots):
    out = shape((CTX, slots[0].shape[0], LOAD), BF16)
    return call("order_conv", order_conv_kernel, sp, slots, [out, out], 12)


def order_gate_kernel(sp, *refs):
    out_ref, keep_ref, send_ref = refs[CTX:]
    zero = sp[1] == 0
    rows = keep_ref.shape[1]
    for m in range(CTX):
        low, high = refs[m][:, :HALF], refs[m][:, HALF:]
        keep_ref[m ^ sp[0], :, :HALF] = choose(zero, low, high)
        send_ref[m ^ sp[0], :, :HALF] = choose(zero, high, low)
    for r in range(2):
        for c in range(2):
            at = slice(r * rows, (r + 1) * rows)
            low = out_ref[at, c * HALF : (c + 1) * HALF]
            high = out_ref[at, (2 + c) * HALF : (3 + c) * HALF]
            keep_ref[2 * r + c, :, HALF:] = choose(zero, low, high)
            send_ref[2 * r + c, :, HALF:] = choose(zero, high, low)


def order_gate(sp, slots, w_out):
    out = shape((CTX, slots[0].shape[0], WIDE), BF16)
    return call("order_gate", order_gate_kernel, sp, slots + [w_out], [out, out], 12)


def join_conv_kernel(sp, mine_ref, other_ref, wc_ref):
    zero = sp[1] == 0
    rows = mine_ref.shape[2]
    for i in range(CTX):
        a, b = mine_ref[0, i, :, :LOAD], other_ref[0, i, :, :LOAD]
        low, high = choose(zero, a, b), choose(zero, b, a)
        at = slice(i * rows, (i + 1) * rows)
        wc_ref[at, 0:HALF] = low[:, :HALF]
        wc_ref[at, HALF:WIDE] = high[:, :HALF]
        wc_ref[at, WIDE : WIDE + STATE] = low[:, HALF : HALF + STATE]
        wc_ref[at, WIDE + STATE : MIX] = high[:, HALF : HALF + STATE]
        wc_ref[at, MIX:] = low[:, HALF + STATE :]


def by_rows(x, count):
    return x, pl.BlockSpec((x.shape[0] // count, x.shape[1]), lambda z, sp: (z, 0))


def join_conv(sp, mine, other):
    dp, _, rows, _ = mine.shape
    out = by_rows(shape((dp * CTX * rows, FULL), BF16), dp)
    ins = [by_first(mine), by_first(other)]
    return call("join_conv", join_conv_kernel, sp, ins, [out], 12, dp)[0]


def join_gate_kernel(first, sp, mine_ref, other_ref, wg_ref, wo_ref):
    zero = sp[1] == 0
    rows = mine_ref.shape[2]
    for i in range(CTX):
        a, b = mine_ref[0, i, :, first:], other_ref[0, i, :, first:]
        low, high = choose(zero, a, b), choose(zero, b, a)
        at = slice(i * rows, (i + 1) * rows)
        wg_ref[at, :HALF] = low[:, :HALF]
        wg_ref[at, HALF:] = high[:, :HALF]
        r, c = i // 2, i % 2
        at = slice(r * rows, (r + 1) * rows)
        wo_ref[at, c * HALF : (c + 1) * HALF] = low[:, HALF:]
        wo_ref[at, (2 + c) * HALF : (3 + c) * HALF] = high[:, HALF:]


def join_gate(sp, mine, other):
    dp, _, rows, cols = mine.shape
    wg, wo = shape((dp * CTX * rows, WIDE), BF16), shape((dp * 2 * rows, 4 * HALF), BF16)
    outs = [by_rows(wg, dp), by_rows(wo, dp)]
    kernel = functools.partial(join_gate_kernel, cols - WIDE)
    ins = [by_first(mine), by_first(other)]
    return call("join_gate", kernel, sp, ins, outs, 12, dp)


def fold_kernel(sp, keep_ref, came_ref, out_ref):
    out_ref[...] = (keep_ref[...].astype(F32) + came_ref[...].astype(F32)).astype(BF16)


def fold(sp, keep, came):
    ins = [by_first(keep), by_first(came)]
    return call("fold", fold_kernel, sp, ins, [by_first(shape(keep.shape, BF16))], 24, keep.shape[0])


def total_kernel(counts, sp, *refs):
    for m in range(CTX):
        parts = [ref[m ^ sp[0], :, :cols] for ref, cols in zip(refs, counts)]
        refs[len(counts) + m][...] = jnp.concatenate(parts, axis=1)


def total_line(sp, sums):
    width = {LOAD: LOAD, WIDE: HALF}
    counts = [width[x.shape[2]] for x in sums]
    outs = [shape((sums[0].shape[1], sum(counts)), BF16)] * CTX
    sums = [far(x) for x in sums]
    return call("total_line", functools.partial(total_kernel, counts), sp, sums, outs)


def mix_kernel(cols, sp, *refs):
    out_ref = refs[-1]
    zero = sp[1] == 0
    for m in range(CTX):
        if cols == LOAD:
            mine, other = refs[CTX + m][...], refs[m][:, :LOAD]
        else:
            mine, other = refs[m][:, LOAD + HALF :], refs[m][:, LOAD : LOAD + HALF]
            out_ref[m, :, HALF:] = choose(zero, refs[CTX + 1][m, :, HALF:], refs[CTX][m, :, HALF:])
        out_ref[m, :, : mine.shape[1]] = choose(zero, other, mine)


def mix(sp, early, late, cols):
    out = shape((CTX, early[0].shape[0], cols), BF16)
    return call("mix", functools.partial(mix_kernel, cols), sp, early + late, [out])[0]


def grad_conv_kernel(sp, n0_ref, n1_ref, d0_ref, d1_ref, keep_ref, send_ref):
    zero = sp[1] == 0
    rows = keep_ref.shape[2]
    total = dot(n0_ref[...], d0_ref[...], ATB) + dot(n1_ref[...], d1_ref[...], ATB)
    total = total.astype(BF16)
    step = total[:, MIX:]
    low = jnp.concatenate([total[:, :HALF], total[:, WIDE : WIDE + STATE], step], axis=1)
    high = jnp.concatenate([total[:, HALF:WIDE], total[:, WIDE + STATE : MIX], step], axis=1)
    keep, send = choose(zero, low, high), choose(zero, high, low)
    for i in range(CTX):
        keep_ref[0, i] = keep[i * rows : (i + 1) * rows]
        send_ref[0, i] = send[i * rows : (i + 1) * rows]


def by_first(x):
    rest = (0,) * (len(x.shape) - 1)
    return x, pl.BlockSpec((1,) + tuple(x.shape[1:]), lambda z, sp: (z,) + rest)


def by_cols(x, count):
    return x, pl.BlockSpec((x.shape[0], x.shape[1] // count), lambda z, sp: (0, z))


def grad_conv(sp, dp, rows, normed, dconv):
    out = shape((dp, CTX, rows, LOAD), BF16)
    return call(
        "grad_conv",
        grad_conv_kernel,
        sp,
        [by_cols(x, dp) for x in normed] + list(dconv),
        [by_first(out), by_first(out)],
        24,
        dp,
    )


def grad_gate_kernel(sp, *refs):
    n_refs, dg_refs, gated_refs, u_refs = refs[0:2], refs[2:4], refs[4:6], refs[6:8]
    keep_ref, send_ref = refs[8:]
    z = pl.program_id(0)
    dp, _, rows, _ = keep_ref.shape
    zero = sp[1] == 0

    def over_tokens(a, b):
        return dot(a[0][...], b[0][...], ATB) + dot(a[1][...], b[1][...], ATB)

    total = over_tokens(n_refs, dg_refs).astype(BF16)
    keep = choose(zero, total[:, :HALF], total[:, HALF:])
    send = choose(zero, total[:, HALF:], total[:, :HALF])
    for i in range(CTX):
        keep_ref[z, i, :, :HALF] = keep[i * rows : (i + 1) * rows]
        send_ref[z, i, :, :HALF] = send[i * rows : (i + 1) * rows]
    total = over_tokens(gated_refs, u_refs).astype(BF16)
    side, c = z // 2, lax.rem(z, 2)

    def put(ref):
        for there in range(dp):
            for r in range(2):
                first = (2 * there + r) * rows
                ref[there, 2 * r + c, :, HALF:] = total[first : first + rows]

    @pl.when(side == sp[1])
    def _():
        put(keep_ref)

    @pl.when(side != sp[1])
    def _():
        put(send_ref)


def grad_gate(sp, dp, rows, normed, dgate, gated, u):
    out = shape((dp, CTX, rows, WIDE), BF16)
    return call(
        "grad_gate",
        grad_gate_kernel,
        sp,
        [by_cols(x, dp) for x in normed]
        + list(dgate)
        + list(gated)
        + [by_cols(x, dp) for x in u],
        [out, out],
        32,
        dp,
    )


def finish_kernel(block, sp, *refs):
    early, late, (gate0, gate1, came_gate, came_conv) = refs[:4], refs[4:8], refs[8:12]
    in_ref, out_ref, lows, highs, glows, ghighs = refs[12:]
    place, zero = sp[0], sp[1] == 0
    rows = in_ref.shape[0]
    for m in range(CTX):
        mine, came = choose(zero, late[m][...], early[m][:, :LOAD]), came_conv[m]
        lows[m ^ place] = choose(zero, mine, came).astype(F32)
        highs[m ^ place] = choose(zero, came, mine).astype(F32)
        mine = choose(zero, early[m][:, LOAD + HALF :], early[m][:, LOAD : LOAD + HALF])
        came = came_gate[m, :, :HALF]
        glows[m ^ place] = choose(zero, mine, came).astype(F32)
        ghighs[m ^ place] = choose(zero, came, mine).astype(F32)
    keys, queries, steps = 0.0, 0.0, 0.0
    for k in range(CTX):
        keys = keys + lows[k, :, HALF : HALF + STATE]
        queries = queries + highs[k, :, HALF : HALF + STATE]
        steps = steps + dot(lows[k, :, HALF + STATE :], head_map(k, block), AB, HIGH)
    for z in range(WIDE // (block * HEAD)):
        def side_by_side(a, b):
            parts = []
            for k in range(CTX):
                here, _, n = spans(k, block)[z]
                source = a if here < HALF else b
                parts.append(source[k, :, here % HALF : here % HALF + n])
            return jnp.concatenate(parts, axis=1)

        wide = CTX * block * HEAD
        in_ref[:, z * wide : (z + 1) * wide] = side_by_side(glows, ghighs)
        in_ref[:, INNER + z * wide : INNER + (z + 1) * wide] = side_by_side(lows, highs)
    in_ref[:, 2 * INNER : 2 * INNER + STATE] = keys
    in_ref[:, 2 * INNER + STATE : 2 * INNER + 2 * STATE] = queries
    in_ref[:, 2 * INNER + 2 * STATE :] = steps[:, :HEADS]
    for i in range(4):
        r, c = i // 2, i % 2
        mine, came = choose(zero, gate0[i, :, HALF:], gate1[i, :, HALF:]), came_gate[i, :, HALF:]
        at = slice(r * rows, (r + 1) * rows)
        out_ref[at, c * HALF : (c + 1) * HALF] = choose(zero, mine, came).astype(F32)
        out_ref[at, (2 + c) * HALF : (3 + c) * HALF] = choose(zero, came, mine).astype(F32)


def finish(sp, block, early, late, gates, came_gate, came_conv):
    rows = came_conv.shape[1]
    return call(
        "finish",
        functools.partial(finish_kernel, block),
        sp,
        early + late + gates + [came_gate, came_conv],
        [shape((rows, 2 * INNER + 2 * STATE + HEADS), F32), shape((2 * rows, 4 * HALF), F32)],
        24,
        scratch=[pltpu.VMEM((CTX, rows, LOAD), F32)] * 2 + [pltpu.VMEM((CTX, rows, HALF), F32)] * 2,
    )


class Direct:
    def __init__(self, order, mine, dp, block, w_in, w_out):
        self.order, self.mine, self.dp, self.block = order, mine, dp, block
        self.rows = w_in.shape[0]
        conv, gate = order(pack, block, w_in)
        conv = order(order_conv, [flip(x, m) if m else x for m, x in enumerate(conv)])
        self.conv = self.trade(*conv)
        self.first = self.gathered(self.conv[0])
        gate = [order.now(x) for x in gate]
        self.slots = [flip(x, m) if m else x for m, x in enumerate(gate)]
        self.w_out = w_out

    def prepare_gate(self):
        self.gate = self.trade(*self.order(order_gate, self.slots, self.w_out))

    def trade(self, keep, send):
        came = swap_core(send)
        return choose(self.mine == 0, keep, came), choose(self.mine == 0, came, keep)

    def gathered(self, x):
        return lax.all_gather(x, "dp", axis=0)

    def start_conv(self):
        return self.first

    def start_gate(self, after):
        x, _ = lax.optimization_barrier((self.order.now(self.gate[0]), after))
        return self.gathered(x)

    def start_second(self):
        return self.gathered(self.order.now(self.conv[1])), self.gathered(self.order.now(self.gate[1]))

    def trade_weights(self, x):
        x = self.order.now(x)
        return x, swap_core(x)

    def conv_weights(self, sp, both):
        return join_conv(sp, *both)

    def gate_weights(self, sp, both):
        return join_gate(sp, *both)

    def grad_gate(self, sp, layer, normed, dgate, gated, u):
        return grad_gate(sp, self.dp, self.rows, normed, dgate, gated, u)

    def grad_conv(self, sp, layer, normed, dconv):
        return grad_conv(sp, self.dp, self.rows, normed, dconv)

    def trade_grads(self, grads):
        return grads[0], swap_core(grads[1])

    def send(self, traded):
        (total,) = self.order(fold, *traded)
        return lax.psum_scatter(total, "dp", scatter_dimension=0, tiled=True)[0]

    def early(self, conv1, gate1, gate0):
        self.gates = [gate0, gate1]
        slots = self.order(total_line, [conv1, gate1, gate0])
        self.slots = [flip(x, m) if m else x for m, x in enumerate(slots)]

    def early_trade(self):
        self.came = swap_core(self.order(mix, self.slots, self.gates, WIDE))

    def late(self, conv0):
        late = self.order(total_line, [conv0])
        self.last = [flip(x, m) if m else x for m, x in enumerate(late)]

    def late_trade(self):
        self.last_came = swap_core(self.order(mix, self.slots, self.last, LOAD))

    def gradients(self):
        arrays = self.slots, self.last, self.gates, self.came, self.last_came
        return self.order(finish, self.block, *arrays)


def grouped(columns, block):
    lead = columns.shape[:-1]
    split = jnp.moveaxis(columns.reshape(lead + (-1, CTX, block)), -2, 0)
    return split.reshape((CTX,) + lead + (-1,))


def ungrouped(groups, block):
    lead = groups.shape[1:-1]
    split = groups.reshape((CTX,) + lead + (-1, block))
    return jnp.moveaxis(split, 0, -2).reshape(lead + (-1,))


def pad_to(x, rows, cols):
    room = [(0, 0)] * (x.ndim - 2) + [(0, rows - x.shape[-2]), (0, cols - x.shape[-1])]
    return jnp.pad(x, room)


class Plain:
    def __init__(self, mine, place, block, w_in, w_out):
        self.mine, self.place, self.block = mine, place, block
        full_in = lax.all_gather(w_in, ("dp", "ctx"), axis=0, tiled=True)
        full_out = lax.all_gather(w_out, ("dp", "ctx"), axis=0, tiled=True)
        self.full = [(full_in, full_out), (swap_core(full_in), swap_core(full_out))]
        self.grads = [{}, {}]

    def prepare_gate(self):
        pass

    def start_conv(self):
        return 0

    def start_gate(self, after):
        return 0

    def start_second(self):
        return 1, 1

    def trade_weights(self, layer):
        return layer

    def trade_grads(self, grads):
        return grads

    def send(self, traded):
        return traded

    def early(self, conv1, gate1, gate0):
        pass

    def early_trade(self):
        pass

    def late(self, conv0):
        pass

    def late_trade(self):
        pass

    def group(self, columns, block):
        return lax.dynamic_index_in_dim(grouped(columns, block), self.place, 0, False)

    def layer(self, layer, which):
        return choose(self.mine == layer, self.full[0][which], self.full[1][which])

    def conv_weights(self, sp, layer):
        one = self.layer(layer, 0)
        values = self.group(one[:, INNER : 2 * INNER], self.block * HEAD)
        step = self.group(one[:, 2 * INNER + 2 * STATE :], self.block)
        shared = one[:, 2 * INNER : 2 * INNER + 2 * STATE]
        return jnp.concatenate([values, shared, pad_to(step, step.shape[0], 128)], 1)

    def gate_weights(self, sp, layer):
        one, out = self.layer(layer, 0), self.layer(layer, 1)
        wide = self.block * HEAD
        return self.group(one[:, :INNER], wide), self.group(out.T, wide).T

    def over_tokens(self, a, b):
        both = [dot(x, y, ATB) for x, y in zip(a, b)]
        return (both[0] + both[1]).astype(BF16)

    def grad_gate(self, sp, layer, normed, dgate, gated, u):
        out = self.over_tokens(gated, u)
        self.grads[layer].update(gate=self.over_tokens(normed, dgate), out=out)
        return [out]

    def grad_conv(self, sp, layer, normed, dconv):
        self.grads[layer].update(conv=self.over_tokens(normed, dconv))
        return [self.grads[layer]["conv"]]

    def spread(self, columns, block):
        at = lax.broadcasted_iota(jnp.int32, (CTX, 1, 1), 0) == self.place
        return ungrouped(jnp.where(at, columns[None], jnp.zeros((), columns.dtype)), block)

    def gradients(self):
        wide = self.block * HEAD
        fulls = []
        for grads in self.grads:
            gate, conv = grads["gate"], grads["conv"]
            grad_in = jnp.concatenate(
                [
                    self.spread(gate, wide),
                    self.spread(conv[:, :WIDE], wide),
                    conv[:, WIDE:MIX],
                    self.spread(conv[:, MIX : MIX + LOCAL], self.block),
                ],
                -1,
            )
            fulls.append((grad_in, self.spread(grads["out"].T, wide).T))
        sums = []
        for a, b in zip(*fulls):
            zero = self.mine == 0
            total = choose(zero, a, b).astype(F32) + swap_core(choose(zero, b, a)).astype(F32)
            total = total.astype(BF16)
            sums.append(
                lax.psum_scatter(total, ("dp", "ctx"), scatter_dimension=0, tiled=True).astype(F32)
            )
        return sums[0], sums[1]


def prepare_kernel(block, sp, norm_ref, taps_ref, bias_ref, dt_ref, log_ref, skip_ref, gain_ref, out_ref):
    out_ref[...] = jnp.zeros_like(out_ref)
    for k in range(CTX):

        @pl.when(sp[0] == k)
        def _():
            for here, there, n in spans(k, block):
                out_ref[0:CONV, here : here + n] = taps_ref[0, :, there : there + n]
                out_ref[4:5, here : here + n] = bias_ref[:, there : there + n]
                out_ref[9:10, here : here + n] = gain_ref[:, there : there + n]
            spare = jnp.zeros((1, 128 - HEADS), F32)
            rows = [jnp.concatenate([ref[...], spare], axis=1) for ref in (dt_ref, log_ref, skip_ref)]
            rows = jnp.concatenate(rows + [jnp.zeros((5, 128), F32)])
            local = dot(rows, head_map(k, block, True), AB, HIGH)
            out_ref[10:11, 0:128] = local[0:1, :]
            out_ref[11:12, 0:128] = jnp.exp(local[1:2, :])
            out_ref[5:6, :WIDE] = dot(local, channel_map(True), AB, HIGH)[2:3, :]

    out_ref[0:CONV, WIDE:MIX] = taps_ref[0, :, INNER:]
    out_ref[4:5, WIDE:MIX] = bias_ref[:, INNER:]
    out_ref[8:9, :] = norm_ref[...]


def prepare(sp, block, arrays):
    out = shape((16, arrays[0].shape[1]), F32)
    return call("prepare", functools.partial(prepare_kernel, block), sp, arrays, [out], 12)[0]


def gather_small_kernel(counts, sp, *refs):
    keep_ref, send_ref = refs[-2:]
    packed, at = [], 0
    for layer in range(2):
        sums = []
        for count in counts[layer]:
            sums.append(sum(ref[...] for ref in refs[at : at + count]))
            at += count
        dcw, dhp, dgain, dnorm = sums
        tall = lax.broadcasted_iota(jnp.int32, (8, MIX), 0)
        gain = jnp.concatenate([dgain, jnp.zeros((8, MIX - WIDE), F32)], axis=1)
        short = dnorm.shape[1] - MIX
        norm_rest = jnp.concatenate([dnorm[:, MIX:], jnp.zeros((8, MIX - short), F32)], axis=1)
        middle = jnp.where(tall == 0, gain, jnp.where(tall == 1, dnorm[:, :MIX], norm_rest))
        heads = jnp.concatenate([dhp, jnp.zeros((8, MIX - 128), F32)], axis=1)
        packed.append(jnp.concatenate([dcw, middle, heads]))
    zero = sp[1] == 0
    keep_ref[...] = choose(zero, packed[0], packed[1])
    send_ref[...] = choose(zero, packed[1], packed[0])


def gather_small(sp, small):
    counts = [[len(kind) for kind in layer] for layer in small]
    arrays = [x for layer in small for kind in layer for x in kind]
    out = shape((PACK, MIX), F32)
    kernel = functools.partial(gather_small_kernel, counts)
    return call("gather_small", kernel, sp, arrays, [out, out], 12)


def spread_small_kernel(block, sp, *refs):
    slots, all_slots = refs[:CTX], refs[-1]
    norm_ref, taps_ref, bias_ref, dt_ref, log_ref, skip_ref, gain_ref = refs[CTX:-1]
    for m in range(CTX):
        all_slots[m ^ sp[0]] = slots[m][...]
    total = sum(all_slots[k] for k in range(CTX))
    norm_ref[:, :MIX] = total[9:10, :]
    norm_ref[:, MIX:] = total[10:11, : norm_ref.shape[1] - MIX]
    taps_ref[0, :, INNER:] = total[0:CONV, WIDE:]
    bias_ref[:, INNER:] = total[4:5, WIDE:]
    pick = channel_map()
    heads = 0.0
    for k in range(CTX):
        for here, there, n in spans(k, block):
            taps_ref[0, :, there : there + n] = all_slots[k, 0:CONV, here : here + n]
            bias_ref[:, there : there + n] = all_slots[k, 4:5, here : here + n]
            gain_ref[:, there : there + n] = all_slots[k, 8:9, here : here + n]
        skip = dot(all_slots[k, 0:8, :WIDE], pick, AB, HIGH)
        both = jnp.concatenate([all_slots[k, 16:24, :128], skip])
        heads = heads + dot(both, head_map(k, block), AB, HIGH)
    dt_ref[...] = heads[0:1, :HEADS]
    log_ref[...] = heads[1:2, :HEADS]
    skip_ref[...] = heads[13:14, :HEADS]


def spread_small(sp, block, slots, d):
    one = shape((1, HEADS), F32)
    return call(
        "spread_small",
        functools.partial(spread_small_kernel, block),
        sp,
        slots,
        [
            shape((1, d), F32),
            shape((1, CONV, CONV_DIM), F32),
            shape((1, CONV_DIM), F32),
            one,
            one,
            one,
            shape((1, INNER), F32),
        ],
        12,
        scratch=[pltpu.VMEM((CTX, PACK, MIX), F32)],
    )


def sum_over_dp(x, dp, step, end):
    if dp & (dp - 1):
        return lax.psum(x, "dp") if step == 1 else x
    while step < end:
        x = x + lax.ppermute(x, "dp", [(i, i ^ step) for i in range(dp)])
        step *= 2
    return x


class Order:
    def __init__(self, sp):
        self.sp = sp

    def __call__(self, kernel, *args):
        out = kernel(self.sp, *args)
        self.after(out[0] if isinstance(out, (list, tuple)) else out)
        return out

    def after(self, x):
        self.sp, _ = lax.optimization_barrier((self.sp, x))

    def now(self, x):
        return lax.optimization_barrier((x, self.sp))[0]


def shards(
    tokens,
    cotangent,
    doc_lengths,
    norm_gain,
    w_in,
    conv_weight,
    conv_bias,
    dt_bias,
    a_log,
    d_skip,
    inner_gain,
    w_out,
):
    mine, place = lax.axis_index("section"), lax.axis_index("ctx")
    dp = lax.axis_size("dp")
    piece, d = tokens.shape[2], tokens.shape[3]
    seg_len = piece * CTX // SEGS
    direct = dp == 4 and w_out.shape[1] % HEAD == 0 and w_out.shape[1] * dp == WIDE
    block = w_out.shape[1] // HEAD if direct else LOCAL

    own_x = lax.dynamic_index_in_dim(tokens, mine, 0, False)[0]
    own_u = lax.dynamic_index_in_dim(cotangent, mine, 0, False)[0]
    lengths = lax.dynamic_index_in_dim(doc_lengths, mine, 0, False)[0]
    start = jnp.stack([place, mine, lax.axis_index("dp")]).astype(jnp.int32)
    sp = jnp.concatenate([start, jnp.cumsum(lengths) - lengths])
    run = Order(sp)
    if direct:
        carrier = Direct(run, mine, dp, block, w_in[0], w_out[0])
    else:
        carrier = Plain(mine, place, block, w_in[0], w_out[0])

    def natural(slots):
        return jnp.concatenate(slots).reshape(CTX, 2, piece // 2, d)

    rows_x = gather_slots(run, run.now(own_x))
    arrays = [norm_gain, conv_weight, conv_bias, dt_bias, a_log, d_skip, inner_gain]
    params = run(prepare, block, arrays)
    other = swap_core(params)
    params = [choose(mine == 0, params, other), choose(mine == 0, other, params)]
    carrier.prepare_gate()
    rows_x = natural(rows_x())
    conv0 = carrier.start_conv()
    run.after(rows_x)
    gate0 = carrier.start_gate(conv0)
    conv0 = carrier.trade_weights(conv0)
    rows_u = gather_slots(run, run.now(own_u))
    no_state, no_tail = jnp.zeros((STATE, WIDE), F32), jnp.zeros((16, MIX), BF16)

    def forward(layer, s, pieces, wc, state, tail, between=None):
        normed, conv_in, step_raw = run(project, pieces, params[layer], wc, seg_len)
        if between is not None:
            between()
        y, states, state, next_tail = run(
            scan_rows, s, conv_in, step_raw, params[layer], state, tail
        )
        return dict(
            normed=normed, conv_in=conv_in, step_raw=step_raw, y=y, states=states, tail=tail
        ), state, next_tail

    wc0 = run(carrier.conv_weights, conv0)
    conv1, gate1 = carrier.start_second()
    first, second = [None, None], [None, None]
    state, tail = no_state, no_tail
    first[0], state, tail = forward(0, 0, natural_slots(rows_x, 0), wc0, state, tail)
    first[1], state, tail = forward(0, 1, natural_slots(rows_x, 1), wc0, state, tail)
    rows_u = rows_u()
    gate0 = carrier.trade_weights(gate0)
    wg0, wo0 = run(carrier.gate_weights, gate0)
    stats, sums = [None, None], [None, None]
    for s in range(SEGS):
        saved = first[s]
        saved["gate"], stats[s], *sums[s] = run(
            out_rows, True, [], [], saved["normed"], saved["y"], params[0], wg0, wo0
        )
        if s == 0:
            sums[0] = scatter_start(*sums[0])

    def own_step(s):
        residual = natural_slots(rows_x, s)[:1]
        first[s]["stats"] = [stats[s]] + [tail_tile(x) for x in sums[s][1:4]]
        own, first[s]["branch"] = run(own_rows, False, first[s]["stats"], sums[s], residual)
        first[s]["own"] = own
        return gather_slots(run, own)

    sums[0] = scatter_slots(run, *sums[0])
    sums[1] = scatter_start(*[run.now(x) for x in sums[1]])
    middle = [own_step(0), None]
    sums[1] = scatter_slots(run, *sums[1])
    middle[0] = middle[0]()
    rows_u = natural(rows_u)
    run.after(rows_u)

    conv1 = carrier.trade_weights(conv1)
    wc1 = run(carrier.conv_weights, conv1)
    middle[1] = own_step(1)
    state, tail = no_state, no_tail
    parts, before = [], []

    def last_rows():
        middle[1] = middle[1]()

    for s in range(SEGS):
        between = last_rows if s == 0 else None
        second[s], state, tail = forward(1, s, middle[s], wc1, state, tail, between)
        if s == 0:
            run.after(middle[1][3:])
            gate1 = carrier.trade_weights(gate1)
    wg1, wo1 = run(carrier.gate_weights, gate1)
    for s in range(SEGS):
        saved = second[s]
        saved["gate"], stats, part = run(
            out_rows,
            False,
            before,
            natural_slots(rows_u, s),
            saved["normed"],
            saved["y"],
            params[1],
            wg1,
            wo1,
        )
        before = [stats]
        parts.append(part)
    stats = from_all(stats)
    part1 = run(collect, parts)
    hidden0 = run(natural_rows, middle)

    def gate_step(layer, s, saved, pieces, stats, first_stat, inners, wo):
        out = run(
            gate_back, pieces, stats, first_stat, inners, saved["y"], saved["gate"], params[layer], wo
        )
        saved.update(zip(("dy", "dgate", "gated", "u", "dgain"), out))

    def scan_step(layer, s, saved, dstate, later):
        saved["dconv"], saved["dcw"], saved["dhp"], dstate, later = run(
            scan_back,
            layer == 0,
            s,
            saved["conv_in"],
            saved["step_raw"],
            saved["dy"],
            saved["states"],
            saved["tail"],
            params[layer],
            dstate,
            later,
        )
        return dstate, later

    def of(saved, *names):
        return [[one[name] for one in saved] for name in names]

    def back_start(s):
        saved = second[s]
        return scatter_start(*run(input_back, True, saved["dconv"], saved["dgate"], wc1, wg1))

    def back_end(s, part):
        up, second[s]["dnorm"] = run(
            own_back,
            16,
            part,
            [far(first[s]["own"])],
            natural_slots(rows_u, s)[:1],
            params[1],
            far(first[s]["branch"]),
        )
        return gather_slots(run, up, 16)

    upper = [None, None]

    def lower_gate(s):
        inners = [head_tile(x) for x in upper[s][:4]]
        gate_step(0, s, first[s], upper[s], first[s]["stats"], 0, inners, wo0)

    for s in (1, 0):
        gate_step(1, s, second[s], natural_slots(rows_u, s), stats, 8 * s, [], wo1)
    gate1 = carrier.trade_grads(run(carrier.grad_gate, 1, *of(second, "normed", "dgate", "gated", "u")))
    part1 = scatter_start(*part1)
    dstate, later = no_state, jnp.zeros((8, MIX), F32)
    dstate, later = scan_step(1, 1, second[1], dstate, later)
    part1 = scatter_slots(run, *part1)
    gate1 = carrier.send(gate1)
    upper[1] = back_start(1)
    dstate, later = scan_step(1, 0, second[0], dstate, later)
    hidden1, _ = run(own_rows, True, stats, part1, [hidden0])
    upper[1] = scatter_slots(run, *upper[1])
    upper[0] = back_start(0)
    upper[1] = back_end(1, upper[1])
    conv1 = carrier.trade_grads(run(carrier.grad_conv, 1, *of(second, "normed", "dconv")))
    upper[1] = upper[1]()
    upper[0] = scatter_slots(run, *upper[0])
    conv1 = carrier.send(conv1)
    lower_gate(1)
    upper[0] = back_end(0, upper[0])
    dstate, later = no_state, jnp.zeros((8, MIX), F32)
    dstate, later = scan_step(0, 1, first[1], dstate, later)
    upper[0] = upper[0]()
    (part_1,) = run(input_back, False, first[1]["dconv"], first[1]["dgate"], wc0, wg0)
    lower_gate(0)
    gate0 = carrier.trade_grads(run(carrier.grad_gate, 0, *of(first, "normed", "dgate", "gated", "u")))
    grads1 = run(natural_rows, upper, 16)
    gate0 = carrier.send(gate0)
    dstate, later = scan_step(0, 0, first[0], dstate, later)
    conv0 = carrier.trade_grads(run(carrier.grad_conv, 0, *of(first, "normed", "dconv")))
    (part_0,) = run(input_back, False, first[0]["dconv"], first[0]["dgate"], wc0, wg0)
    conv0 = carrier.send(conv0)
    part = scatter_start(*run(collect, [far(part_0), far(part_1)]))
    part = scatter_slots(run, *part)
    carrier.early(conv1, gate1, gate0)
    branch = jnp.zeros((piece, d), F32)
    grads0, dnorm0 = run(own_back, 0, part, [own_x], [grads1], params[0], branch)
    carrier.early_trade()
    small = [
        of(first, "dcw", "dhp", "dgain") + [[dnorm0]],
        of(second, "dcw", "dhp", "dgain", "dnorm"),
    ]
    keep, small_sent = run(gather_small, small)
    total = sum_over_dp(keep + swap_core(small_sent), dp, 1, dp)
    carrier.late(conv0)
    carrier.late_trade()
    total = from_all(run.now(total))
    shard_in, shard_out = carrier.gradients()
    norm, taps, bias, dt, log, skip, gain = spread_small(sp, block, total, d)

    def to_layers(a, b):
        here, there = choose(mine == 0, a, b), swap_core(choose(mine == 0, b, a))
        both = jnp.stack([choose(mine == 0, here, there), choose(mine == 0, there, here)])
        return both[None, :, None]

    return (
        to_layers(hidden0, hidden1),
        to_layers(grads0, grads1),
        norm,
        shard_in[None],
        taps,
        bias,
        dt,
        log,
        skip,
        gain,
        shard_out[None],
    )


def solution(mesh):
    in_specs = (
        P(None, "dp", "ctx", None),
        P(None, "dp", "ctx", None),
        P(None, "dp", None),
        P("section", None),
        P("section", ("dp", "ctx"), None),
        P("section", None, None),
        P("section", None),
        P("section", None),
        P("section", None),
        P("section", None),
        P("section", None),
        P("section", ("dp", "ctx"), None),
    )
    out_specs = (
        P("section", None, "dp", "ctx", None),
        P("section", None, "dp", "ctx", None),
        P("section", None),
        P("section", ("dp", "ctx"), None),
        P("section", None, None),
        P("section", None),
        P("section", None),
        P("section", None),
        P("section", None),
        P("section", None),
        P("section", ("dp", "ctx"), None),
    )
    return jax.shard_map(shards, mesh=mesh, in_specs=in_specs, out_specs=out_specs, check_vma=False)
```

```python
import functools

import jax
import jax.numpy as jnp
from jax import lax
from jax.experimental import pallas as pl
from jax.experimental.pallas import tpu as pltpu
from jax.sharding import PartitionSpec as P

HEADS = 48
HEAD = 64
STATE = 128
CONV = 4
INNER = 3072
CONV_DIM = 3328
NORM_EPS = 1e-05

F32 = jnp.float32
BF16 = jnp.bfloat16
HIGH = lax.Precision.HIGHEST
CTX = 4
SEGS = 2
LOCAL = HEADS // CTX
WIDE = LOCAL * HEAD
MIX = WIDE + 2 * STATE
FULL = MIX + 128
HALF = WIDE // 2
LOAD = HALF + STATE + 128
PACK = 24
MIB = 1024 * 1024
MICROS = {
    "project": 3,
    "scan_rows": 8,
    "out_rows": 4,
    "gate_back": 3,
    "scan_back": 16,
    "input_back": 4,
    "grad_gate": 8,
    "grad_conv": 6,
}


def swap_core(x):
    return lax.ppermute(x, "section", [(0, 1), (1, 0)])


def flip(x, bits):
    return lax.ppermute(x, "ctx", [(i, i ^ bits) for i in range(CTX)])


def gather_slots(order, own, extra=0):
    half = (own.shape[0] - extra) // 2
    x, y = flip(own, 1), flip(own, 2)

    def forward():
        order.after((x, y))
        first, second = order.now(y[: extra + half]), order.now(x[extra + half :])
        return [own, x, y, flip(first, 1), flip(second, 2)]

    return forward


def scatter_start(own, to_x, to_y, late_x, late_y):
    return own, flip(to_x, 1), flip(to_y, 2), late_x, late_y


def scatter_slots(order, own, from_x, from_y, late_x, late_y):
    extra = from_x.shape[0] - 2 * late_x.shape[0]
    outs = [shape((late_x.shape[0] + extra, late_x.shape[1]), BF16), late_y]
    late_x, late_y = order(call_with("turn", turn_kernel, [from_x, from_y, late_x, late_y], outs))
    return [own, from_x, from_y, flip(late_x, 1), flip(late_y, 2)]


def from_all(x):
    return [x] + [flip(x, m) for m in range(1, CTX)]


def dot(a, b, dims, precision=None):
    return lax.dot_general(a, b, (dims, ((), ())), precision=precision, preferred_element_type=F32)


AB = ((1,), (0,))
ABT = ((1,), (1,))
ATB = ((0,), (0,))


def far(x):
    return pltpu.with_memory_space_constraint(x, pltpu.HBM)


def call_with(name, kernel, ins, outs):
    return lambda sp: call(name, kernel, sp, ins, outs)


def split_dot(a, b, dims):
    a_high, b_high = a.astype(BF16), b.astype(BF16)
    a_low = (a - a_high.astype(F32)).astype(BF16)
    b_low = (b - b_high.astype(F32)).astype(BF16)
    return dot(a_high, b_high, dims) + dot(a_low, b_high, dims) + dot(a_high, b_low, dims)


def whole(x):
    zeros = (0,) * len(x.shape)
    return pl.BlockSpec(tuple(x.shape), lambda i, sp: zeros)


def shape(dims, dtype):
    return jax.ShapeDtypeStruct(dims, dtype)


def call(name, kernel, sp, ins, outs, vmem=20, grid=1, scratch=()):
    ins = [x if isinstance(x, tuple) else (x, whole(x)) for x in ins]
    outs = [x if isinstance(x, tuple) else (x, whole(x)) for x in outs]
    return pl.pallas_call(
        kernel,
        grid_spec=pltpu.PrefetchScalarGridSpec(
            num_scalar_prefetch=1,
            grid=(grid,),
            in_specs=[spec for _, spec in ins],
            out_specs=[spec for _, spec in outs],
            scratch_shapes=list(scratch),
        ),
        out_shape=[x for x, _ in outs],
        compiler_params=pltpu.CompilerParams(
            dimension_semantics=("arbitrary",), vmem_limit_bytes=vmem * MIB
        ),
        cost_estimate=pl.CostEstimate(
            flops=int(MICROS.get(name, 1) * 1e9), bytes_accessed=1, transcendentals=0
        ),
        name=name,
    )(sp, *[x for x, _ in ins])


def natural_spec(x, seg, slot):
    def at(i, sp):
        inside = slot ^ sp[0]
        return (2 * seg + (inside >> 1)) ^ sp[0], inside & 1, 0, 0

    return pl.BlockSpec((1, 1) + x.shape[2:], at)


def natural_slots(x, seg):
    x = far(x)
    return [(x, natural_spec(x, seg, m)) for m in range(CTX)]


def load_rows(refs, extra=0):
    first = 0
    for n, ref in enumerate(refs):
        value = ref[...]
        value = value.reshape(value.shape[-2:])
        if extra and n < 4:
            value = value[extra:]
        yield first, value
        first += value.shape[0]


def row_scale(x):
    return lax.rsqrt(jnp.mean(x * x, axis=-1, keepdims=True) + NORM_EPS)


def project_kernel(count, sp, *refs):
    cw_ref, wc_ref, normed_ref, conv_ref, step_ref = refs[count:]
    gain = cw_ref[8:9, :]
    for first, x in load_rows(refs[:count]):
        x = x.astype(F32)
        rows = pl.ds(first, x.shape[0])
        normed_ref[rows, :] = (x * row_scale(x) * gain).astype(BF16)
    normed = normed_ref[...]
    conv_ref[...] = dot(normed, wc_ref[:, :MIX], AB).astype(BF16)
    step_ref[...] = dot(normed, wc_ref[:, MIX:], AB)


def project(sp, pieces, cw, wc, tokens):
    return call(
        "project",
        functools.partial(project_kernel, len(pieces)),
        sp,
        pieces + [cw, wc],
        [
            shape((tokens, wc.shape[0]), BF16),
            shape((tokens, MIX), BF16),
            shape((tokens, 128), F32),
        ],
    )


def bounds_of(sp):
    return [sp[3 + d] for d in range(sp.shape[0] - 3)]


def distances(sp, first, rows):
    at = lax.broadcasted_iota(jnp.int32, (rows, 1), 0) + first
    since = at
    for bound in bounds_of(sp):
        gap = at - bound
        since = jnp.where(gap >= 0, jnp.minimum(since, gap), since)
    return since


def segment(sp, at):
    total = jnp.zeros_like(at)
    for bound in bounds_of(sp):
        total = total + jnp.where(at >= bound, 1, 0)
    return total


def pair_lanes(a, pair):
    rows = a.shape[0]
    low = lax.broadcasted_iota(jnp.int32, (rows, 2 * HEAD), 1) < HEAD
    first = jnp.broadcast_to(a[:, 2 * pair : 2 * pair + 1], (rows, 2 * HEAD))
    second = jnp.broadcast_to(a[:, 2 * pair + 1 : 2 * pair + 2], (rows, 2 * HEAD))
    return jnp.where(low, first, second)


def conv_forward(ext, cw_ref, since, cols, q):
    total = cw_ref[4:5, cols] + cw_ref[3:4, cols] * ext[8 : 8 + q, cols]
    for shift in range(1, CONV):
        tap = cw_ref[3 - shift : 4 - shift, cols]
        rows = ext[8 - shift : 8 - shift + q, cols]
        total = total + jnp.where(since >= shift, tap * rows, 0.0)
    return total


def block_terms(sp, first, q, raw, cw_ref):
    row = lax.broadcasted_iota(jnp.int32, (q, 1), 0)
    col = lax.broadcasted_iota(jnp.int32, (1, q), 1)
    seg_col, seg_row = segment(sp, row + first), segment(sp, col + first)
    seg_before, seg_last = jnp.int32(0), jnp.int32(0)
    for bound in bounds_of(sp):
        seg_before = seg_before + jnp.where(first - 1 >= bound, 1, 0)
        seg_last = seg_last + jnp.where(first + q - 1 >= bound, 1, 0)
    same = seg_col == seg_row
    shifted = raw + cw_ref[10:11, 0:128]
    stepsize = jax.nn.softplus(shifted)
    decay = -stepsize * cw_ref[11:12, 0:128]
    lower = jnp.where(row >= col, 1.0, 0.0)
    cum = dot(lower, decay, AB, HIGH)
    last = cum[q - 1 : q, :]
    open_w = jnp.where(seg_col == seg_before, jnp.exp(cum), 0.0)
    tail = jnp.where(seg_col == seg_last, jnp.exp(jnp.minimum(last - cum, 0.0)), 0.0)
    passed = jnp.where(seg_last == seg_before, jnp.exp(last), 0.0)
    return row, col, same, shifted, stepsize, decay, cum, open_w, tail, passed


def pair_cols(pair):
    return slice(2 * HEAD * pair, 2 * HEAD * (pair + 1))


def scan_kernel(
    seg,
    sp,
    ci_ref,
    raw_ref,
    cw_ref,
    st_in_ref,
    tail_in_ref,
    y_ref,
    st_ref,
    st_out_ref,
    tail_out_ref,
    ext,
    mix,
    state,
    flow,
    fresh,
):
    k = pl.program_id(0)
    q = ci_ref.shape[0]
    first = (CTX * seg + k) * q

    @pl.when(k == 0)
    def _():
        state[...] = st_in_ref[...]
        ext[0:8, :] = tail_in_ref[...].astype(F32)[8:16, :]

    ci = ci_ref[...]
    tail_out_ref[...] = ci[q - 16 : q, :]
    ext[8 : 8 + q, :] = ci.astype(F32)
    since = distances(sp, first, q)
    for c in range(0, MIX, 128):
        cols = slice(c, c + 128)
        pre = conv_forward(ext, cw_ref, since, cols, q)
        mix[:, cols] = pre * jax.nn.sigmoid(pre)
    ext[0:8, :] = ext[q : q + 8, :]

    row, col, same, _, stepsize, _, cum, open_w, tail, passed = block_terms(
        sp, first, q, raw_ref[...], cw_ref
    )
    cum_t = cum.T
    keys = mix[:, WIDE : WIDE + STATE]
    kt = keys.T.astype(BF16)
    queries = mix[:, WIDE + STATE :]
    qb = queries.astype(BF16)
    scores = jnp.where(same & (row >= col), split_dot(queries, keys, ABT), 0.0)
    st_ref[...] = state[...]
    flow[...] = split_dot(queries, state[...], AB)
    low = lax.broadcasted_iota(jnp.int32, (q, 2 * HEAD), 1) < HEAD
    tail = tail * stepsize
    for pair in range(LOCAL // 2):
        cols = pair_cols(pair)
        v = mix[:, cols]
        vs = v * pair_lanes(stepsize, pair)
        outs = []
        for h in (2 * pair, 2 * pair + 1):
            damp = jnp.exp(jnp.minimum(cum[:, h : h + 1] - cum_t[h : h + 1, :], 0.0))
            outs.append(split_dot(scores * damp, vs, AB))
        inflow = flow[:, cols] * pair_lanes(open_w, pair)
        y = jnp.where(low, outs[0], outs[1]) + inflow + cw_ref[5:6, cols] * v
        y_ref[:, cols] = y
        fresh[:, cols] = (v * pair_lanes(tail, pair)).astype(BF16)
    update = dot(kt, fresh[...], AB)
    for pair in range(LOCAL // 2):
        cols = pair_cols(pair)
        state[:, cols] = state[:, cols] * pair_lanes(passed, pair) + update[:, cols]
    st_out_ref[...] = state[...]


def scan_rows(sp, seg, conv_in, step_raw, cw, state, tail):
    q = conv_in.shape[0] // CTX

    def here(x):
        return x, pl.BlockSpec((q, x.shape[1]), lambda k, sp: (k ^ sp[0], 0))

    tokens = conv_in.shape[0]
    states = pltpu.HBM((CTX * STATE, WIDE), F32)
    return call(
        "scan_rows",
        functools.partial(scan_kernel, seg),
        sp,
        [here(conv_in), here(step_raw), cw, state, tail],
        [
            here(shape((tokens, WIDE), F32)),
            (states, pl.BlockSpec((STATE, WIDE), lambda k, sp: (k, 0))),
            shape((STATE, WIDE), F32),
            shape((16, MIX), BF16),
        ],
        16,
        grid=CTX,
        scratch=[
            pltpu.VMEM((q + 8, MIX), F32),
            pltpu.VMEM((q, MIX), F32),
            pltpu.VMEM((STATE, WIDE), F32),
            pltpu.VMEM((q, WIDE), F32),
            pltpu.VMEM((q, WIDE), BF16),
        ],
    )


def stat_rows(columns):
    rows = columns[0].shape[0]
    lane = lax.broadcasted_iota(jnp.int32, (rows, 128), 1)
    table = jnp.zeros((rows, 128), F32)
    for i, column in enumerate(columns):
        table = jnp.where(lane == i, column, table)
    return table.T[0:8, :]


def stat_columns(rows):
    return jnp.concatenate([rows, jnp.zeros((120, rows.shape[1]), F32)]).T


def split_rows(row, cols):
    high = row.astype(BF16).astype(F32)
    middle = (row - high).astype(BF16).astype(F32)
    low = row - high - middle
    sub = lax.broadcasted_iota(jnp.int32, (16, row.shape[1]), 0)
    tile = jnp.where(sub == 0, high, jnp.where(sub == 1, middle, jnp.where(sub == 2, low, 0.0)))
    spare = jnp.zeros((16, cols - row.shape[1]), F32)
    return jnp.concatenate([tile, spare], axis=1).astype(BF16)


def stat_row(ref, row, count):
    if ref.dtype == F32:
        return ref[row : row + 1, :count]
    tile = ref[...].astype(F32)
    return tile[0:1, :count] + tile[1:2, :count] + tile[2:3, :count]


def store_slots(part, stat, part_refs):
    own_ref, x_ref, y_ref, late_x_ref, late_y_ref = part_refs
    q = own_ref.shape[0]
    half = q // 2
    part = part.astype(BF16)
    own_ref[...] = part[:q]
    x_ref[:half, :] = part[3 * q : 3 * q + half]
    x_ref[half:q, :] = part[q : q + half]
    y_ref[:half, :] = part[3 * q + half :]
    y_ref[half:q, :] = part[2 * q + half : 3 * q]
    late_x_ref[...] = part[q + half : 2 * q]
    late_y_ref[...] = part[2 * q : 2 * q + half]
    if stat is not None:
        tile = split_rows(stat, part.shape[1])
        x_ref[q:, :] = tile
        y_ref[q:, :] = tile


def store_part(part, stat, part_refs):
    if len(part_refs) == 1:
        part_refs[0][...] = part.astype(BF16)
    else:
        store_slots(part, stat, part_refs)


def part_shapes(slots, tokens, d, extra=0):
    if not slots:
        return [shape((tokens, d), BF16)]
    q = tokens // CTX
    sent = shape((q + extra, d), BF16)
    return [shape((q, d), BF16), sent, sent] + [shape((q // 2, d), BF16)] * 2


def tail_tile(x):
    return x, pl.BlockSpec((16, x.shape[1]), lambda i, sp: (x.shape[0] // 16 - 1, 0))


def head_tile(x):
    return x, pl.BlockSpec((16, x.shape[1]), lambda i, sp: (0, 0))


def turn_kernel(sp, from_x_ref, from_y_ref, late_x_ref, late_y_ref, x_ref, y_ref):
    half = y_ref.shape[0]
    x_ref[:half, :] = (late_x_ref[...].astype(F32) + from_y_ref[:half, :].astype(F32)).astype(BF16)
    y_ref[...] = (late_y_ref[...].astype(F32) + from_x_ref[:half, :].astype(F32)).astype(BF16)
    if x_ref.shape[0] > half:
        x_ref[half:, :] = from_y_ref[2 * half :, :]


def out_kernel(count, before, sp, *refs):
    if before:
        before_ref, refs = refs[0], refs[1:]
    normed_ref, y_ref, cw_ref, wg_ref, wo_ref = refs[count : count + 5]
    gate_ref, stat_ref = refs[count + 5 : count + 7]
    gate = dot(normed_ref[...], wg_ref[...], AB)
    gate_ref[...] = gate
    g = y_ref[...] * gate * jax.nn.sigmoid(gate)
    part = dot((g * cw_ref[9:10, :WIDE]).astype(BF16), wo_ref[...], AB)
    square = jnp.sum(g * g, axis=-1, keepdims=True)
    inner = [
        jnp.sum(part[first : first + u.shape[0]] * u.astype(F32), axis=-1, keepdims=True)
        for first, u in load_rows(refs[:count])
    ]
    rows = stat_rows([square] + ([jnp.concatenate(inner)] if inner else []))
    store_part(part, rows[0:1, :], refs[count + 7 :])
    if before:
        rows = jnp.concatenate([before_ref[...], rows])
    stat_ref[...] = rows


def out_rows(sp, slots, before, pieces, normed, y, cw, wg, wo):
    tokens, d = normed.shape
    return call(
        "out_rows",
        functools.partial(out_kernel, len(pieces), len(before)),
        sp,
        before + pieces + [normed, y, cw, wg, wo],
        [shape((tokens, WIDE), F32), shape((8 + 8 * len(before), tokens), F32)] + part_shapes(slots, tokens, d, 16),
        28,
    )


def slot_sums(stat_refs, row, q):
    out = []
    for slot in range(CTX):
        total = 0.0
        for m, ref in enumerate(stat_refs):
            total = total + stat_row(ref, row, CTX * q)[:, (slot ^ m) * q : (slot ^ m) * q + q]
        out.append(total)
    return jnp.concatenate(out, axis=1)


def own_sum(refs):
    own, from_x, from_y, late_x, late_y = [ref[...].astype(F32) for ref in refs]
    half = late_y.shape[0]
    x = jnp.concatenate([from_x[half : 2 * half], late_x[:half]])
    return own + x + jnp.concatenate([late_y, from_y[half : 2 * half]])


def own_squares(stats, sp, natural, q):
    if not natural:
        rows = [stat_row(ref, 0, CTX * q) for ref in stats]
        return sum(row[:, m * q : m * q + q] for m, row in enumerate(rows))
    place, out = sp[0], []
    block = q // 2
    for half in range(2):
        total = jnp.zeros((1, block), F32)
        for s in range(SEGS):
            for slot in range(CTX):
                here = ((place >> 1) == s) & ((slot ^ place) == 2 * (place & 1) + half)
                for m, ref in enumerate(stats):
                    value = ref[8 * s : 8 * s + 1, pl.ds((slot ^ m) * block, block)]
                    total = total + jnp.where(here, value, 0.0)
        out.append(total)
    return jnp.concatenate(out, axis=1)


def own_kernel(count, natural, sp, *refs):
    stats, partial = refs[:CTX], refs[CTX : CTX + 5]
    residual = jnp.concatenate([x for _, x in load_rows(refs[CTX + 5 : CTX + 5 + count])])
    own_ref, branch_ref = refs[CTX + 5 + count :]
    square = own_squares(stats, sp, natural, own_ref.shape[0])
    square = jnp.concatenate([square, jnp.zeros((7, square.shape[1]), F32)])
    scale = lax.rsqrt(stat_columns(square)[:, 0:1] / INNER + NORM_EPS)
    branch = own_sum(partial) * scale
    branch_ref[...] = branch
    own_ref[...] = (residual.astype(F32) + branch).astype(BF16)


def own_rows(sp, natural, stats, partial, residual):
    q, d = partial[0].shape
    return call(
        "own_rows",
        functools.partial(own_kernel, len(residual), natural),
        sp,
        stats + partial + residual,
        [shape((q, d), BF16), shape((q, d), F32)],
        16,
    )


def collect_kernel(sp, part0_ref, part1_ref, own_ref, x_ref, y_ref, late_x_ref, late_y_ref):
    place = sp[0]
    q = late_x_ref.shape[0]
    goals = [
        [own_ref.at[pl.ds(0, q)], own_ref.at[pl.ds(q, q)]],
        [x_ref.at[pl.ds(q, q)], late_x_ref],
        [late_y_ref, y_ref.at[pl.ds(q, q)]],
        [x_ref.at[pl.ds(0, q)], y_ref.at[pl.ds(0, q)]],
    ]
    for m in range(CTX):
        owner = place ^ m
        for half in range(2):
            slot = (2 * (owner & 1) + half) ^ place
            rows = pl.ds(pl.multiple_of(slot * q, q), q)
            goals[m][half][...] = choose((owner >> 1) == 0, part0_ref[rows, :], part1_ref[rows, :])


def collect(sp, parts):
    tokens, d = parts[0].shape
    return call("collect", collect_kernel, sp, list(parts), part_shapes(True, 2 * tokens, d), 20)


def natural_kernel(extra, sp, *refs):
    out_ref = refs[-1]
    q = out_ref.shape[0] // 2
    for place in range(CTX):
        s = place >> 1
        own, x, y, first, second = refs[5 * s : 5 * s + 5]

        @pl.when(sp[0] == place)
        def _():
            for half in range(2):
                slot = (2 * (place & 1) + half) ^ place
                at = half * q
                if slot < 3:
                    out_ref[at : at + q, :] = (own, x, y)[slot][extra:, :]
                else:
                    out_ref[at : at + q // 2, :] = first[extra:, :]
                    out_ref[at + q // 2 : at + q, :] = second[...]


def natural_rows(sp, pieces, extra=0):
    q, d = pieces[0][0].shape
    ins = [x for one in pieces for x in one]
    kernel = functools.partial(natural_kernel, extra)
    return call("natural_rows", kernel, sp, ins, [shape((2 * (q - extra), d), BF16)])[0]


def gate_back_kernel(count, inners, first_stat, sp, *refs):
    pieces, stats = refs[:count], refs[count : count + CTX]
    inner_refs = refs[count + CTX : count + CTX + inners]
    rest = refs[count + CTX + inners :]
    y_ref, gate_ref, cw_ref, wo_ref, dy_ref, dgate_ref, gated_ref, u_ref, dgain_ref = rest
    gain = cw_ref[9:10, :WIDE]
    tokens = y_ref.shape[0]
    q = tokens // CTX
    for first, u in load_rows(pieces, 16 if inners else 0):
        u_ref[pl.ds(first, u.shape[0]), :] = u
    back = dot(u_ref[...], wo_ref[...], ABT)
    scale = lax.rsqrt(slot_sums(stats, first_stat, q) / INNER + NORM_EPS)
    if inners:
        inner = jnp.concatenate([stat_row(ref, 0, q) for ref in inner_refs], axis=1)
    else:
        inner = slot_sums(stats, first_stat + 1, q) * scale
    pull = scale * scale * inner / INNER
    table = stat_columns(jnp.concatenate([scale, pull, jnp.zeros((6, tokens), F32)]))
    scale, pull = table[:, 0:1], table[:, 1:2]
    gate = gate_ref[...]
    y = y_ref[...]
    sig = jax.nn.sigmoid(gate)
    act = gate * sig
    g = y * act
    unit = g * scale
    gated_ref[...] = (unit * gain).astype(BF16)
    dg = back * gain * scale - g * pull
    dy_ref[...] = (dg * act).astype(BF16)
    dgate_ref[...] = (dg * y * (sig + act * (1.0 - sig))).astype(BF16)
    dgain_ref[...] = jnp.broadcast_to(jnp.sum(back * unit, axis=0, keepdims=True), (8, WIDE))


def gate_back(sp, pieces, stats, first_stat, inners, y, gate, cw, wo):
    tokens, d = y.shape[0], wo.shape[1]
    return call(
        "gate_back",
        functools.partial(gate_back_kernel, len(pieces), len(inners), first_stat),
        sp,
        pieces + stats + inners + [y, gate, cw, wo],
        [shape((tokens, WIDE), BF16)] * 3 + [shape((tokens, d), BF16), shape((8, WIDE), F32)],
        28,
    )


def scan_back_kernel(
    seg,
    sp,
    ci_ref,
    prev_ref,
    raw_ref,
    dy_ref,
    st_ref,
    tail_in_ref,
    cw_ref,
    dst_in_ref,
    next_in_ref,
    dci_ref,
    dcw_ref,
    dhp_ref,
    dst_out_ref,
    next_out_ref,
    ext,
    mix,
    slope,
    dext,
    dstate,
    tails,
    dyw,
    flow,
    kept_all,
    ends,
):
    i = pl.program_id(0)
    k = CTX - 1 - i
    q = ci_ref.shape[0]
    first = (CTX * seg + k) * q

    @pl.when(i == 0)
    def _():
        dstate[...] = dst_in_ref[...]
        dext[q : q + 8, :] = next_in_ref[...]
        ends[...] = jnp.zeros_like(ends)
        dcw_ref[...] = jnp.zeros_like(dcw_ref)
        dhp_ref[...] = jnp.zeros_like(dhp_ref)

    @pl.when(k == 0)
    def _():
        ext[0:8, :] = tail_in_ref[...].astype(F32)[8:16, :]

    @pl.when(k > 0)
    def _():
        ext[0:8, :] = prev_ref[...].astype(F32)[8:16, :]

    ext[8 : 8 + q, :] = ci_ref[...].astype(F32)
    since = distances(sp, first, q + 8)
    for c in range(0, MIX, 128):
        cols = slice(c, c + 128)
        pre = conv_forward(ext, cw_ref, since[0:q], cols, q)
        sig = jax.nn.sigmoid(pre)
        act = pre * sig
        mix[:, cols] = act
        slope[:, cols] = sig + act * (1.0 - sig)

    row, col, same, shifted, stepsize, decay, cum, open_w, tail, passed = block_terms(
        sp, first, q, raw_ref[...], cw_ref
    )
    cum_t = cum.T
    keys = mix[:, WIDE : WIDE + STATE]
    kb = keys.astype(BF16)
    queries = mix[:, WIDE + STATE :]
    qb = queries.astype(BF16)
    qt = queries.T.astype(BF16)
    inside = same & (col >= row)
    scores = jnp.where(inside, split_dot(keys, queries, ABT), 0.0)
    stb, dstb = st_ref[...].astype(BF16), dstate[...].astype(BF16)
    flow[...] = dot(qb, stb, AB)
    kept_all[...] = dot(kb, dstb, AB)
    low = lax.broadcasted_iota(jnp.int32, (q, 2 * HEAD), 1) < HEAD
    lane = lax.broadcasted_iota(jnp.int32, (q, 128), 1)
    sub = lax.broadcasted_iota(jnp.int32, (16, q), 0)
    dscores = jnp.zeros((q, q), F32)
    plus_t = jnp.zeros((16, q), F32)
    dstep = jnp.zeros((q, 128), F32)
    dcum = jnp.zeros((q, 128), F32)
    for pair in range(LOCAL // 2):
        cols = pair_cols(pair)
        v = mix[:, cols]
        step_e = pair_lanes(stepsize, pair)
        vs = v * step_e
        vsb = vs.astype(BF16)
        dyb = dy_ref[:, cols]
        dyf = dyb.astype(F32)
        dvs = []
        for side, h in ((0, 2 * pair), (1, 2 * pair + 1)):
            mine = low if side == 0 else ~low
            damp = jnp.exp(jnp.minimum(cum_t[h : h + 1, :] - cum[:, h : h + 1], 0.0))
            raw = dot(jnp.where(mine, vs, 0.0).astype(BF16), dyb, ABT)
            mixing = (scores * damp).astype(BF16)
            dscores = dscores + raw * damp
            both = raw * mixing.astype(F32)
            plus_t = plus_t + jnp.where(sub == h, jnp.sum(both, axis=0, keepdims=True), 0.0)
            dvs.append(dot(mixing, dyb, AB))
        dv = jnp.where(low, dvs[0], dvs[1])
        weighted = dyf * pair_lanes(open_w, pair)
        dyw[:, cols] = weighted.astype(BF16)
        tail_e = pair_lanes(tail, pair)
        kept = kept_all[:, cols] * tail_e
        tails[:, cols] = (vs * tail_e).astype(BF16)
        u = dv + kept
        dext[0:q, cols] = (u * step_e + cw_ref[5:6, cols] * dyf) * slope[:, cols]
        from_tail = kept * vs
        dcw_ref[5:6, cols] += jnp.sum(dyf * v, axis=0, keepdims=True)
        ends[1:2, cols] = jnp.sum(from_tail, axis=0, keepdims=True)
        uv = u * v
        change = weighted * flow[:, cols] - dv * vsb.astype(F32) - from_tail
        for side, h in ((0, 2 * pair), (1, 2 * pair + 1)):
            mine = low if side == 0 else ~low

            def per_row(x):
                return jnp.sum(jnp.where(mine, x, 0.0), axis=1, keepdims=True)

            dstep = jnp.where(lane == h, per_row(uv), dstep)
            dcum = jnp.where(lane == h, per_row(change), dcum)

    dcum = dcum + jnp.concatenate([plus_t, jnp.zeros((112, q), F32)]).T
    ends[0:1, :] = jnp.sum(st_ref[...] * dstate[...], axis=0, keepdims=True)
    by_head = dot(ends[...], channel_map(), AB, HIGH)
    at_end = by_head[0:1, :] * passed + by_head[1:2, :]
    dcum = dcum + jnp.where(row == q - 1, at_end, 0.0)
    upper = jnp.where(col >= row, 1.0, 0.0)
    ddecay = dot(upper, dcum, AB, HIGH)
    draw = (dstep - ddecay * cw_ref[11:12, 0:128]) * jax.nn.sigmoid(shifted)
    dci_ref[:, MIX:] = draw.astype(BF16)
    dhp_ref[0:1, :] += jnp.sum(draw, axis=0, keepdims=True)
    dhp_ref[1:2, :] += jnp.sum(ddecay * decay, axis=0, keepdims=True)

    dsb = jnp.where(inside, dscores, 0.0).astype(BF16)
    dkeys = dot(dsb, qb, AB) + dot(tails[...], dstb, ABT)
    dqueries = dot(dsb, kb, ATB) + dot(dyw[...], stb, ABT)
    kcols, qcols = slice(WIDE, WIDE + STATE), slice(WIDE + STATE, MIX)
    dext[0:q, kcols] = dkeys * slope[:, kcols]
    dext[0:q, qcols] = dqueries * slope[:, qcols]
    update = dot(qt, dyw[...], AB)
    for pair in range(LOCAL // 2):
        cols = pair_cols(pair)
        dstate[:, cols] = dstate[:, cols] * pair_lanes(passed, pair) + update[:, cols]
    dst_out_ref[...] = dstate[...]

    for c in range(0, MIX, 128):
        cols = slice(c, c + 128)
        here = dext[0:q, cols]
        total = cw_ref[3:4, cols] * here
        dcw_ref[3:4, cols] += jnp.sum(here * ext[8 : 8 + q, cols], axis=0, keepdims=True)
        dcw_ref[4:5, cols] += jnp.sum(here, axis=0, keepdims=True)
        for shift in range(1, CONV):
            later = jnp.where(since[shift : shift + q] >= shift, dext[shift : shift + q, cols], 0.0)
            total = total + cw_ref[3 - shift : 4 - shift, cols] * later
            used = jnp.where(since[0:q] >= shift, ext[8 - shift : 8 - shift + q, cols], 0.0)
            dcw_ref[3 - shift : 4 - shift, cols] += jnp.sum(here * used, axis=0, keepdims=True)
        dci_ref[:, cols] = total.astype(BF16)
    head_rows = dext[0:8, :]
    dext[q : q + 8, :] = head_rows
    next_out_ref[...] = head_rows


def scan_back(sp, stored, seg, conv_in, step_raw, dy, states, tail, cw, dstate, following):
    tokens = conv_in.shape[0]
    q = tokens // CTX

    def here(x):
        return x, pl.BlockSpec((q, x.shape[1]), lambda i, sp: ((CTX - 1 - i) ^ sp[0], 0))

    if stored:
        conv_in, step_raw, dy, states = [far(x) for x in (conv_in, step_raw, dy, states)]
        tail, cw, dstate, following = [far(x) for x in (tail, cw, dstate, following)]

    def before(i, sp):
        return (jnp.maximum(CTX - 2 - i, 0) ^ sp[0]) * (q // 16) + q // 16 - 1, 0

    return call(
        "scan_back",
        functools.partial(scan_back_kernel, seg),
        sp,
        [
            here(conv_in),
            (conv_in, pl.BlockSpec((16, MIX), before)),
            here(step_raw),
            here(dy),
            (states, pl.BlockSpec((STATE, WIDE), lambda i, sp: (CTX - 1 - i, 0))),
            tail,
            cw,
            dstate,
            following,
        ],
        [
            here(shape((tokens, FULL), BF16)),
            shape((8, MIX), F32),
            shape((8, 128), F32),
            shape((STATE, WIDE), F32),
            shape((8, MIX), F32),
        ],
        24,
        grid=CTX,
        scratch=[
            pltpu.VMEM((q + 8, MIX), F32),
            pltpu.VMEM((q, MIX), F32),
            pltpu.VMEM((q, MIX), F32),
            pltpu.VMEM((q + 8, MIX), F32),
            pltpu.VMEM((STATE, WIDE), F32),
            pltpu.VMEM((q, WIDE), BF16),
            pltpu.VMEM((q, WIDE), BF16),
            pltpu.VMEM((q, WIDE), F32),
            pltpu.VMEM((q, WIDE), F32),
            pltpu.VMEM((8, WIDE), F32),
        ],
    )


def input_back_kernel(sp, dc_ref, dg_ref, wc_ref, wg_ref, *part_refs):
    part = dot(dc_ref[...], wc_ref[...], ABT) + dot(dg_ref[...], wg_ref[...], ABT)
    store_part(part, None, part_refs)


def input_back(sp, slots, dconv, dgate, wc, wg):
    outs = part_shapes(slots, dconv.shape[0], wc.shape[0])
    return call("input_back", input_back_kernel, sp, [dconv, dgate, wc, wg], outs, 24)


def own_back_kernel(count, sp, *refs):
    partial, rest = refs[:5], refs[5:]
    x = jnp.concatenate([v for _, v in load_rows(rest[:count])]).astype(F32)
    u = jnp.concatenate([v for _, v in load_rows(rest[count : 2 * count])]).astype(F32)
    cw_ref, branch_ref, up_ref, dnorm_ref = rest[2 * count :]
    grad = own_sum(partial)
    scale = row_scale(x)
    gained = grad * cw_ref[8:9, :]
    centre = jnp.mean(gained * x, axis=-1, keepdims=True)
    up = (u + scale * (gained - x * (scale * scale * centre))).astype(BF16)
    extra = up_ref.shape[0] - up.shape[0]
    up_ref[extra:, :] = up
    if extra:
        inner = jnp.sum(up.astype(F32) * branch_ref[...], axis=-1, keepdims=True)
        up_ref[:extra, :] = split_rows(stat_rows([inner])[0:1, :], up.shape[1])
    dnorm_ref[...] = jnp.broadcast_to(
        jnp.sum(grad * x * scale, axis=0, keepdims=True), dnorm_ref.shape
    )


def own_back(sp, extra, partial, x, u, cw, branch):
    q, d = partial[0].shape
    return call(
        "own_back",
        functools.partial(own_back_kernel, len(x)),
        sp,
        partial + x + u + [cw, branch],
        [shape((q + extra, d), BF16), shape((8, d), F32)],
    )


def head_map(group, block, flipped=False):
    here = lax.broadcasted_iota(jnp.int32, (128, 128), 1 if flipped else 0)
    there = lax.broadcasted_iota(jnp.int32, (128, 128), 0 if flipped else 1)
    turn = jnp.zeros_like(here)
    for edge in range(block, LOCAL, block):
        turn = turn + jnp.where(here >= edge, 1, 0)
    goal = here + (turn * (CTX - 1) + group) * block
    return jnp.where((here < LOCAL) & (there == goal), 1.0, 0.0)


def channel_map(flipped=False):
    dims = (128, WIDE) if flipped else (WIDE, 128)
    chan = lax.broadcasted_iota(jnp.int32, dims, 1 if flipped else 0)
    head = lax.broadcasted_iota(jnp.int32, dims, 0 if flipped else 1)
    return jnp.where((chan >= head * HEAD) & (chan < (head + 1) * HEAD), 1.0, 0.0)


def spans(group, block):
    wide = block * HEAD
    return [(z * wide, (z * CTX + group) * wide, wide) for z in range(WIDE // wide)]


def choose(first, a, b):
    return jnp.where(first, a, b)


def pack_kernel(block, sp, w_ref, *refs):
    conv_refs, gate_refs, conv, gate = refs[:CTX], refs[CTX : 2 * CTX], refs[-2], refs[-1]
    place = sp[0]
    keys = w_ref[:, 2 * INNER : 2 * INNER + STATE]
    queries = w_ref[:, 2 * INNER + STATE : 2 * INNER + 2 * STATE]
    steps = w_ref[:, 2 * INNER + 2 * STATE :]
    rows = w_ref.shape[0]
    steps = jnp.concatenate([steps, jnp.zeros((rows, 128 - HEADS), BF16)], axis=1)
    for k in range(CTX):
        values = jnp.concatenate(
            [w_ref[:, INNER + there : INNER + there + n] for _, there, n in spans(k, block)], axis=1
        )
        gates = jnp.concatenate(
            [w_ref[:, there : there + n] for _, there, n in spans(k, block)], axis=1
        )
        step = dot(steps, head_map(k, block, True).astype(BF16), AB).astype(BF16)
        conv[k] = jnp.concatenate(
            [values[:, :HALF], keys, step, values[:, HALF:], queries, step], axis=1
        )
        gate[k] = gates
    for m in range(CTX):
        conv_refs[m][...] = conv[m ^ place]
        gate_refs[m][...] = gate[m ^ place]


def pack(sp, block, w_in):
    rows = w_in.shape[0]
    outs = call(
        "pack",
        functools.partial(pack_kernel, block),
        sp,
        [w_in],
        [shape((rows, 2 * LOAD), BF16)] * CTX + [shape((rows, WIDE), BF16)] * CTX,
        16,
        scratch=[
            pltpu.VMEM((CTX, rows, 2 * LOAD), BF16),
            pltpu.VMEM((CTX, rows, WIDE), BF16),
        ],
    )
    return outs[:CTX], outs[CTX:]


def order_conv_kernel(sp, *refs):
    keep_ref, send_ref = refs[CTX:]
    zero = sp[1] == 0
    for m in range(CTX):
        low, high = refs[m][:, :LOAD], refs[m][:, LOAD:]
        keep_ref[m ^ sp[0]] = choose(zero, low, high)
        send_ref[m ^ sp[0]] = choose(zero, high, low)


def order_conv(sp, slots):
    out = shape((CTX, slots[0].shape[0], LOAD), BF16)
    return call("order_conv", order_conv_kernel, sp, slots, [out, out], 12)


def order_gate_kernel(sp, *refs):
    out_ref, keep_ref, send_ref = refs[CTX:]
    zero = sp[1] == 0
    rows = keep_ref.shape[1]
    for m in range(CTX):
        low, high = refs[m][:, :HALF], refs[m][:, HALF:]
        keep_ref[m ^ sp[0], :, :HALF] = choose(zero, low, high)
        send_ref[m ^ sp[0], :, :HALF] = choose(zero, high, low)
    for r in range(2):
        for c in range(2):
            at = slice(r * rows, (r + 1) * rows)
            low = out_ref[at, c * HALF : (c + 1) * HALF]
            high = out_ref[at, (2 + c) * HALF : (3 + c) * HALF]
            keep_ref[2 * r + c, :, HALF:] = choose(zero, low, high)
            send_ref[2 * r + c, :, HALF:] = choose(zero, high, low)


def order_gate(sp, slots, w_out):
    out = shape((CTX, slots[0].shape[0], WIDE), BF16)
    return call("order_gate", order_gate_kernel, sp, slots + [w_out], [out, out], 12)


def join_conv_kernel(sp, mine_ref, other_ref, wc_ref):
    zero = sp[1] == 0
    rows = mine_ref.shape[2]
    for i in range(CTX):
        a, b = mine_ref[0, i, :, :LOAD], other_ref[0, i, :, :LOAD]
        low, high = choose(zero, a, b), choose(zero, b, a)
        at = slice(i * rows, (i + 1) * rows)
        wc_ref[at, 0:HALF] = low[:, :HALF]
        wc_ref[at, HALF:WIDE] = high[:, :HALF]
        wc_ref[at, WIDE : WIDE + STATE] = low[:, HALF : HALF + STATE]
        wc_ref[at, WIDE + STATE : MIX] = high[:, HALF : HALF + STATE]
        wc_ref[at, MIX:] = low[:, HALF + STATE :]


def by_rows(x, count):
    return x, pl.BlockSpec((x.shape[0] // count, x.shape[1]), lambda z, sp: (z, 0))


def join_conv(sp, mine, other):
    dp, _, rows, _ = mine.shape
    out = by_rows(shape((dp * CTX * rows, FULL), BF16), dp)
    ins = [by_first(mine), by_first(other)]
    return call("join_conv", join_conv_kernel, sp, ins, [out], 12, dp)[0]


def join_gate_kernel(first, sp, mine_ref, other_ref, wg_ref, wo_ref):
    zero = sp[1] == 0
    rows = mine_ref.shape[2]
    for i in range(CTX):
        a, b = mine_ref[0, i, :, first:], other_ref[0, i, :, first:]
        low, high = choose(zero, a, b), choose(zero, b, a)
        at = slice(i * rows, (i + 1) * rows)
        wg_ref[at, :HALF] = low[:, :HALF]
        wg_ref[at, HALF:] = high[:, :HALF]
        r, c = i // 2, i % 2
        at = slice(r * rows, (r + 1) * rows)
        wo_ref[at, c * HALF : (c + 1) * HALF] = low[:, HALF:]
        wo_ref[at, (2 + c) * HALF : (3 + c) * HALF] = high[:, HALF:]


def join_gate(sp, mine, other):
    dp, _, rows, cols = mine.shape
    wg, wo = shape((dp * CTX * rows, WIDE), BF16), shape((dp * 2 * rows, 4 * HALF), BF16)
    outs = [by_rows(wg, dp), by_rows(wo, dp)]
    kernel = functools.partial(join_gate_kernel, cols - WIDE)
    ins = [by_first(mine), by_first(other)]
    return call("join_gate", kernel, sp, ins, outs, 12, dp)


def fold_kernel(sp, keep_ref, came_ref, out_ref):
    out_ref[...] = (keep_ref[...].astype(F32) + came_ref[...].astype(F32)).astype(BF16)


def fold(sp, keep, came):
    ins = [by_first(keep), by_first(came)]
    return call("fold", fold_kernel, sp, ins, [by_first(shape(keep.shape, BF16))], 24, keep.shape[0])


def total_kernel(counts, sp, *refs):
    for m in range(CTX):
        parts = [ref[m ^ sp[0], :, :cols] for ref, cols in zip(refs, counts)]
        refs[len(counts) + m][...] = jnp.concatenate(parts, axis=1)


def total_line(sp, sums):
    width = {LOAD: LOAD, WIDE: HALF}
    counts = [width[x.shape[2]] for x in sums]
    outs = [shape((sums[0].shape[1], sum(counts)), BF16)] * CTX
    sums = [far(x) for x in sums]
    return call("total_line", functools.partial(total_kernel, counts), sp, sums, outs)


def mix_kernel(cols, sp, *refs):
    out_ref = refs[-1]
    zero = sp[1] == 0
    for m in range(CTX):
        if cols == LOAD:
            mine, other = refs[CTX + m][...], refs[m][:, :LOAD]
        else:
            mine, other = refs[m][:, LOAD + HALF :], refs[m][:, LOAD : LOAD + HALF]
            out_ref[m, :, HALF:] = choose(zero, refs[CTX + 1][m, :, HALF:], refs[CTX][m, :, HALF:])
        out_ref[m, :, : mine.shape[1]] = choose(zero, other, mine)


def mix(sp, early, late, cols):
    out = shape((CTX, early[0].shape[0], cols), BF16)
    return call("mix", functools.partial(mix_kernel, cols), sp, early + late, [out])[0]


def grad_conv_kernel(sp, n0_ref, n1_ref, d0_ref, d1_ref, keep_ref, send_ref):
    zero = sp[1] == 0
    rows = keep_ref.shape[2]
    total = dot(n0_ref[...], d0_ref[...], ATB) + dot(n1_ref[...], d1_ref[...], ATB)
    total = total.astype(BF16)
    step = total[:, MIX:]
    low = jnp.concatenate([total[:, :HALF], total[:, WIDE : WIDE + STATE], step], axis=1)
    high = jnp.concatenate([total[:, HALF:WIDE], total[:, WIDE + STATE : MIX], step], axis=1)
    keep, send = choose(zero, low, high), choose(zero, high, low)
    for i in range(CTX):
        keep_ref[0, i] = keep[i * rows : (i + 1) * rows]
        send_ref[0, i] = send[i * rows : (i + 1) * rows]


def by_first(x):
    rest = (0,) * (len(x.shape) - 1)
    return x, pl.BlockSpec((1,) + tuple(x.shape[1:]), lambda z, sp: (z,) + rest)


def by_cols(x, count):
    return x, pl.BlockSpec((x.shape[0], x.shape[1] // count), lambda z, sp: (0, z))


def grad_conv(sp, dp, rows, normed, dconv):
    out = shape((dp, CTX, rows, LOAD), BF16)
    return call(
        "grad_conv",
        grad_conv_kernel,
        sp,
        [by_cols(x, dp) for x in normed] + list(dconv),
        [by_first(out), by_first(out)],
        24,
        dp,
    )


def grad_gate_kernel(sp, *refs):
    n_refs, dg_refs, gated_refs, u_refs = refs[0:2], refs[2:4], refs[4:6], refs[6:8]
    keep_ref, send_ref = refs[8:]
    z = pl.program_id(0)
    dp, _, rows, _ = keep_ref.shape
    zero = sp[1] == 0

    def over_tokens(a, b):
        return dot(a[0][...], b[0][...], ATB) + dot(a[1][...], b[1][...], ATB)

    total = over_tokens(n_refs, dg_refs).astype(BF16)
    keep = choose(zero, total[:, :HALF], total[:, HALF:])
    send = choose(zero, total[:, HALF:], total[:, :HALF])
    for i in range(CTX):
        keep_ref[z, i, :, :HALF] = keep[i * rows : (i + 1) * rows]
        send_ref[z, i, :, :HALF] = send[i * rows : (i + 1) * rows]
    total = over_tokens(gated_refs, u_refs).astype(BF16)
    side, c = z // 2, lax.rem(z, 2)

    def put(ref):
        for there in range(dp):
            for r in range(2):
                first = (2 * there + r) * rows
                ref[there, 2 * r + c, :, HALF:] = total[first : first + rows]

    @pl.when(side == sp[1])
    def _():
        put(keep_ref)

    @pl.when(side != sp[1])
    def _():
        put(send_ref)


def grad_gate(sp, dp, rows, normed, dgate, gated, u):
    out = shape((dp, CTX, rows, WIDE), BF16)
    return call(
        "grad_gate",
        grad_gate_kernel,
        sp,
        [by_cols(x, dp) for x in normed]
        + list(dgate)
        + list(gated)
        + [by_cols(x, dp) for x in u],
        [out, out],
        32,
        dp,
    )


def finish_kernel(block, sp, *refs):
    early, late, (gate0, gate1, came_gate, came_conv) = refs[:4], refs[4:8], refs[8:12]
    in_ref, out_ref, lows, highs, glows, ghighs = refs[12:]
    place, zero = sp[0], sp[1] == 0
    rows = in_ref.shape[0]
    for m in range(CTX):
        mine, came = choose(zero, late[m][...], early[m][:, :LOAD]), came_conv[m]
        lows[m ^ place] = choose(zero, mine, came).astype(F32)
        highs[m ^ place] = choose(zero, came, mine).astype(F32)
        mine = choose(zero, early[m][:, LOAD + HALF :], early[m][:, LOAD : LOAD + HALF])
        came = came_gate[m, :, :HALF]
        glows[m ^ place] = choose(zero, mine, came).astype(F32)
        ghighs[m ^ place] = choose(zero, came, mine).astype(F32)
    keys, queries, steps = 0.0, 0.0, 0.0
    for k in range(CTX):
        keys = keys + lows[k, :, HALF : HALF + STATE]
        queries = queries + highs[k, :, HALF : HALF + STATE]
        steps = steps + dot(lows[k, :, HALF + STATE :], head_map(k, block), AB, HIGH)
    for z in range(WIDE // (block * HEAD)):
        def side_by_side(a, b):
            parts = []
            for k in range(CTX):
                here, _, n = spans(k, block)[z]
                source = a if here < HALF else b
                parts.append(source[k, :, here % HALF : here % HALF + n])
            return jnp.concatenate(parts, axis=1)

        wide = CTX * block * HEAD
        in_ref[:, z * wide : (z + 1) * wide] = side_by_side(glows, ghighs)
        in_ref[:, INNER + z * wide : INNER + (z + 1) * wide] = side_by_side(lows, highs)
    in_ref[:, 2 * INNER : 2 * INNER + STATE] = keys
    in_ref[:, 2 * INNER + STATE : 2 * INNER + 2 * STATE] = queries
    in_ref[:, 2 * INNER + 2 * STATE :] = steps[:, :HEADS]
    for i in range(4):
        r, c = i // 2, i % 2
        mine, came = choose(zero, gate0[i, :, HALF:], gate1[i, :, HALF:]), came_gate[i, :, HALF:]
        at = slice(r * rows, (r + 1) * rows)
        out_ref[at, c * HALF : (c + 1) * HALF] = choose(zero, mine, came).astype(F32)
        out_ref[at, (2 + c) * HALF : (3 + c) * HALF] = choose(zero, came, mine).astype(F32)


def finish(sp, block, early, late, gates, came_gate, came_conv):
    rows = came_conv.shape[1]
    return call(
        "finish",
        functools.partial(finish_kernel, block),
        sp,
        early + late + gates + [came_gate, came_conv],
        [shape((rows, 2 * INNER + 2 * STATE + HEADS), F32), shape((2 * rows, 4 * HALF), F32)],
        24,
        scratch=[pltpu.VMEM((CTX, rows, LOAD), F32)] * 2 + [pltpu.VMEM((CTX, rows, HALF), F32)] * 2,
    )


class Direct:
    def __init__(self, order, mine, dp, block, w_in, w_out):
        self.order, self.mine, self.dp, self.block = order, mine, dp, block
        self.rows = w_in.shape[0]
        conv, gate = order(pack, block, w_in)
        conv = order(order_conv, [flip(x, m) if m else x for m, x in enumerate(conv)])
        self.conv = self.trade(*conv)
        self.first = self.gathered(self.conv[0])
        gate = [order.now(x) for x in gate]
        self.slots = [flip(x, m) if m else x for m, x in enumerate(gate)]
        self.w_out = w_out

    def prepare_gate(self):
        self.gate = self.trade(*self.order(order_gate, self.slots, self.w_out))

    def trade(self, keep, send):
        came = swap_core(send)
        return choose(self.mine == 0, keep, came), choose(self.mine == 0, came, keep)

    def gathered(self, x):
        return lax.all_gather(x, "dp", axis=0)

    def start_conv(self):
        return self.first

    def start_gate(self, after):
        x, _ = lax.optimization_barrier((self.order.now(self.gate[0]), after))
        return self.gathered(x)

    def start_second(self):
        return self.gathered(self.order.now(self.conv[1])), self.gathered(self.order.now(self.gate[1]))

    def trade_weights(self, x):
        x = self.order.now(x)
        return x, swap_core(x)

    def conv_weights(self, sp, both):
        return join_conv(sp, *both)

    def gate_weights(self, sp, both):
        return join_gate(sp, *both)

    def grad_gate(self, sp, layer, normed, dgate, gated, u):
        return grad_gate(sp, self.dp, self.rows, normed, dgate, gated, u)

    def grad_conv(self, sp, layer, normed, dconv):
        return grad_conv(sp, self.dp, self.rows, normed, dconv)

    def trade_grads(self, grads):
        return grads[0], swap_core(grads[1])

    def send(self, traded):
        (total,) = self.order(fold, *traded)
        return lax.psum_scatter(total, "dp", scatter_dimension=0, tiled=True)[0]

    def early(self, conv1, gate1, gate0):
        self.gates = [gate0, gate1]
        slots = self.order(total_line, [conv1, gate1, gate0])
        self.slots = [flip(x, m) if m else x for m, x in enumerate(slots)]

    def early_trade(self):
        self.came = swap_core(self.order(mix, self.slots, self.gates, WIDE))

    def late(self, conv0):
        late = self.order(total_line, [conv0])
        self.last = [flip(x, m) if m else x for m, x in enumerate(late)]

    def late_trade(self):
        self.last_came = swap_core(self.order(mix, self.slots, self.last, LOAD))

    def gradients(self):
        arrays = self.slots, self.last, self.gates, self.came, self.last_came
        return self.order(finish, self.block, *arrays)


def grouped(columns, block):
    lead = columns.shape[:-1]
    split = jnp.moveaxis(columns.reshape(lead + (-1, CTX, block)), -2, 0)
    return split.reshape((CTX,) + lead + (-1,))


def ungrouped(groups, block):
    lead = groups.shape[1:-1]
    split = groups.reshape((CTX,) + lead + (-1, block))
    return jnp.moveaxis(split, 0, -2).reshape(lead + (-1,))


def pad_to(x, rows, cols):
    room = [(0, 0)] * (x.ndim - 2) + [(0, rows - x.shape[-2]), (0, cols - x.shape[-1])]
    return jnp.pad(x, room)


class Plain:
    def __init__(self, mine, place, block, w_in, w_out):
        self.mine, self.place, self.block = mine, place, block
        full_in = lax.all_gather(w_in, ("dp", "ctx"), axis=0, tiled=True)
        full_out = lax.all_gather(w_out, ("dp", "ctx"), axis=0, tiled=True)
        self.full = [(full_in, full_out), (swap_core(full_in), swap_core(full_out))]
        self.grads = [{}, {}]

    def prepare_gate(self):
        pass

    def start_conv(self):
        return 0

    def start_gate(self, after):
        return 0

    def start_second(self):
        return 1, 1

    def trade_weights(self, layer):
        return layer

    def trade_grads(self, grads):
        return grads

    def send(self, traded):
        return traded

    def early(self, conv1, gate1, gate0):
        pass

    def early_trade(self):
        pass

    def late(self, conv0):
        pass

    def late_trade(self):
        pass

    def group(self, columns, block):
        return lax.dynamic_index_in_dim(grouped(columns, block), self.place, 0, False)

    def layer(self, layer, which):
        return choose(self.mine == layer, self.full[0][which], self.full[1][which])

    def conv_weights(self, sp, layer):
        one = self.layer(layer, 0)
        values = self.group(one[:, INNER : 2 * INNER], self.block * HEAD)
        step = self.group(one[:, 2 * INNER + 2 * STATE :], self.block)
        shared = one[:, 2 * INNER : 2 * INNER + 2 * STATE]
        return jnp.concatenate([values, shared, pad_to(step, step.shape[0], 128)], 1)

    def gate_weights(self, sp, layer):
        one, out = self.layer(layer, 0), self.layer(layer, 1)
        wide = self.block * HEAD
        return self.group(one[:, :INNER], wide), self.group(out.T, wide).T

    def over_tokens(self, a, b):
        both = [dot(x, y, ATB) for x, y in zip(a, b)]
        return (both[0] + both[1]).astype(BF16)

    def grad_gate(self, sp, layer, normed, dgate, gated, u):
        out = self.over_tokens(gated, u)
        self.grads[layer].update(gate=self.over_tokens(normed, dgate), out=out)
        return [out]

    def grad_conv(self, sp, layer, normed, dconv):
        self.grads[layer].update(conv=self.over_tokens(normed, dconv))
        return [self.grads[layer]["conv"]]

    def spread(self, columns, block):
        at = lax.broadcasted_iota(jnp.int32, (CTX, 1, 1), 0) == self.place
        return ungrouped(jnp.where(at, columns[None], jnp.zeros((), columns.dtype)), block)

    def gradients(self):
        wide = self.block * HEAD
        fulls = []
        for grads in self.grads:
            gate, conv = grads["gate"], grads["conv"]
            grad_in = jnp.concatenate(
                [
                    self.spread(gate, wide),
                    self.spread(conv[:, :WIDE], wide),
                    conv[:, WIDE:MIX],
                    self.spread(conv[:, MIX : MIX + LOCAL], self.block),
                ],
                -1,
            )
            fulls.append((grad_in, self.spread(grads["out"].T, wide).T))
        sums = []
        for a, b in zip(*fulls):
            zero = self.mine == 0
            total = choose(zero, a, b).astype(F32) + swap_core(choose(zero, b, a)).astype(F32)
            total = total.astype(BF16)
            sums.append(
                lax.psum_scatter(total, ("dp", "ctx"), scatter_dimension=0, tiled=True).astype(F32)
            )
        return sums[0], sums[1]


def prepare_kernel(block, sp, norm_ref, taps_ref, bias_ref, dt_ref, log_ref, skip_ref, gain_ref, out_ref):
    out_ref[...] = jnp.zeros_like(out_ref)
    for k in range(CTX):

        @pl.when(sp[0] == k)
        def _():
            for here, there, n in spans(k, block):
                out_ref[0:CONV, here : here + n] = taps_ref[0, :, there : there + n]
                out_ref[4:5, here : here + n] = bias_ref[:, there : there + n]
                out_ref[9:10, here : here + n] = gain_ref[:, there : there + n]
            spare = jnp.zeros((1, 128 - HEADS), F32)
            rows = [jnp.concatenate([ref[...], spare], axis=1) for ref in (dt_ref, log_ref, skip_ref)]
            rows = jnp.concatenate(rows + [jnp.zeros((5, 128), F32)])
            local = dot(rows, head_map(k, block, True), AB, HIGH)
            out_ref[10:11, 0:128] = local[0:1, :]
            out_ref[11:12, 0:128] = jnp.exp(local[1:2, :])
            out_ref[5:6, :WIDE] = dot(local, channel_map(True), AB, HIGH)[2:3, :]

    out_ref[0:CONV, WIDE:MIX] = taps_ref[0, :, INNER:]
    out_ref[4:5, WIDE:MIX] = bias_ref[:, INNER:]
    out_ref[8:9, :] = norm_ref[...]


def prepare(sp, block, arrays):
    out = shape((16, arrays[0].shape[1]), F32)
    return call("prepare", functools.partial(prepare_kernel, block), sp, arrays, [out], 12)[0]


def gather_small_kernel(counts, sp, *refs):
    keep_ref, send_ref = refs[-2:]
    packed, at = [], 0
    for layer in range(2):
        sums = []
        for count in counts[layer]:
            sums.append(sum(ref[...] for ref in refs[at : at + count]))
            at += count
        dcw, dhp, dgain, dnorm = sums
        tall = lax.broadcasted_iota(jnp.int32, (8, MIX), 0)
        gain = jnp.concatenate([dgain, jnp.zeros((8, MIX - WIDE), F32)], axis=1)
        short = dnorm.shape[1] - MIX
        norm_rest = jnp.concatenate([dnorm[:, MIX:], jnp.zeros((8, MIX - short), F32)], axis=1)
        middle = jnp.where(tall == 0, gain, jnp.where(tall == 1, dnorm[:, :MIX], norm_rest))
        heads = jnp.concatenate([dhp, jnp.zeros((8, MIX - 128), F32)], axis=1)
        packed.append(jnp.concatenate([dcw, middle, heads]))
    zero = sp[1] == 0
    keep_ref[...] = choose(zero, packed[0], packed[1])
    send_ref[...] = choose(zero, packed[1], packed[0])


def gather_small(sp, small):
    counts = [[len(kind) for kind in layer] for layer in small]
    arrays = [x for layer in small for kind in layer for x in kind]
    out = shape((PACK, MIX), F32)
    kernel = functools.partial(gather_small_kernel, counts)
    return call("gather_small", kernel, sp, arrays, [out, out], 12)


def spread_small_kernel(block, sp, *refs):
    slots, all_slots = refs[:CTX], refs[-1]
    norm_ref, taps_ref, bias_ref, dt_ref, log_ref, skip_ref, gain_ref = refs[CTX:-1]
    for m in range(CTX):
        all_slots[m ^ sp[0]] = slots[m][...]
    total = sum(all_slots[k] for k in range(CTX))
    norm_ref[:, :MIX] = total[9:10, :]
    norm_ref[:, MIX:] = total[10:11, : norm_ref.shape[1] - MIX]
    taps_ref[0, :, INNER:] = total[0:CONV, WIDE:]
    bias_ref[:, INNER:] = total[4:5, WIDE:]
    pick = channel_map()
    heads = 0.0
    for k in range(CTX):
        for here, there, n in spans(k, block):
            taps_ref[0, :, there : there + n] = all_slots[k, 0:CONV, here : here + n]
            bias_ref[:, there : there + n] = all_slots[k, 4:5, here : here + n]
            gain_ref[:, there : there + n] = all_slots[k, 8:9, here : here + n]
        skip = dot(all_slots[k, 0:8, :WIDE], pick, AB, HIGH)
        both = jnp.concatenate([all_slots[k, 16:24, :128], skip])
        heads = heads + dot(both, head_map(k, block), AB, HIGH)
    dt_ref[...] = heads[0:1, :HEADS]
    log_ref[...] = heads[1:2, :HEADS]
    skip_ref[...] = heads[13:14, :HEADS]


def spread_small(sp, block, slots, d):
    one = shape((1, HEADS), F32)
    return call(
        "spread_small",
        functools.partial(spread_small_kernel, block),
        sp,
        slots,
        [
            shape((1, d), F32),
            shape((1, CONV, CONV_DIM), F32),
            shape((1, CONV_DIM), F32),
            one,
            one,
            one,
            shape((1, INNER), F32),
        ],
        12,
        scratch=[pltpu.VMEM((CTX, PACK, MIX), F32)],
    )


def sum_over_dp(x, dp, step, end):
    if dp & (dp - 1):
        return lax.psum(x, "dp") if step == 1 else x
    while step < end:
        x = x + lax.ppermute(x, "dp", [(i, i ^ step) for i in range(dp)])
        step *= 2
    return x


class Order:
    def __init__(self, sp):
        self.sp = sp

    def __call__(self, kernel, *args):
        out = kernel(self.sp, *args)
        self.after(out[0] if isinstance(out, (list, tuple)) else out)
        return out

    def after(self, x):
        self.sp, _ = lax.optimization_barrier((self.sp, x))

    def now(self, x):
        return lax.optimization_barrier((x, self.sp))[0]


def shards(
    tokens,
    cotangent,
    doc_lengths,
    norm_gain,
    w_in,
    conv_weight,
    conv_bias,
    dt_bias,
    a_log,
    d_skip,
    inner_gain,
    w_out,
):
    mine, place = lax.axis_index("section"), lax.axis_index("ctx")
    dp = lax.axis_size("dp")
    piece, d = tokens.shape[2], tokens.shape[3]
    seg_len = piece * CTX // SEGS
    direct = dp == 4 and w_out.shape[1] % HEAD == 0 and w_out.shape[1] * dp == WIDE
    block = w_out.shape[1] // HEAD if direct else LOCAL

    own_x = lax.dynamic_index_in_dim(tokens, mine, 0, False)[0]
    own_u = lax.dynamic_index_in_dim(cotangent, mine, 0, False)[0]
    lengths = lax.dynamic_index_in_dim(doc_lengths, mine, 0, False)[0]
    start = jnp.stack([place, mine, lax.axis_index("dp")]).astype(jnp.int32)
    sp = jnp.concatenate([start, jnp.cumsum(lengths) - lengths])
    run = Order(sp)
    if direct:
        carrier = Direct(run, mine, dp, block, w_in[0], w_out[0])
    else:
        carrier = Plain(mine, place, block, w_in[0], w_out[0])

    def natural(slots):
        return jnp.concatenate(slots).reshape(CTX, 2, piece // 2, d)

    rows_x = gather_slots(run, run.now(own_x))
    arrays = [norm_gain, conv_weight, conv_bias, dt_bias, a_log, d_skip, inner_gain]
    params = run(prepare, block, arrays)
    other = swap_core(params)
    params = [choose(mine == 0, params, other), choose(mine == 0, other, params)]
    carrier.prepare_gate()
    rows_x = natural(rows_x())
    conv0 = carrier.start_conv()
    run.after(rows_x)
    gate0 = carrier.start_gate(conv0)
    conv0 = carrier.trade_weights(conv0)
    rows_u = gather_slots(run, run.now(own_u))
    no_state, no_tail = jnp.zeros((STATE, WIDE), F32), jnp.zeros((16, MIX), BF16)

    def forward(layer, s, pieces, wc, state, tail, between=None):
        normed, conv_in, step_raw = run(project, pieces, params[layer], wc, seg_len)
        if between is not None:
            between()
        y, states, state, next_tail = run(
            scan_rows, s, conv_in, step_raw, params[layer], state, tail
        )
        return dict(
            normed=normed, conv_in=conv_in, step_raw=step_raw, y=y, states=states, tail=tail
        ), state, next_tail

    wc0 = run(carrier.conv_weights, conv0)
    conv1, gate1 = carrier.start_second()
    first, second = [None, None], [None, None]
    state, tail = no_state, no_tail
    first[0], state, tail = forward(0, 0, natural_slots(rows_x, 0), wc0, state, tail)
    first[1], state, tail = forward(0, 1, natural_slots(rows_x, 1), wc0, state, tail)
    rows_u = rows_u()
    gate0 = carrier.trade_weights(gate0)
    wg0, wo0 = run(carrier.gate_weights, gate0)
    stats, sums = [None, None], [None, None]
    for s in range(SEGS):
        saved = first[s]
        saved["gate"], stats[s], *sums[s] = run(
            out_rows, True, [], [], saved["normed"], saved["y"], params[0], wg0, wo0
        )
        if s == 0:
            sums[0] = scatter_start(*sums[0])

    def own_step(s):
        residual = natural_slots(rows_x, s)[:1]
        first[s]["stats"] = [stats[s]] + [tail_tile(x) for x in sums[s][1:4]]
        own, first[s]["branch"] = run(own_rows, False, first[s]["stats"], sums[s], residual)
        first[s]["own"] = own
        return gather_slots(run, own)

    sums[0] = scatter_slots(run, *sums[0])
    sums[1] = scatter_start(*[run.now(x) for x in sums[1]])
    middle = [own_step(0), None]
    sums[1] = scatter_slots(run, *sums[1])
    middle[0] = middle[0]()
    rows_u = natural(rows_u)
    run.after(rows_u)

    conv1 = carrier.trade_weights(conv1)
    wc1 = run(carrier.conv_weights, conv1)
    middle[1] = own_step(1)
    state, tail = no_state, no_tail
    parts, before = [], []

    def last_rows():
        middle[1] = middle[1]()

    for s in range(SEGS):
        between = last_rows if s == 0 else None
        second[s], state, tail = forward(1, s, middle[s], wc1, state, tail, between)
        if s == 0:
            run.after(middle[1][3:])
            gate1 = carrier.trade_weights(gate1)
    wg1, wo1 = run(carrier.gate_weights, gate1)
    for s in range(SEGS):
        saved = second[s]
        saved["gate"], stats, part = run(
            out_rows,
            False,
            before,
            natural_slots(rows_u, s),
            saved["normed"],
            saved["y"],
            params[1],
            wg1,
            wo1,
        )
        before = [stats]
        parts.append(part)
    stats = from_all(stats)
    part1 = run(collect, parts)
    hidden0 = run(natural_rows, middle)

    def gate_step(layer, s, saved, pieces, stats, first_stat, inners, wo):
        out = run(
            gate_back, pieces, stats, first_stat, inners, saved["y"], saved["gate"], params[layer], wo
        )
        saved.update(zip(("dy", "dgate", "gated", "u", "dgain"), out))

    def scan_step(layer, s, saved, dstate, later):
        saved["dconv"], saved["dcw"], saved["dhp"], dstate, later = run(
            scan_back,
            layer == 0,
            s,
            saved["conv_in"],
            saved["step_raw"],
            saved["dy"],
            saved["states"],
            saved["tail"],
            params[layer],
            dstate,
            later,
        )
        return dstate, later

    def of(saved, *names):
        return [[one[name] for one in saved] for name in names]

    def back_start(s):
        saved = second[s]
        return scatter_start(*run(input_back, True, saved["dconv"], saved["dgate"], wc1, wg1))

    def back_end(s, part):
        up, second[s]["dnorm"] = run(
            own_back,
            16,
            part,
            [far(first[s]["own"])],
            natural_slots(rows_u, s)[:1],
            params[1],
            far(first[s]["branch"]),
        )
        return gather_slots(run, up, 16)

    upper = [None, None]

    def lower_gate(s):
        inners = [head_tile(x) for x in upper[s][:4]]
        gate_step(0, s, first[s], upper[s], first[s]["stats"], 0, inners, wo0)

    for s in (1, 0):
        gate_step(1, s, second[s], natural_slots(rows_u, s), stats, 8 * s, [], wo1)
    gate1 = carrier.trade_grads(run(carrier.grad_gate, 1, *of(second, "normed", "dgate", "gated", "u")))
    part1 = scatter_start(*part1)
    dstate, later = no_state, jnp.zeros((8, MIX), F32)
    dstate, later = scan_step(1, 1, second[1], dstate, later)
    part1 = scatter_slots(run, *part1)
    gate1 = carrier.send(gate1)
    upper[1] = back_start(1)
    dstate, later = scan_step(1, 0, second[0], dstate, later)
    hidden1, _ = run(own_rows, True, stats, part1, [hidden0])
    upper[1] = scatter_slots(run, *upper[1])
    upper[0] = back_start(0)
    upper[1] = back_end(1, upper[1])
    conv1 = run(carrier.grad_conv, 1, *of(second, "normed", "dconv"))
    upper[1] = upper[1]()
    upper[0] = scatter_slots(run, *upper[0])
    conv1 = carrier.trade_grads([run.now(x) for x in conv1])
    lower_gate(1)
    conv1 = carrier.send(conv1)
    upper[0] = back_end(0, upper[0])
    dstate, later = no_state, jnp.zeros((8, MIX), F32)
    dstate, later = scan_step(0, 1, first[1], dstate, later)
    upper[0] = upper[0]()
    (part_1,) = run(input_back, False, first[1]["dconv"], first[1]["dgate"], wc0, wg0)
    lower_gate(0)
    gate0 = carrier.trade_grads(run(carrier.grad_gate, 0, *of(first, "normed", "dgate", "gated", "u")))
    grads1 = run(natural_rows, upper, 16)
    gate0 = carrier.send(gate0)
    dstate, later = scan_step(0, 0, first[0], dstate, later)
    conv0 = carrier.trade_grads(run(carrier.grad_conv, 0, *of(first, "normed", "dconv")))
    (part_0,) = run(input_back, False, first[0]["dconv"], first[0]["dgate"], wc0, wg0)
    conv0 = carrier.send(conv0)
    part = scatter_start(*run(collect, [far(part_0), far(part_1)]))
    part = scatter_slots(run, *part)
    carrier.early(conv1, gate1, gate0)
    branch = jnp.zeros((piece, d), F32)
    grads0, dnorm0 = run(own_back, 0, part, [own_x], [grads1], params[0], branch)
    carrier.early_trade()
    small = [
        of(first, "dcw", "dhp", "dgain") + [[dnorm0]],
        of(second, "dcw", "dhp", "dgain", "dnorm"),
    ]
    keep, small_sent = run(gather_small, small)
    total = sum_over_dp(keep + swap_core(small_sent), dp, 1, dp)
    carrier.late(conv0)
    carrier.late_trade()
    total = from_all(run.now(total))
    shard_in, shard_out = carrier.gradients()
    norm, taps, bias, dt, log, skip, gain = run(spread_small, block, total, d)

    def to_layers(a, b):
        here, there = choose(mine == 0, a, b), swap_core(choose(mine == 0, b, a))
        both = jnp.stack([choose(mine == 0, here, there), choose(mine == 0, there, here)])
        return both[None, :, None]

    return (
        to_layers(hidden0, hidden1),
        to_layers(grads0, grads1),
        norm,
        shard_in[None],
        taps,
        bias,
        dt,
        log,
        skip,
        gain,
        shard_out[None],
    )


def solution(mesh):
    in_specs = (
        P(None, "dp", "ctx", None),
        P(None, "dp", "ctx", None),
        P(None, "dp", None),
        P("section", None),
        P("section", ("dp", "ctx"), None),
        P("section", None, None),
        P("section", None),
        P("section", None),
        P("section", None),
        P("section", None),
        P("section", None),
        P("section", ("dp", "ctx"), None),
    )
    out_specs = (
        P("section", None, "dp", "ctx", None),
        P("section", None, "dp", "ctx", None),
        P("section", None),
        P("section", ("dp", "ctx"), None),
        P("section", None, None),
        P("section", None),
        P("section", None),
        P("section", None),
        P("section", None),
        P("section", None),
        P("section", ("dp", "ctx"), None),
    )
    return jax.shard_map(shards, mesh=mesh, in_specs=in_specs, out_specs=out_specs, check_vma=False)
```

```python
import functools

import jax
import jax.numpy as jnp
from jax import lax
from jax.experimental import pallas as pl
from jax.experimental.pallas import tpu as pltpu
from jax.sharding import PartitionSpec as P

HEADS = 48
HEAD = 64
STATE = 128
CONV = 4
INNER = 3072
CONV_DIM = 3328
NORM_EPS = 1e-05

F32 = jnp.float32
BF16 = jnp.bfloat16
HIGH = lax.Precision.HIGHEST
CTX = 4
SEGS = 2
LOCAL = HEADS // CTX
WIDE = LOCAL * HEAD
MIX = WIDE + 2 * STATE
FULL = MIX + 128
HALF = WIDE // 2
LOAD = HALF + STATE + 128
PACK = 24
MIB = 1024 * 1024
MICROS = {
    "project": 3,
    "scan_rows": 8,
    "out_rows": 4,
    "gate_back": 3,
    "scan_back": 16,
    "input_back": 4,
    "grad_gate": 8,
    "grad_conv": 6,
}


def swap_core(x):
    return lax.ppermute(x, "section", [(0, 1), (1, 0)])


def flip(x, bits):
    return lax.ppermute(x, "ctx", [(i, i ^ bits) for i in range(CTX)])


def gather_slots(order, own, extra=0):
    half = (own.shape[0] - extra) // 2
    x, y = flip(own, 1), flip(own, 2)

    def forward():
        order.after((x, y))
        first, second = order.now(y[: extra + half]), order.now(x[extra + half :])
        return [own, x, y, flip(first, 1), flip(second, 2)]

    return forward


def scatter_start(own, to_x, to_y, late_x, late_y):
    return own, flip(to_x, 1), flip(to_y, 2), late_x, late_y


def scatter_slots(order, own, from_x, from_y, late_x, late_y):
    extra = from_x.shape[0] - 2 * late_x.shape[0]
    outs = [shape((late_x.shape[0] + extra, late_x.shape[1]), BF16), late_y]
    late_x, late_y = order(call_with("turn", turn_kernel, [from_x, from_y, late_x, late_y], outs))
    return [own, from_x, from_y, flip(late_x, 1), flip(late_y, 2)]


def from_all(x):
    return [x] + [flip(x, m) for m in range(1, CTX)]


def dot(a, b, dims, precision=None):
    return lax.dot_general(a, b, (dims, ((), ())), precision=precision, preferred_element_type=F32)


AB = ((1,), (0,))
ABT = ((1,), (1,))
ATB = ((0,), (0,))


def far(x):
    return pltpu.with_memory_space_constraint(x, pltpu.HBM)


def call_with(name, kernel, ins, outs):
    return lambda sp: call(name, kernel, sp, ins, outs)


def split_dot(a, b, dims):
    a_high, b_high = a.astype(BF16), b.astype(BF16)
    a_low = (a - a_high.astype(F32)).astype(BF16)
    b_low = (b - b_high.astype(F32)).astype(BF16)
    return dot(a_high, b_high, dims) + dot(a_low, b_high, dims) + dot(a_high, b_low, dims)


def whole(x):
    zeros = (0,) * len(x.shape)
    return pl.BlockSpec(tuple(x.shape), lambda i, sp: zeros)


def shape(dims, dtype):
    return jax.ShapeDtypeStruct(dims, dtype)


def call(name, kernel, sp, ins, outs, vmem=20, grid=1, scratch=()):
    ins = [x if isinstance(x, tuple) else (x, whole(x)) for x in ins]
    outs = [x if isinstance(x, tuple) else (x, whole(x)) for x in outs]
    return pl.pallas_call(
        kernel,
        grid_spec=pltpu.PrefetchScalarGridSpec(
            num_scalar_prefetch=1,
            grid=(grid,),
            in_specs=[spec for _, spec in ins],
            out_specs=[spec for _, spec in outs],
            scratch_shapes=list(scratch),
        ),
        out_shape=[x for x, _ in outs],
        compiler_params=pltpu.CompilerParams(
            dimension_semantics=("arbitrary",), vmem_limit_bytes=vmem * MIB
        ),
        cost_estimate=pl.CostEstimate(
            flops=int(MICROS.get(name, 1) * 1e9), bytes_accessed=1, transcendentals=0
        ),
        name=name,
    )(sp, *[x for x, _ in ins])


def natural_spec(x, seg, slot):
    def at(i, sp):
        inside = slot ^ sp[0]
        return (2 * seg + (inside >> 1)) ^ sp[0], inside & 1, 0, 0

    return pl.BlockSpec((1, 1) + x.shape[2:], at)


def natural_slots(x, seg):
    x = far(x)
    return [(x, natural_spec(x, seg, m)) for m in range(CTX)]


def load_rows(refs, extra=0):
    first = 0
    for n, ref in enumerate(refs):
        value = ref[...]
        value = value.reshape(value.shape[-2:])
        if extra and n < 4:
            value = value[extra:]
        yield first, value
        first += value.shape[0]


def row_scale(x):
    return lax.rsqrt(jnp.mean(x * x, axis=-1, keepdims=True) + NORM_EPS)


def project_kernel(count, sp, *refs):
    cw_ref, wc_ref, normed_ref, conv_ref, step_ref = refs[count:]
    gain = cw_ref[8:9, :]
    for first, x in load_rows(refs[:count]):
        x = x.astype(F32)
        rows = pl.ds(first, x.shape[0])
        normed_ref[rows, :] = (x * row_scale(x) * gain).astype(BF16)
    normed = normed_ref[...]
    conv_ref[...] = dot(normed, wc_ref[:, :MIX], AB).astype(BF16)
    step_ref[...] = dot(normed, wc_ref[:, MIX:], AB)


def project(sp, pieces, cw, wc, tokens):
    return call(
        "project",
        functools.partial(project_kernel, len(pieces)),
        sp,
        pieces + [cw, wc],
        [
            shape((tokens, wc.shape[0]), BF16),
            shape((tokens, MIX), BF16),
            shape((tokens, 128), F32),
        ],
    )


def bounds_of(sp):
    return [sp[3 + d] for d in range(sp.shape[0] - 3)]


def distances(sp, first, rows):
    at = lax.broadcasted_iota(jnp.int32, (rows, 1), 0) + first
    since = at
    for bound in bounds_of(sp):
        gap = at - bound
        since = jnp.where(gap >= 0, jnp.minimum(since, gap), since)
    return since


def segment(sp, at):
    total = jnp.zeros_like(at)
    for bound in bounds_of(sp):
        total = total + jnp.where(at >= bound, 1, 0)
    return total


def pair_lanes(a, pair):
    rows = a.shape[0]
    low = lax.broadcasted_iota(jnp.int32, (rows, 2 * HEAD), 1) < HEAD
    first = jnp.broadcast_to(a[:, 2 * pair : 2 * pair + 1], (rows, 2 * HEAD))
    second = jnp.broadcast_to(a[:, 2 * pair + 1 : 2 * pair + 2], (rows, 2 * HEAD))
    return jnp.where(low, first, second)


def conv_forward(ext, cw_ref, since, cols, q):
    total = cw_ref[4:5, cols] + cw_ref[3:4, cols] * ext[8 : 8 + q, cols]
    for shift in range(1, CONV):
        tap = cw_ref[3 - shift : 4 - shift, cols]
        rows = ext[8 - shift : 8 - shift + q, cols]
        total = total + jnp.where(since >= shift, tap * rows, 0.0)
    return total


def block_terms(sp, first, q, raw, cw_ref):
    row = lax.broadcasted_iota(jnp.int32, (q, 1), 0)
    col = lax.broadcasted_iota(jnp.int32, (1, q), 1)
    seg_col, seg_row = segment(sp, row + first), segment(sp, col + first)
    seg_before, seg_last = jnp.int32(0), jnp.int32(0)
    for bound in bounds_of(sp):
        seg_before = seg_before + jnp.where(first - 1 >= bound, 1, 0)
        seg_last = seg_last + jnp.where(first + q - 1 >= bound, 1, 0)
    same = seg_col == seg_row
    shifted = raw + cw_ref[10:11, 0:128]
    stepsize = jax.nn.softplus(shifted)
    decay = -stepsize * cw_ref[11:12, 0:128]
    lower = jnp.where(row >= col, 1.0, 0.0)
    cum = dot(lower, decay, AB, HIGH)
    last = cum[q - 1 : q, :]
    open_w = jnp.where(seg_col == seg_before, jnp.exp(cum), 0.0)
    tail = jnp.where(seg_col == seg_last, jnp.exp(jnp.minimum(last - cum, 0.0)), 0.0)
    passed = jnp.where(seg_last == seg_before, jnp.exp(last), 0.0)
    return row, col, same, shifted, stepsize, decay, cum, open_w, tail, passed


def pair_cols(pair):
    return slice(2 * HEAD * pair, 2 * HEAD * (pair + 1))


def scan_kernel(
    seg,
    sp,
    ci_ref,
    raw_ref,
    cw_ref,
    st_in_ref,
    tail_in_ref,
    y_ref,
    st_ref,
    st_out_ref,
    tail_out_ref,
    ext,
    mix,
    state,
    flow,
    fresh,
):
    k = pl.program_id(0)
    q = ci_ref.shape[0]
    first = (CTX * seg + k) * q

    @pl.when(k == 0)
    def _():
        state[...] = st_in_ref[...]
        ext[0:8, :] = tail_in_ref[...].astype(F32)[8:16, :]

    ci = ci_ref[...]
    tail_out_ref[...] = ci[q - 16 : q, :]
    ext[8 : 8 + q, :] = ci.astype(F32)
    since = distances(sp, first, q)
    for c in range(0, MIX, 128):
        cols = slice(c, c + 128)
        pre = conv_forward(ext, cw_ref, since, cols, q)
        mix[:, cols] = pre * jax.nn.sigmoid(pre)
    ext[0:8, :] = ext[q : q + 8, :]

    row, col, same, _, stepsize, _, cum, open_w, tail, passed = block_terms(
        sp, first, q, raw_ref[...], cw_ref
    )
    cum_t = cum.T
    keys = mix[:, WIDE : WIDE + STATE]
    kt = keys.T.astype(BF16)
    queries = mix[:, WIDE + STATE :]
    qb = queries.astype(BF16)
    scores = jnp.where(same & (row >= col), split_dot(queries, keys, ABT), 0.0)
    st_ref[...] = state[...]
    flow[...] = split_dot(queries, state[...], AB)
    low = lax.broadcasted_iota(jnp.int32, (q, 2 * HEAD), 1) < HEAD
    tail = tail * stepsize
    for pair in range(LOCAL // 2):
        cols = pair_cols(pair)
        v = mix[:, cols]
        vs = v * pair_lanes(stepsize, pair)
        outs = []
        for h in (2 * pair, 2 * pair + 1):
            damp = jnp.exp(jnp.minimum(cum[:, h : h + 1] - cum_t[h : h + 1, :], 0.0))
            outs.append(split_dot(scores * damp, vs, AB))
        inflow = flow[:, cols] * pair_lanes(open_w, pair)
        y = jnp.where(low, outs[0], outs[1]) + inflow + cw_ref[5:6, cols] * v
        y_ref[:, cols] = y
        fresh[:, cols] = (v * pair_lanes(tail, pair)).astype(BF16)
    update = dot(kt, fresh[...], AB)
    for pair in range(LOCAL // 2):
        cols = pair_cols(pair)
        state[:, cols] = state[:, cols] * pair_lanes(passed, pair) + update[:, cols]
    st_out_ref[...] = state[...]


def scan_rows(sp, seg, conv_in, step_raw, cw, state, tail):
    q = conv_in.shape[0] // CTX

    def here(x):
        return x, pl.BlockSpec((q, x.shape[1]), lambda k, sp: (k ^ sp[0], 0))

    tokens = conv_in.shape[0]
    states = pltpu.HBM((CTX * STATE, WIDE), F32)
    return call(
        "scan_rows",
        functools.partial(scan_kernel, seg),
        sp,
        [here(conv_in), here(step_raw), cw, state, tail],
        [
            here(shape((tokens, WIDE), F32)),
            (states, pl.BlockSpec((STATE, WIDE), lambda k, sp: (k, 0))),
            shape((STATE, WIDE), F32),
            shape((16, MIX), BF16),
        ],
        16,
        grid=CTX,
        scratch=[
            pltpu.VMEM((q + 8, MIX), F32),
            pltpu.VMEM((q, MIX), F32),
            pltpu.VMEM((STATE, WIDE), F32),
            pltpu.VMEM((q, WIDE), F32),
            pltpu.VMEM((q, WIDE), BF16),
        ],
    )


def stat_rows(columns):
    rows = columns[0].shape[0]
    lane = lax.broadcasted_iota(jnp.int32, (rows, 128), 1)
    table = jnp.zeros((rows, 128), F32)
    for i, column in enumerate(columns):
        table = jnp.where(lane == i, column, table)
    return table.T[0:8, :]


def stat_columns(rows):
    return jnp.concatenate([rows, jnp.zeros((120, rows.shape[1]), F32)]).T


def split_rows(row, cols):
    high = row.astype(BF16).astype(F32)
    middle = (row - high).astype(BF16).astype(F32)
    low = row - high - middle
    sub = lax.broadcasted_iota(jnp.int32, (16, row.shape[1]), 0)
    tile = jnp.where(sub == 0, high, jnp.where(sub == 1, middle, jnp.where(sub == 2, low, 0.0)))
    spare = jnp.zeros((16, cols - row.shape[1]), F32)
    return jnp.concatenate([tile, spare], axis=1).astype(BF16)


def stat_row(ref, row, count):
    if ref.dtype == F32:
        return ref[row : row + 1, :count]
    tile = ref[...].astype(F32)
    return tile[0:1, :count] + tile[1:2, :count] + tile[2:3, :count]


def store_slots(part, stat, part_refs):
    own_ref, x_ref, y_ref, late_x_ref, late_y_ref = part_refs
    q = own_ref.shape[0]
    half = q // 2
    part = part.astype(BF16)
    own_ref[...] = part[:q]
    x_ref[:half, :] = part[3 * q : 3 * q + half]
    x_ref[half:q, :] = part[q : q + half]
    y_ref[:half, :] = part[3 * q + half :]
    y_ref[half:q, :] = part[2 * q + half : 3 * q]
    late_x_ref[...] = part[q + half : 2 * q]
    late_y_ref[...] = part[2 * q : 2 * q + half]
    if stat is not None:
        tile = split_rows(stat, part.shape[1])
        x_ref[q:, :] = tile
        y_ref[q:, :] = tile


def store_part(part, stat, part_refs):
    if len(part_refs) == 1:
        part_refs[0][...] = part.astype(BF16)
    else:
        store_slots(part, stat, part_refs)


def part_shapes(slots, tokens, d, extra=0):
    if not slots:
        return [shape((tokens, d), BF16)]
    q = tokens // CTX
    sent = shape((q + extra, d), BF16)
    return [shape((q, d), BF16), sent, sent] + [shape((q // 2, d), BF16)] * 2


def tail_tile(x):
    return x, pl.BlockSpec((16, x.shape[1]), lambda i, sp: (x.shape[0] // 16 - 1, 0))


def head_tile(x):
    return x, pl.BlockSpec((16, x.shape[1]), lambda i, sp: (0, 0))


def turn_kernel(sp, from_x_ref, from_y_ref, late_x_ref, late_y_ref, x_ref, y_ref):
    half = y_ref.shape[0]
    x_ref[:half, :] = (late_x_ref[...].astype(F32) + from_y_ref[:half, :].astype(F32)).astype(BF16)
    y_ref[...] = (late_y_ref[...].astype(F32) + from_x_ref[:half, :].astype(F32)).astype(BF16)
    if x_ref.shape[0] > half:
        x_ref[half:, :] = from_y_ref[2 * half :, :]


def out_kernel(count, before, sp, *refs):
    if before:
        before_ref, refs = refs[0], refs[1:]
    normed_ref, y_ref, cw_ref, wg_ref, wo_ref = refs[count : count + 5]
    gate_ref, stat_ref = refs[count + 5 : count + 7]
    gate = dot(normed_ref[...], wg_ref[...], AB)
    gate_ref[...] = gate
    g = y_ref[...] * gate * jax.nn.sigmoid(gate)
    part = dot((g * cw_ref[9:10, :WIDE]).astype(BF16), wo_ref[...], AB)
    square = jnp.sum(g * g, axis=-1, keepdims=True)
    inner = [
        jnp.sum(part[first : first + u.shape[0]] * u.astype(F32), axis=-1, keepdims=True)
        for first, u in load_rows(refs[:count])
    ]
    rows = stat_rows([square] + ([jnp.concatenate(inner)] if inner else []))
    store_part(part, rows[0:1, :], refs[count + 7 :])
    if before:
        rows = jnp.concatenate([before_ref[...], rows])
    stat_ref[...] = rows


def out_rows(sp, slots, before, pieces, normed, y, cw, wg, wo):
    tokens, d = normed.shape
    return call(
        "out_rows",
        functools.partial(out_kernel, len(pieces), len(before)),
        sp,
        before + pieces + [normed, y, cw, wg, wo],
        [shape((tokens, WIDE), F32), shape((8 + 8 * len(before), tokens), F32)] + part_shapes(slots, tokens, d, 16),
        28,
    )


def slot_sums(stat_refs, row, q):
    out = []
    for slot in range(CTX):
        total = 0.0
        for m, ref in enumerate(stat_refs):
            total = total + stat_row(ref, row, CTX * q)[:, (slot ^ m) * q : (slot ^ m) * q + q]
        out.append(total)
    return jnp.concatenate(out, axis=1)


def own_sum(refs):
    own, from_x, from_y, late_x, late_y = [ref[...].astype(F32) for ref in refs]
    half = late_y.shape[0]
    x = jnp.concatenate([from_x[half : 2 * half], late_x[:half]])
    return own + x + jnp.concatenate([late_y, from_y[half : 2 * half]])


def own_squares(stats, sp, natural, q):
    if not natural:
        rows = [stat_row(ref, 0, CTX * q) for ref in stats]
        return sum(row[:, m * q : m * q + q] for m, row in enumerate(rows))
    place, out = sp[0], []
    block = q // 2
    for half in range(2):
        total = jnp.zeros((1, block), F32)
        for s in range(SEGS):
            for slot in range(CTX):
                here = ((place >> 1) == s) & ((slot ^ place) == 2 * (place & 1) + half)
                for m, ref in enumerate(stats):
                    value = ref[8 * s : 8 * s + 1, pl.ds((slot ^ m) * block, block)]
                    total = total + jnp.where(here, value, 0.0)
        out.append(total)
    return jnp.concatenate(out, axis=1)


def own_kernel(count, natural, sp, *refs):
    stats, partial = refs[:CTX], refs[CTX : CTX + 5]
    residual = jnp.concatenate([x for _, x in load_rows(refs[CTX + 5 : CTX + 5 + count])])
    own_ref, branch_ref = refs[CTX + 5 + count :]
    square = own_squares(stats, sp, natural, own_ref.shape[0])
    square = jnp.concatenate([square, jnp.zeros((7, square.shape[1]), F32)])
    scale = lax.rsqrt(stat_columns(square)[:, 0:1] / INNER + NORM_EPS)
    branch = own_sum(partial) * scale
    branch_ref[...] = branch
    own_ref[...] = (residual.astype(F32) + branch).astype(BF16)


def own_rows(sp, natural, stats, partial, residual):
    q, d = partial[0].shape
    return call(
        "own_rows",
        functools.partial(own_kernel, len(residual), natural),
        sp,
        stats + partial + residual,
        [shape((q, d), BF16), shape((q, d), F32)],
        16,
    )


def collect_kernel(sp, part0_ref, part1_ref, own_ref, x_ref, y_ref, late_x_ref, late_y_ref):
    place = sp[0]
    q = late_x_ref.shape[0]
    goals = [
        [own_ref.at[pl.ds(0, q)], own_ref.at[pl.ds(q, q)]],
        [x_ref.at[pl.ds(q, q)], late_x_ref],
        [late_y_ref, y_ref.at[pl.ds(q, q)]],
        [x_ref.at[pl.ds(0, q)], y_ref.at[pl.ds(0, q)]],
    ]
    for m in range(CTX):
        owner = place ^ m
        for half in range(2):
            slot = (2 * (owner & 1) + half) ^ place
            rows = pl.ds(pl.multiple_of(slot * q, q), q)
            goals[m][half][...] = choose((owner >> 1) == 0, part0_ref[rows, :], part1_ref[rows, :])


def collect(sp, parts):
    tokens, d = parts[0].shape
    return call("collect", collect_kernel, sp, list(parts), part_shapes(True, 2 * tokens, d), 20)


def natural_kernel(extra, sp, *refs):
    out_ref = refs[-1]
    q = out_ref.shape[0] // 2
    for place in range(CTX):
        s = place >> 1
        own, x, y, first, second = refs[5 * s : 5 * s + 5]

        @pl.when(sp[0] == place)
        def _():
            for half in range(2):
                slot = (2 * (place & 1) + half) ^ place
                at = half * q
                if slot < 3:
                    out_ref[at : at + q, :] = (own, x, y)[slot][extra:, :]
                else:
                    out_ref[at : at + q // 2, :] = first[extra:, :]
                    out_ref[at + q // 2 : at + q, :] = second[...]


def natural_rows(sp, pieces, extra=0):
    q, d = pieces[0][0].shape
    ins = [x for one in pieces for x in one]
    kernel = functools.partial(natural_kernel, extra)
    return call("natural_rows", kernel, sp, ins, [shape((2 * (q - extra), d), BF16)])[0]


def gate_back_kernel(count, inners, first_stat, sp, *refs):
    pieces, stats = refs[:count], refs[count : count + CTX]
    inner_refs = refs[count + CTX : count + CTX + inners]
    rest = refs[count + CTX + inners :]
    y_ref, gate_ref, cw_ref, wo_ref, dy_ref, dgate_ref, gated_ref, u_ref, dgain_ref = rest
    gain = cw_ref[9:10, :WIDE]
    tokens = y_ref.shape[0]
    q = tokens // CTX
    for first, u in load_rows(pieces, 16 if inners else 0):
        u_ref[pl.ds(first, u.shape[0]), :] = u
    back = dot(u_ref[...], wo_ref[...], ABT)
    scale = lax.rsqrt(slot_sums(stats, first_stat, q) / INNER + NORM_EPS)
    if inners:
        inner = jnp.concatenate([stat_row(ref, 0, q) for ref in inner_refs], axis=1)
    else:
        inner = slot_sums(stats, first_stat + 1, q) * scale
    pull = scale * scale * inner / INNER
    table = stat_columns(jnp.concatenate([scale, pull, jnp.zeros((6, tokens), F32)]))
    scale, pull = table[:, 0:1], table[:, 1:2]
    gate = gate_ref[...]
    y = y_ref[...]
    sig = jax.nn.sigmoid(gate)
    act = gate * sig
    g = y * act
    unit = g * scale
    gated_ref[...] = (unit * gain).astype(BF16)
    dg = back * gain * scale - g * pull
    dy_ref[...] = (dg * act).astype(BF16)
    dgate_ref[...] = (dg * y * (sig + act * (1.0 - sig))).astype(BF16)
    dgain_ref[...] = jnp.broadcast_to(jnp.sum(back * unit, axis=0, keepdims=True), (8, WIDE))


def gate_back(sp, pieces, stats, first_stat, inners, y, gate, cw, wo):
    tokens, d = y.shape[0], wo.shape[1]
    return call(
        "gate_back",
        functools.partial(gate_back_kernel, len(pieces), len(inners), first_stat),
        sp,
        pieces + stats + inners + [y, gate, cw, wo],
        [shape((tokens, WIDE), BF16)] * 3 + [shape((tokens, d), BF16), shape((8, WIDE), F32)],
        28,
    )


def scan_back_kernel(
    seg,
    sp,
    ci_ref,
    prev_ref,
    raw_ref,
    dy_ref,
    st_ref,
    tail_in_ref,
    cw_ref,
    dst_in_ref,
    next_in_ref,
    dci_ref,
    dcw_ref,
    dhp_ref,
    dst_out_ref,
    next_out_ref,
    ext,
    mix,
    slope,
    dext,
    dstate,
    tails,
    dyw,
    flow,
    kept_all,
    ends,
):
    i = pl.program_id(0)
    k = CTX - 1 - i
    q = ci_ref.shape[0]
    first = (CTX * seg + k) * q

    @pl.when(i == 0)
    def _():
        dstate[...] = dst_in_ref[...]
        dext[q : q + 8, :] = next_in_ref[...]
        ends[...] = jnp.zeros_like(ends)
        dcw_ref[...] = jnp.zeros_like(dcw_ref)
        dhp_ref[...] = jnp.zeros_like(dhp_ref)

    @pl.when(k == 0)
    def _():
        ext[0:8, :] = tail_in_ref[...].astype(F32)[8:16, :]

    @pl.when(k > 0)
    def _():
        ext[0:8, :] = prev_ref[...].astype(F32)[8:16, :]

    ext[8 : 8 + q, :] = ci_ref[...].astype(F32)
    since = distances(sp, first, q + 8)
    for c in range(0, MIX, 128):
        cols = slice(c, c + 128)
        pre = conv_forward(ext, cw_ref, since[0:q], cols, q)
        sig = jax.nn.sigmoid(pre)
        act = pre * sig
        mix[:, cols] = act
        slope[:, cols] = sig + act * (1.0 - sig)

    row, col, same, shifted, stepsize, decay, cum, open_w, tail, passed = block_terms(
        sp, first, q, raw_ref[...], cw_ref
    )
    cum_t = cum.T
    keys = mix[:, WIDE : WIDE + STATE]
    kb = keys.astype(BF16)
    queries = mix[:, WIDE + STATE :]
    qb = queries.astype(BF16)
    qt = queries.T.astype(BF16)
    inside = same & (col >= row)
    scores = jnp.where(inside, split_dot(keys, queries, ABT), 0.0)
    stb, dstb = st_ref[...].astype(BF16), dstate[...].astype(BF16)
    flow[...] = dot(qb, stb, AB)
    kept_all[...] = dot(kb, dstb, AB)
    low = lax.broadcasted_iota(jnp.int32, (q, 2 * HEAD), 1) < HEAD
    lane = lax.broadcasted_iota(jnp.int32, (q, 128), 1)
    sub = lax.broadcasted_iota(jnp.int32, (16, q), 0)
    dscores = jnp.zeros((q, q), F32)
    plus_t = jnp.zeros((16, q), F32)
    dstep = jnp.zeros((q, 128), F32)
    dcum = jnp.zeros((q, 128), F32)
    for pair in range(LOCAL // 2):
        cols = pair_cols(pair)
        v = mix[:, cols]
        step_e = pair_lanes(stepsize, pair)
        vs = v * step_e
        vsb = vs.astype(BF16)
        dyb = dy_ref[:, cols]
        dyf = dyb.astype(F32)
        dvs = []
        for side, h in ((0, 2 * pair), (1, 2 * pair + 1)):
            mine = low if side == 0 else ~low
            damp = jnp.exp(jnp.minimum(cum_t[h : h + 1, :] - cum[:, h : h + 1], 0.0))
            raw = dot(jnp.where(mine, vs, 0.0).astype(BF16), dyb, ABT)
            mixing = (scores * damp).astype(BF16)
            dscores = dscores + raw * damp
            both = raw * mixing.astype(F32)
            plus_t = plus_t + jnp.where(sub == h, jnp.sum(both, axis=0, keepdims=True), 0.0)
            dvs.append(dot(mixing, dyb, AB))
        dv = jnp.where(low, dvs[0], dvs[1])
        weighted = dyf * pair_lanes(open_w, pair)
        dyw[:, cols] = weighted.astype(BF16)
        tail_e = pair_lanes(tail, pair)
        kept = kept_all[:, cols] * tail_e
        tails[:, cols] = (vs * tail_e).astype(BF16)
        u = dv + kept
        dext[0:q, cols] = (u * step_e + cw_ref[5:6, cols] * dyf) * slope[:, cols]
        from_tail = kept * vs
        dcw_ref[5:6, cols] += jnp.sum(dyf * v, axis=0, keepdims=True)
        ends[1:2, cols] = jnp.sum(from_tail, axis=0, keepdims=True)
        uv = u * v
        change = weighted * flow[:, cols] - dv * vsb.astype(F32) - from_tail
        for side, h in ((0, 2 * pair), (1, 2 * pair + 1)):
            mine = low if side == 0 else ~low

            def per_row(x):
                return jnp.sum(jnp.where(mine, x, 0.0), axis=1, keepdims=True)

            dstep = jnp.where(lane == h, per_row(uv), dstep)
            dcum = jnp.where(lane == h, per_row(change), dcum)

    dcum = dcum + jnp.concatenate([plus_t, jnp.zeros((112, q), F32)]).T
    ends[0:1, :] = jnp.sum(st_ref[...] * dstate[...], axis=0, keepdims=True)
    by_head = dot(ends[...], channel_map(), AB, HIGH)
    at_end = by_head[0:1, :] * passed + by_head[1:2, :]
    dcum = dcum + jnp.where(row == q - 1, at_end, 0.0)
    upper = jnp.where(col >= row, 1.0, 0.0)
    ddecay = dot(upper, dcum, AB, HIGH)
    draw = (dstep - ddecay * cw_ref[11:12, 0:128]) * jax.nn.sigmoid(shifted)
    dci_ref[:, MIX:] = draw.astype(BF16)
    dhp_ref[0:1, :] += jnp.sum(draw, axis=0, keepdims=True)
    dhp_ref[1:2, :] += jnp.sum(ddecay * decay, axis=0, keepdims=True)

    dsb = jnp.where(inside, dscores, 0.0).astype(BF16)
    dkeys = dot(dsb, qb, AB) + dot(tails[...], dstb, ABT)
    dqueries = dot(dsb, kb, ATB) + dot(dyw[...], stb, ABT)
    kcols, qcols = slice(WIDE, WIDE + STATE), slice(WIDE + STATE, MIX)
    dext[0:q, kcols] = dkeys * slope[:, kcols]
    dext[0:q, qcols] = dqueries * slope[:, qcols]
    update = dot(qt, dyw[...], AB)
    for pair in range(LOCAL // 2):
        cols = pair_cols(pair)
        dstate[:, cols] = dstate[:, cols] * pair_lanes(passed, pair) + update[:, cols]
    dst_out_ref[...] = dstate[...]

    for c in range(0, MIX, 128):
        cols = slice(c, c + 128)
        here = dext[0:q, cols]
        total = cw_ref[3:4, cols] * here
        dcw_ref[3:4, cols] += jnp.sum(here * ext[8 : 8 + q, cols], axis=0, keepdims=True)
        dcw_ref[4:5, cols] += jnp.sum(here, axis=0, keepdims=True)
        for shift in range(1, CONV):
            later = jnp.where(since[shift : shift + q] >= shift, dext[shift : shift + q, cols], 0.0)
            total = total + cw_ref[3 - shift : 4 - shift, cols] * later
            used = jnp.where(since[0:q] >= shift, ext[8 - shift : 8 - shift + q, cols], 0.0)
            dcw_ref[3 - shift : 4 - shift, cols] += jnp.sum(here * used, axis=0, keepdims=True)
        dci_ref[:, cols] = total.astype(BF16)
    head_rows = dext[0:8, :]
    dext[q : q + 8, :] = head_rows
    next_out_ref[...] = head_rows


def scan_back(sp, stored, seg, conv_in, step_raw, dy, states, tail, cw, dstate, following):
    tokens = conv_in.shape[0]
    q = tokens // CTX

    def here(x):
        return x, pl.BlockSpec((q, x.shape[1]), lambda i, sp: ((CTX - 1 - i) ^ sp[0], 0))

    if stored:
        conv_in, step_raw, dy, states = [far(x) for x in (conv_in, step_raw, dy, states)]
        tail, cw, dstate, following = [far(x) for x in (tail, cw, dstate, following)]

    def before(i, sp):
        return (jnp.maximum(CTX - 2 - i, 0) ^ sp[0]) * (q // 16) + q // 16 - 1, 0

    return call(
        "scan_back",
        functools.partial(scan_back_kernel, seg),
        sp,
        [
            here(conv_in),
            (conv_in, pl.BlockSpec((16, MIX), before)),
            here(step_raw),
            here(dy),
            (states, pl.BlockSpec((STATE, WIDE), lambda i, sp: (CTX - 1 - i, 0))),
            tail,
            cw,
            dstate,
            following,
        ],
        [
            here(shape((tokens, FULL), BF16)),
            shape((8, MIX), F32),
            shape((8, 128), F32),
            shape((STATE, WIDE), F32),
            shape((8, MIX), F32),
        ],
        24,
        grid=CTX,
        scratch=[
            pltpu.VMEM((q + 8, MIX), F32),
            pltpu.VMEM((q, MIX), F32),
            pltpu.VMEM((q, MIX), F32),
            pltpu.VMEM((q + 8, MIX), F32),
            pltpu.VMEM((STATE, WIDE), F32),
            pltpu.VMEM((q, WIDE), BF16),
            pltpu.VMEM((q, WIDE), BF16),
            pltpu.VMEM((q, WIDE), F32),
            pltpu.VMEM((q, WIDE), F32),
            pltpu.VMEM((8, WIDE), F32),
        ],
    )


def input_back_kernel(sp, dc_ref, dg_ref, wc_ref, wg_ref, *part_refs):
    part = dot(dc_ref[...], wc_ref[...], ABT) + dot(dg_ref[...], wg_ref[...], ABT)
    store_part(part, None, part_refs)


def input_back(sp, slots, dconv, dgate, wc, wg):
    outs = part_shapes(slots, dconv.shape[0], wc.shape[0])
    return call("input_back", input_back_kernel, sp, [dconv, dgate, wc, wg], outs, 24)


def own_back_kernel(count, sp, *refs):
    partial, rest = refs[:5], refs[5:]
    x = jnp.concatenate([v for _, v in load_rows(rest[:count])]).astype(F32)
    u = jnp.concatenate([v for _, v in load_rows(rest[count : 2 * count])]).astype(F32)
    cw_ref, branch_ref, up_ref, dnorm_ref = rest[2 * count :]
    grad = own_sum(partial)
    scale = row_scale(x)
    gained = grad * cw_ref[8:9, :]
    centre = jnp.mean(gained * x, axis=-1, keepdims=True)
    up = (u + scale * (gained - x * (scale * scale * centre))).astype(BF16)
    extra = up_ref.shape[0] - up.shape[0]
    up_ref[extra:, :] = up
    if extra:
        inner = jnp.sum(up.astype(F32) * branch_ref[...], axis=-1, keepdims=True)
        up_ref[:extra, :] = split_rows(stat_rows([inner])[0:1, :], up.shape[1])
    dnorm_ref[...] = jnp.broadcast_to(
        jnp.sum(grad * x * scale, axis=0, keepdims=True), dnorm_ref.shape
    )


def own_back(sp, extra, partial, x, u, cw, branch):
    q, d = partial[0].shape
    return call(
        "own_back",
        functools.partial(own_back_kernel, len(x)),
        sp,
        partial + x + u + [cw, branch],
        [shape((q + extra, d), BF16), shape((8, d), F32)],
    )


def head_map(group, block, flipped=False):
    here = lax.broadcasted_iota(jnp.int32, (128, 128), 1 if flipped else 0)
    there = lax.broadcasted_iota(jnp.int32, (128, 128), 0 if flipped else 1)
    turn = jnp.zeros_like(here)
    for edge in range(block, LOCAL, block):
        turn = turn + jnp.where(here >= edge, 1, 0)
    goal = here + (turn * (CTX - 1) + group) * block
    return jnp.where((here < LOCAL) & (there == goal), 1.0, 0.0)


def channel_map(flipped=False):
    dims = (128, WIDE) if flipped else (WIDE, 128)
    chan = lax.broadcasted_iota(jnp.int32, dims, 1 if flipped else 0)
    head = lax.broadcasted_iota(jnp.int32, dims, 0 if flipped else 1)
    return jnp.where((chan >= head * HEAD) & (chan < (head + 1) * HEAD), 1.0, 0.0)


def spans(group, block):
    wide = block * HEAD
    return [(z * wide, (z * CTX + group) * wide, wide) for z in range(WIDE // wide)]


def choose(first, a, b):
    return jnp.where(first, a, b)


def pack_kernel(block, sp, w_ref, *refs):
    conv_refs, gate_refs, conv, gate = refs[:CTX], refs[CTX : 2 * CTX], refs[-2], refs[-1]
    place = sp[0]
    keys = w_ref[:, 2 * INNER : 2 * INNER + STATE]
    queries = w_ref[:, 2 * INNER + STATE : 2 * INNER + 2 * STATE]
    steps = w_ref[:, 2 * INNER + 2 * STATE :]
    rows = w_ref.shape[0]
    steps = jnp.concatenate([steps, jnp.zeros((rows, 128 - HEADS), BF16)], axis=1)
    for k in range(CTX):
        values = jnp.concatenate(
            [w_ref[:, INNER + there : INNER + there + n] for _, there, n in spans(k, block)], axis=1
        )
        gates = jnp.concatenate(
            [w_ref[:, there : there + n] for _, there, n in spans(k, block)], axis=1
        )
        step = dot(steps, head_map(k, block, True).astype(BF16), AB).astype(BF16)
        conv[k] = jnp.concatenate(
            [values[:, :HALF], keys, step, values[:, HALF:], queries, step], axis=1
        )
        gate[k] = gates
    for m in range(CTX):
        conv_refs[m][...] = conv[m ^ place]
        gate_refs[m][...] = gate[m ^ place]


def pack(sp, block, w_in):
    rows = w_in.shape[0]
    outs = call(
        "pack",
        functools.partial(pack_kernel, block),
        sp,
        [w_in],
        [shape((rows, 2 * LOAD), BF16)] * CTX + [shape((rows, WIDE), BF16)] * CTX,
        16,
        scratch=[
            pltpu.VMEM((CTX, rows, 2 * LOAD), BF16),
            pltpu.VMEM((CTX, rows, WIDE), BF16),
        ],
    )
    return outs[:CTX], outs[CTX:]


def order_conv_kernel(sp, *refs):
    keep_ref, send_ref = refs[CTX:]
    zero = sp[1] == 0
    for m in range(CTX):
        low, high = refs[m][:, :LOAD], refs[m][:, LOAD:]
        keep_ref[m ^ sp[0]] = choose(zero, low, high)
        send_ref[m ^ sp[0]] = choose(zero, high, low)


def order_conv(sp, slots):
    out = shape((CTX, slots[0].shape[0], LOAD), BF16)
    return call("order_conv", order_conv_kernel, sp, slots, [out, out], 12)


def order_gate_kernel(sp, *refs):
    out_ref, keep_ref, send_ref = refs[CTX:]
    zero = sp[1] == 0
    rows = keep_ref.shape[1]
    for m in range(CTX):
        low, high = refs[m][:, :HALF], refs[m][:, HALF:]
        keep_ref[m ^ sp[0], :, :HALF] = choose(zero, low, high)
        send_ref[m ^ sp[0], :, :HALF] = choose(zero, high, low)
    for r in range(2):
        for c in range(2):
            at = slice(r * rows, (r + 1) * rows)
            low = out_ref[at, c * HALF : (c + 1) * HALF]
            high = out_ref[at, (2 + c) * HALF : (3 + c) * HALF]
            keep_ref[2 * r + c, :, HALF:] = choose(zero, low, high)
            send_ref[2 * r + c, :, HALF:] = choose(zero, high, low)


def order_gate(sp, slots, w_out):
    out = shape((CTX, slots[0].shape[0], WIDE), BF16)
    return call("order_gate", order_gate_kernel, sp, slots + [w_out], [out, out], 12)


def join_conv_kernel(sp, mine_ref, other_ref, wc_ref):
    zero = sp[1] == 0
    rows = mine_ref.shape[2]
    for i in range(CTX):
        a, b = mine_ref[0, i, :, :LOAD], other_ref[0, i, :, :LOAD]
        low, high = choose(zero, a, b), choose(zero, b, a)
        at = slice(i * rows, (i + 1) * rows)
        wc_ref[at, 0:HALF] = low[:, :HALF]
        wc_ref[at, HALF:WIDE] = high[:, :HALF]
        wc_ref[at, WIDE : WIDE + STATE] = low[:, HALF : HALF + STATE]
        wc_ref[at, WIDE + STATE : MIX] = high[:, HALF : HALF + STATE]
        wc_ref[at, MIX:] = low[:, HALF + STATE :]


def by_rows(x, count):
    return x, pl.BlockSpec((x.shape[0] // count, x.shape[1]), lambda z, sp: (z, 0))


def join_conv(sp, mine, other):
    dp, _, rows, _ = mine.shape
    out = by_rows(shape((dp * CTX * rows, FULL), BF16), dp)
    ins = [by_first(mine), by_first(other)]
    return call("join_conv", join_conv_kernel, sp, ins, [out], 12, dp)[0]


def join_gate_kernel(first, sp, mine_ref, other_ref, wg_ref, wo_ref):
    zero = sp[1] == 0
    rows = mine_ref.shape[2]
    for i in range(CTX):
        a, b = mine_ref[0, i, :, first:], other_ref[0, i, :, first:]
        low, high = choose(zero, a, b), choose(zero, b, a)
        at = slice(i * rows, (i + 1) * rows)
        wg_ref[at, :HALF] = low[:, :HALF]
        wg_ref[at, HALF:] = high[:, :HALF]
        r, c = i // 2, i % 2
        at = slice(r * rows, (r + 1) * rows)
        wo_ref[at, c * HALF : (c + 1) * HALF] = low[:, HALF:]
        wo_ref[at, (2 + c) * HALF : (3 + c) * HALF] = high[:, HALF:]


def join_gate(sp, mine, other):
    dp, _, rows, cols = mine.shape
    wg, wo = shape((dp * CTX * rows, WIDE), BF16), shape((dp * 2 * rows, 4 * HALF), BF16)
    outs = [by_rows(wg, dp), by_rows(wo, dp)]
    kernel = functools.partial(join_gate_kernel, cols - WIDE)
    ins = [by_first(mine), by_first(other)]
    return call("join_gate", kernel, sp, ins, outs, 12, dp)


def fold_kernel(sp, keep_ref, came_ref, out_ref):
    out_ref[...] = (keep_ref[...].astype(F32) + came_ref[...].astype(F32)).astype(BF16)


def fold(sp, keep, came):
    ins = [by_first(keep), by_first(came)]
    return call("fold", fold_kernel, sp, ins, [by_first(shape(keep.shape, BF16))], 24, keep.shape[0])


def total_kernel(counts, sp, *refs):
    for m in range(CTX):
        parts = [ref[m ^ sp[0], :, :cols] for ref, cols in zip(refs, counts)]
        refs[len(counts) + m][...] = jnp.concatenate(parts, axis=1)


def total_line(sp, sums):
    width = {LOAD: LOAD, WIDE: HALF}
    counts = [width[x.shape[2]] for x in sums]
    outs = [shape((sums[0].shape[1], sum(counts)), BF16)] * CTX
    sums = [far(x) for x in sums]
    return call("total_line", functools.partial(total_kernel, counts), sp, sums, outs)


def mix_kernel(cols, sp, *refs):
    out_ref = refs[-1]
    zero = sp[1] == 0
    for m in range(CTX):
        if cols == LOAD:
            mine, other = refs[CTX + m][...], refs[m][:, :LOAD]
        else:
            mine, other = refs[m][:, LOAD + HALF :], refs[m][:, LOAD : LOAD + HALF]
            out_ref[m, :, HALF:] = choose(zero, refs[CTX + 1][m, :, HALF:], refs[CTX][m, :, HALF:])
        out_ref[m, :, : mine.shape[1]] = choose(zero, other, mine)


def mix(sp, early, late, cols):
    out = shape((CTX, early[0].shape[0], cols), BF16)
    return call("mix", functools.partial(mix_kernel, cols), sp, early + late, [out])[0]


def grad_conv_kernel(sp, n0_ref, n1_ref, d0_ref, d1_ref, keep_ref, send_ref):
    zero = sp[1] == 0
    rows = keep_ref.shape[2]
    total = dot(n0_ref[...], d0_ref[...], ATB) + dot(n1_ref[...], d1_ref[...], ATB)
    total = total.astype(BF16)
    step = total[:, MIX:]
    low = jnp.concatenate([total[:, :HALF], total[:, WIDE : WIDE + STATE], step], axis=1)
    high = jnp.concatenate([total[:, HALF:WIDE], total[:, WIDE + STATE : MIX], step], axis=1)
    keep, send = choose(zero, low, high), choose(zero, high, low)
    for i in range(CTX):
        keep_ref[0, i] = keep[i * rows : (i + 1) * rows]
        send_ref[0, i] = send[i * rows : (i + 1) * rows]


def by_first(x):
    rest = (0,) * (len(x.shape) - 1)
    return x, pl.BlockSpec((1,) + tuple(x.shape[1:]), lambda z, sp: (z,) + rest)


def by_cols(x, count):
    return x, pl.BlockSpec((x.shape[0], x.shape[1] // count), lambda z, sp: (0, z))


def grad_conv(sp, dp, rows, normed, dconv):
    out = shape((dp, CTX, rows, LOAD), BF16)
    return call(
        "grad_conv",
        grad_conv_kernel,
        sp,
        [by_cols(x, dp) for x in normed] + list(dconv),
        [by_first(out), by_first(out)],
        24,
        dp,
    )


def grad_gate_kernel(sp, *refs):
    n_refs, dg_refs, gated_refs, u_refs = refs[0:2], refs[2:4], refs[4:6], refs[6:8]
    keep_ref, send_ref = refs[8:]
    z = pl.program_id(0)
    dp, _, rows, _ = keep_ref.shape
    zero = sp[1] == 0

    def over_tokens(a, b):
        return dot(a[0][...], b[0][...], ATB) + dot(a[1][...], b[1][...], ATB)

    total = over_tokens(n_refs, dg_refs).astype(BF16)
    keep = choose(zero, total[:, :HALF], total[:, HALF:])
    send = choose(zero, total[:, HALF:], total[:, :HALF])
    for i in range(CTX):
        keep_ref[z, i, :, :HALF] = keep[i * rows : (i + 1) * rows]
        send_ref[z, i, :, :HALF] = send[i * rows : (i + 1) * rows]
    total = over_tokens(gated_refs, u_refs).astype(BF16)
    side, c = z // 2, lax.rem(z, 2)

    def put(ref):
        for there in range(dp):
            for r in range(2):
                first = (2 * there + r) * rows
                ref[there, 2 * r + c, :, HALF:] = total[first : first + rows]

    @pl.when(side == sp[1])
    def _():
        put(keep_ref)

    @pl.when(side != sp[1])
    def _():
        put(send_ref)


def grad_gate(sp, dp, rows, normed, dgate, gated, u):
    out = shape((dp, CTX, rows, WIDE), BF16)
    return call(
        "grad_gate",
        grad_gate_kernel,
        sp,
        [by_cols(x, dp) for x in normed]
        + list(dgate)
        + list(gated)
        + [by_cols(x, dp) for x in u],
        [out, out],
        32,
        dp,
    )


def finish_kernel(block, sp, *refs):
    early, late, (gate0, gate1, came_gate, came_conv) = refs[:4], refs[4:8], refs[8:12]
    in_ref, out_ref, lows, highs, glows, ghighs = refs[12:]
    place, zero = sp[0], sp[1] == 0
    rows = in_ref.shape[0]
    for m in range(CTX):
        mine, came = choose(zero, late[m][...], early[m][:, :LOAD]), came_conv[m]
        lows[m ^ place] = choose(zero, mine, came).astype(F32)
        highs[m ^ place] = choose(zero, came, mine).astype(F32)
        mine = choose(zero, early[m][:, LOAD + HALF :], early[m][:, LOAD : LOAD + HALF])
        came = came_gate[m, :, :HALF]
        glows[m ^ place] = choose(zero, mine, came).astype(F32)
        ghighs[m ^ place] = choose(zero, came, mine).astype(F32)
    keys, queries, steps = 0.0, 0.0, 0.0
    for k in range(CTX):
        keys = keys + lows[k, :, HALF : HALF + STATE]
        queries = queries + highs[k, :, HALF : HALF + STATE]
        steps = steps + dot(lows[k, :, HALF + STATE :], head_map(k, block), AB, HIGH)
    for z in range(WIDE // (block * HEAD)):
        def side_by_side(a, b):
            parts = []
            for k in range(CTX):
                here, _, n = spans(k, block)[z]
                source = a if here < HALF else b
                parts.append(source[k, :, here % HALF : here % HALF + n])
            return jnp.concatenate(parts, axis=1)

        wide = CTX * block * HEAD
        in_ref[:, z * wide : (z + 1) * wide] = side_by_side(glows, ghighs)
        in_ref[:, INNER + z * wide : INNER + (z + 1) * wide] = side_by_side(lows, highs)
    in_ref[:, 2 * INNER : 2 * INNER + STATE] = keys
    in_ref[:, 2 * INNER + STATE : 2 * INNER + 2 * STATE] = queries
    in_ref[:, 2 * INNER + 2 * STATE :] = steps[:, :HEADS]
    for i in range(4):
        r, c = i // 2, i % 2
        mine, came = choose(zero, gate0[i, :, HALF:], gate1[i, :, HALF:]), came_gate[i, :, HALF:]
        at = slice(r * rows, (r + 1) * rows)
        out_ref[at, c * HALF : (c + 1) * HALF] = choose(zero, mine, came).astype(F32)
        out_ref[at, (2 + c) * HALF : (3 + c) * HALF] = choose(zero, came, mine).astype(F32)


def finish(sp, block, early, late, gates, came_gate, came_conv):
    rows = came_conv.shape[1]
    return call(
        "finish",
        functools.partial(finish_kernel, block),
        sp,
        early + late + gates + [came_gate, came_conv],
        [shape((rows, 2 * INNER + 2 * STATE + HEADS), F32), shape((2 * rows, 4 * HALF), F32)],
        24,
        scratch=[pltpu.VMEM((CTX, rows, LOAD), F32)] * 2 + [pltpu.VMEM((CTX, rows, HALF), F32)] * 2,
    )


class Direct:
    def __init__(self, order, mine, dp, block, w_in, w_out):
        self.order, self.mine, self.dp, self.block = order, mine, dp, block
        self.rows = w_in.shape[0]
        conv, gate = order(pack, block, w_in)
        conv = order(order_conv, [flip(x, m) if m else x for m, x in enumerate(conv)])
        self.conv = self.trade(*conv)
        self.first = self.gathered(self.conv[0])
        gate = [order.now(x) for x in gate]
        self.slots = [flip(x, m) if m else x for m, x in enumerate(gate)]
        self.w_out = w_out

    def prepare_gate(self):
        self.gate = self.trade(*self.order(order_gate, self.slots, self.w_out))

    def trade(self, keep, send):
        came = swap_core(send)
        return choose(self.mine == 0, keep, came), choose(self.mine == 0, came, keep)

    def gathered(self, x):
        return lax.all_gather(x, "dp", axis=0)

    def start_conv(self):
        return self.first

    def start_gate(self, after):
        x, _ = lax.optimization_barrier((self.order.now(self.gate[0]), after))
        return self.gathered(x)

    def start_second(self):
        return self.gathered(self.order.now(self.conv[1])), self.gathered(self.order.now(self.gate[1]))

    def trade_weights(self, x):
        x = self.order.now(x)
        return x, swap_core(x)

    def conv_weights(self, sp, both):
        return join_conv(sp, *both)

    def gate_weights(self, sp, both):
        return join_gate(sp, *both)

    def grad_gate(self, sp, layer, normed, dgate, gated, u):
        return grad_gate(sp, self.dp, self.rows, normed, dgate, gated, u)

    def grad_conv(self, sp, layer, normed, dconv):
        return grad_conv(sp, self.dp, self.rows, normed, dconv)

    def trade_grads(self, grads):
        return grads[0], swap_core(grads[1])

    def send(self, traded):
        (total,) = self.order(fold, *traded)
        return lax.psum_scatter(total, "dp", scatter_dimension=0, tiled=True)[0]

    def early(self, conv1, gate1, gate0):
        self.gates = [gate0, gate1]
        slots = self.order(total_line, [conv1, gate1, gate0])
        self.slots = [flip(x, m) if m else x for m, x in enumerate(slots)]

    def early_trade(self):
        self.came = swap_core(self.order(mix, self.slots, self.gates, WIDE))

    def late(self, conv0):
        late = self.order(total_line, [conv0])
        self.last = [flip(x, m) if m else x for m, x in enumerate(late)]

    def late_trade(self):
        self.last_came = swap_core(self.order(mix, self.slots, self.last, LOAD))

    def gradients(self):
        arrays = self.slots, self.last, self.gates, self.came, self.last_came
        return self.order(finish, self.block, *arrays)


def grouped(columns, block):
    lead = columns.shape[:-1]
    split = jnp.moveaxis(columns.reshape(lead + (-1, CTX, block)), -2, 0)
    return split.reshape((CTX,) + lead + (-1,))


def ungrouped(groups, block):
    lead = groups.shape[1:-1]
    split = groups.reshape((CTX,) + lead + (-1, block))
    return jnp.moveaxis(split, 0, -2).reshape(lead + (-1,))


def pad_to(x, rows, cols):
    room = [(0, 0)] * (x.ndim - 2) + [(0, rows - x.shape[-2]), (0, cols - x.shape[-1])]
    return jnp.pad(x, room)


class Plain:
    def __init__(self, mine, place, block, w_in, w_out):
        self.mine, self.place, self.block = mine, place, block
        full_in = lax.all_gather(w_in, ("dp", "ctx"), axis=0, tiled=True)
        full_out = lax.all_gather(w_out, ("dp", "ctx"), axis=0, tiled=True)
        self.full = [(full_in, full_out), (swap_core(full_in), swap_core(full_out))]
        self.grads = [{}, {}]

    def prepare_gate(self):
        pass

    def start_conv(self):
        return 0

    def start_gate(self, after):
        return 0

    def start_second(self):
        return 1, 1

    def trade_weights(self, layer):
        return layer

    def trade_grads(self, grads):
        return grads

    def send(self, traded):
        return traded

    def early(self, conv1, gate1, gate0):
        pass

    def early_trade(self):
        pass

    def late(self, conv0):
        pass

    def late_trade(self):
        pass

    def group(self, columns, block):
        return lax.dynamic_index_in_dim(grouped(columns, block), self.place, 0, False)

    def layer(self, layer, which):
        return choose(self.mine == layer, self.full[0][which], self.full[1][which])

    def conv_weights(self, sp, layer):
        one = self.layer(layer, 0)
        values = self.group(one[:, INNER : 2 * INNER], self.block * HEAD)
        step = self.group(one[:, 2 * INNER + 2 * STATE :], self.block)
        shared = one[:, 2 * INNER : 2 * INNER + 2 * STATE]
        return jnp.concatenate([values, shared, pad_to(step, step.shape[0], 128)], 1)

    def gate_weights(self, sp, layer):
        one, out = self.layer(layer, 0), self.layer(layer, 1)
        wide = self.block * HEAD
        return self.group(one[:, :INNER], wide), self.group(out.T, wide).T

    def over_tokens(self, a, b):
        both = [dot(x, y, ATB) for x, y in zip(a, b)]
        return (both[0] + both[1]).astype(BF16)

    def grad_gate(self, sp, layer, normed, dgate, gated, u):
        out = self.over_tokens(gated, u)
        self.grads[layer].update(gate=self.over_tokens(normed, dgate), out=out)
        return [out]

    def grad_conv(self, sp, layer, normed, dconv):
        self.grads[layer].update(conv=self.over_tokens(normed, dconv))
        return [self.grads[layer]["conv"]]

    def spread(self, columns, block):
        at = lax.broadcasted_iota(jnp.int32, (CTX, 1, 1), 0) == self.place
        return ungrouped(jnp.where(at, columns[None], jnp.zeros((), columns.dtype)), block)

    def gradients(self):
        wide = self.block * HEAD
        fulls = []
        for grads in self.grads:
            gate, conv = grads["gate"], grads["conv"]
            grad_in = jnp.concatenate(
                [
                    self.spread(gate, wide),
                    self.spread(conv[:, :WIDE], wide),
                    conv[:, WIDE:MIX],
                    self.spread(conv[:, MIX : MIX + LOCAL], self.block),
                ],
                -1,
            )
            fulls.append((grad_in, self.spread(grads["out"].T, wide).T))
        sums = []
        for a, b in zip(*fulls):
            zero = self.mine == 0
            total = choose(zero, a, b).astype(F32) + swap_core(choose(zero, b, a)).astype(F32)
            total = total.astype(BF16)
            sums.append(
                lax.psum_scatter(total, ("dp", "ctx"), scatter_dimension=0, tiled=True).astype(F32)
            )
        return sums[0], sums[1]


def prepare_kernel(block, sp, norm_ref, taps_ref, bias_ref, dt_ref, log_ref, skip_ref, gain_ref, out_ref):
    out_ref[...] = jnp.zeros_like(out_ref)
    for k in range(CTX):

        @pl.when(sp[0] == k)
        def _():
            for here, there, n in spans(k, block):
                out_ref[0:CONV, here : here + n] = taps_ref[0, :, there : there + n]
                out_ref[4:5, here : here + n] = bias_ref[:, there : there + n]
                out_ref[9:10, here : here + n] = gain_ref[:, there : there + n]
            spare = jnp.zeros((1, 128 - HEADS), F32)
            rows = [jnp.concatenate([ref[...], spare], axis=1) for ref in (dt_ref, log_ref, skip_ref)]
            rows = jnp.concatenate(rows + [jnp.zeros((5, 128), F32)])
            local = dot(rows, head_map(k, block, True), AB, HIGH)
            out_ref[10:11, 0:128] = local[0:1, :]
            out_ref[11:12, 0:128] = jnp.exp(local[1:2, :])
            out_ref[5:6, :WIDE] = dot(local, channel_map(True), AB, HIGH)[2:3, :]

    out_ref[0:CONV, WIDE:MIX] = taps_ref[0, :, INNER:]
    out_ref[4:5, WIDE:MIX] = bias_ref[:, INNER:]
    out_ref[8:9, :] = norm_ref[...]


def prepare(sp, block, arrays):
    out = shape((16, arrays[0].shape[1]), F32)
    return call("prepare", functools.partial(prepare_kernel, block), sp, arrays, [out], 12)[0]


def gather_small_kernel(counts, sp, *refs):
    keep_ref, send_ref = refs[-2:]
    packed, at = [], 0
    for layer in range(2):
        sums = []
        for count in counts[layer]:
            sums.append(sum(ref[...] for ref in refs[at : at + count]))
            at += count
        dcw, dhp, dgain, dnorm = sums
        tall = lax.broadcasted_iota(jnp.int32, (8, MIX), 0)
        gain = jnp.concatenate([dgain, jnp.zeros((8, MIX - WIDE), F32)], axis=1)
        short = dnorm.shape[1] - MIX
        norm_rest = jnp.concatenate([dnorm[:, MIX:], jnp.zeros((8, MIX - short), F32)], axis=1)
        middle = jnp.where(tall == 0, gain, jnp.where(tall == 1, dnorm[:, :MIX], norm_rest))
        heads = jnp.concatenate([dhp, jnp.zeros((8, MIX - 128), F32)], axis=1)
        packed.append(jnp.concatenate([dcw, middle, heads]))
    zero = sp[1] == 0
    keep_ref[...] = choose(zero, packed[0], packed[1])
    send_ref[...] = choose(zero, packed[1], packed[0])


def gather_small(sp, small):
    counts = [[len(kind) for kind in layer] for layer in small]
    arrays = [x for layer in small for kind in layer for x in kind]
    out = shape((PACK, MIX), F32)
    kernel = functools.partial(gather_small_kernel, counts)
    return call("gather_small", kernel, sp, arrays, [out, out], 12)


def spread_small_kernel(block, sp, *refs):
    slots, all_slots = refs[:CTX], refs[-1]
    norm_ref, taps_ref, bias_ref, dt_ref, log_ref, skip_ref, gain_ref = refs[CTX:-1]
    for m in range(CTX):
        all_slots[m ^ sp[0]] = slots[m][...]
    total = sum(all_slots[k] for k in range(CTX))
    norm_ref[:, :MIX] = total[9:10, :]
    norm_ref[:, MIX:] = total[10:11, : norm_ref.shape[1] - MIX]
    taps_ref[0, :, INNER:] = total[0:CONV, WIDE:]
    bias_ref[:, INNER:] = total[4:5, WIDE:]
    pick = channel_map()
    heads = 0.0
    for k in range(CTX):
        for here, there, n in spans(k, block):
            taps_ref[0, :, there : there + n] = all_slots[k, 0:CONV, here : here + n]
            bias_ref[:, there : there + n] = all_slots[k, 4:5, here : here + n]
            gain_ref[:, there : there + n] = all_slots[k, 8:9, here : here + n]
        skip = dot(all_slots[k, 0:8, :WIDE], pick, AB, HIGH)
        both = jnp.concatenate([all_slots[k, 16:24, :128], skip])
        heads = heads + dot(both, head_map(k, block), AB, HIGH)
    dt_ref[...] = heads[0:1, :HEADS]
    log_ref[...] = heads[1:2, :HEADS]
    skip_ref[...] = heads[13:14, :HEADS]


def spread_small(sp, block, slots, d):
    one = shape((1, HEADS), F32)
    return call(
        "spread_small",
        functools.partial(spread_small_kernel, block),
        sp,
        slots,
        [
            shape((1, d), F32),
            shape((1, CONV, CONV_DIM), F32),
            shape((1, CONV_DIM), F32),
            one,
            one,
            one,
            shape((1, INNER), F32),
        ],
        12,
        scratch=[pltpu.VMEM((CTX, PACK, MIX), F32)],
    )


def sum_over_dp(x, dp, step, end):
    if dp & (dp - 1):
        return lax.psum(x, "dp") if step == 1 else x
    while step < end:
        x = x + lax.ppermute(x, "dp", [(i, i ^ step) for i in range(dp)])
        step *= 2
    return x


class Order:
    def __init__(self, sp):
        self.sp = sp

    def __call__(self, kernel, *args):
        out = kernel(self.sp, *args)
        self.after(out[0] if isinstance(out, (list, tuple)) else out)
        return out

    def after(self, x):
        self.sp, _ = lax.optimization_barrier((self.sp, x))

    def now(self, x):
        return lax.optimization_barrier((x, self.sp))[0]


def shards(
    tokens,
    cotangent,
    doc_lengths,
    norm_gain,
    w_in,
    conv_weight,
    conv_bias,
    dt_bias,
    a_log,
    d_skip,
    inner_gain,
    w_out,
):
    mine, place = lax.axis_index("section"), lax.axis_index("ctx")
    dp = lax.axis_size("dp")
    piece, d = tokens.shape[2], tokens.shape[3]
    seg_len = piece * CTX // SEGS
    direct = dp == 4 and w_out.shape[1] % HEAD == 0 and w_out.shape[1] * dp == WIDE
    block = w_out.shape[1] // HEAD if direct else LOCAL

    own_x = lax.dynamic_index_in_dim(tokens, mine, 0, False)[0]
    own_u = lax.dynamic_index_in_dim(cotangent, mine, 0, False)[0]
    lengths = lax.dynamic_index_in_dim(doc_lengths, mine, 0, False)[0]
    start = jnp.stack([place, mine, lax.axis_index("dp")]).astype(jnp.int32)
    sp = jnp.concatenate([start, jnp.cumsum(lengths) - lengths])
    run = Order(sp)
    if direct:
        carrier = Direct(run, mine, dp, block, w_in[0], w_out[0])
    else:
        carrier = Plain(mine, place, block, w_in[0], w_out[0])

    def natural(slots):
        return jnp.concatenate(slots).reshape(CTX, 2, piece // 2, d)

    rows_x = gather_slots(run, run.now(own_x))
    arrays = [norm_gain, conv_weight, conv_bias, dt_bias, a_log, d_skip, inner_gain]
    params = run(prepare, block, arrays)
    other = swap_core(params)
    params = [choose(mine == 0, params, other), choose(mine == 0, other, params)]
    carrier.prepare_gate()
    rows_x = natural(rows_x())
    conv0 = carrier.start_conv()
    run.after(rows_x)
    gate0 = carrier.start_gate(conv0)
    conv0 = carrier.trade_weights(conv0)
    rows_u = gather_slots(run, run.now(own_u))
    no_state, no_tail = jnp.zeros((STATE, WIDE), F32), jnp.zeros((16, MIX), BF16)

    def forward(layer, s, pieces, wc, state, tail, between=None):
        normed, conv_in, step_raw = run(project, pieces, params[layer], wc, seg_len)
        if between is not None:
            between()
        y, states, state, next_tail = run(
            scan_rows, s, conv_in, step_raw, params[layer], state, tail
        )
        return dict(
            normed=normed, conv_in=conv_in, step_raw=step_raw, y=y, states=states, tail=tail
        ), state, next_tail

    wc0 = run(carrier.conv_weights, conv0)
    conv1, gate1 = carrier.start_second()
    first, second = [None, None], [None, None]
    state, tail = no_state, no_tail
    first[0], state, tail = forward(0, 0, natural_slots(rows_x, 0), wc0, state, tail)
    first[1], state, tail = forward(0, 1, natural_slots(rows_x, 1), wc0, state, tail)
    rows_u = rows_u()
    gate0 = carrier.trade_weights(gate0)
    wg0, wo0 = run(carrier.gate_weights, gate0)
    stats, sums = [None, None], [None, None]
    for s in range(SEGS):
        saved = first[s]
        saved["gate"], stats[s], *sums[s] = run(
            out_rows, True, [], [], saved["normed"], saved["y"], params[0], wg0, wo0
        )
        if s == 0:
            sums[0] = scatter_start(*sums[0])

    def own_step(s):
        residual = natural_slots(rows_x, s)[:1]
        first[s]["stats"] = [stats[s]] + [tail_tile(x) for x in sums[s][1:4]]
        own, first[s]["branch"] = run(own_rows, False, first[s]["stats"], sums[s], residual)
        first[s]["own"] = own
        return gather_slots(run, own)

    sums[0] = scatter_slots(run, *sums[0])
    sums[1] = scatter_start(*[run.now(x) for x in sums[1]])
    middle = [own_step(0), None]
    sums[1] = scatter_slots(run, *sums[1])
    middle[0] = middle[0]()
    rows_u = natural(rows_u)
    run.after(rows_u)

    conv1 = carrier.trade_weights(conv1)
    wc1 = run(carrier.conv_weights, conv1)
    middle[1] = own_step(1)
    state, tail = no_state, no_tail
    parts, before = [], []

    def last_rows():
        middle[1] = middle[1]()

    for s in range(SEGS):
        between = last_rows if s == 0 else None
        second[s], state, tail = forward(1, s, middle[s], wc1, state, tail, between)
        if s == 0:
            run.after(middle[1][3:])
            gate1 = carrier.trade_weights(gate1)
    wg1, wo1 = run(carrier.gate_weights, gate1)
    for s in range(SEGS):
        saved = second[s]
        saved["gate"], stats, part = run(
            out_rows,
            False,
            before,
            natural_slots(rows_u, s),
            saved["normed"],
            saved["y"],
            params[1],
            wg1,
            wo1,
        )
        before = [stats]
        parts.append(part)
    stats = from_all(stats)
    part1 = run(collect, parts)
    hidden0 = run(natural_rows, middle)

    def gate_step(layer, s, saved, pieces, stats, first_stat, inners, wo):
        out = run(
            gate_back, pieces, stats, first_stat, inners, saved["y"], saved["gate"], params[layer], wo
        )
        saved.update(zip(("dy", "dgate", "gated", "u", "dgain"), out))

    def scan_step(layer, s, saved, dstate, later):
        saved["dconv"], saved["dcw"], saved["dhp"], dstate, later = run(
            scan_back,
            layer == 0,
            s,
            saved["conv_in"],
            saved["step_raw"],
            saved["dy"],
            saved["states"],
            saved["tail"],
            params[layer],
            dstate,
            later,
        )
        return dstate, later

    def of(saved, *names):
        return [[one[name] for one in saved] for name in names]

    def back_start(s):
        saved = second[s]
        return scatter_start(*run(input_back, True, saved["dconv"], saved["dgate"], wc1, wg1))

    def back_end(s, part):
        up, second[s]["dnorm"] = run(
            own_back,
            16,
            part,
            [far(first[s]["own"])],
            natural_slots(rows_u, s)[:1],
            params[1],
            far(first[s]["branch"]),
        )
        return gather_slots(run, up, 16)

    upper = [None, None]

    def lower_gate(s):
        inners = [head_tile(x) for x in upper[s][:4]]
        gate_step(0, s, first[s], upper[s], first[s]["stats"], 0, inners, wo0)

    for s in (1, 0):
        gate_step(1, s, second[s], natural_slots(rows_u, s), stats, 8 * s, [], wo1)
    gate1 = carrier.trade_grads(run(carrier.grad_gate, 1, *of(second, "normed", "dgate", "gated", "u")))
    part1 = scatter_start(*part1)
    dstate, later = no_state, jnp.zeros((8, MIX), F32)
    dstate, later = scan_step(1, 1, second[1], dstate, later)
    part1 = scatter_slots(run, *part1)
    gate1 = carrier.send(gate1)
    upper[1] = back_start(1)
    dstate, later = scan_step(1, 0, second[0], dstate, later)
    hidden1, _ = run(own_rows, True, stats, part1, [hidden0])
    upper[1] = scatter_slots(run, *upper[1])
    upper[0] = back_start(0)
    upper[1] = back_end(1, upper[1])
    conv1 = run(carrier.grad_conv, 1, *of(second, "normed", "dconv"))
    upper[1] = upper[1]()
    upper[0] = scatter_slots(run, *upper[0])
    conv1 = carrier.trade_grads([run.now(x) for x in conv1])
    lower_gate(1)
    conv1 = carrier.send(conv1)
    upper[0] = back_end(0, upper[0])
    dstate, later = no_state, jnp.zeros((8, MIX), F32)
    dstate, later = scan_step(0, 1, first[1], dstate, later)
    upper[0] = upper[0]()
    lower_gate(0)
    gate0 = carrier.trade_grads(run(carrier.grad_gate, 0, *of(first, "normed", "dgate", "gated", "u")))
    (part_1,) = run(input_back, False, first[1]["dconv"], first[1]["dgate"], wc0, wg0)
    gate0 = carrier.send(gate0)
    dstate, later = scan_step(0, 0, first[0], dstate, later)
    conv0 = carrier.trade_grads(run(carrier.grad_conv, 0, *of(first, "normed", "dconv")))
    (part_0,) = run(input_back, False, first[0]["dconv"], first[0]["dgate"], wc0, wg0)
    conv0 = carrier.send(conv0)
    part = scatter_start(*run(collect, [far(part_0), far(part_1)]))
    grads1 = run(natural_rows, upper, 16)
    part = scatter_slots(run, *part)
    carrier.early(conv1, gate1, gate0)
    branch = jnp.zeros((piece, d), F32)
    grads0, dnorm0 = run(own_back, 0, part, [own_x], [grads1], params[0], branch)
    carrier.early_trade()
    small = [
        of(first, "dcw", "dhp", "dgain") + [[dnorm0]],
        of(second, "dcw", "dhp", "dgain", "dnorm"),
    ]
    keep, small_sent = run(gather_small, small)
    total = sum_over_dp(keep + swap_core(small_sent), dp, 1, dp)
    carrier.late(conv0)
    carrier.late_trade()
    total = from_all(run.now(total))
    shard_in, shard_out = carrier.gradients()
    norm, taps, bias, dt, log, skip, gain = run(spread_small, block, total, d)

    def to_layers(a, b):
        here, there = choose(mine == 0, a, b), swap_core(choose(mine == 0, b, a))
        both = jnp.stack([choose(mine == 0, here, there), choose(mine == 0, there, here)])
        return both[None, :, None]

    return (
        to_layers(hidden0, hidden1),
        to_layers(grads0, grads1),
        norm,
        shard_in[None],
        taps,
        bias,
        dt,
        log,
        skip,
        gain,
        shard_out[None],
    )


def solution(mesh):
    in_specs = (
        P(None, "dp", "ctx", None),
        P(None, "dp", "ctx", None),
        P(None, "dp", None),
        P("section", None),
        P("section", ("dp", "ctx"), None),
        P("section", None, None),
        P("section", None),
        P("section", None),
        P("section", None),
        P("section", None),
        P("section", None),
        P("section", ("dp", "ctx"), None),
    )
    out_specs = (
        P("section", None, "dp", "ctx", None),
        P("section", None, "dp", "ctx", None),
        P("section", None),
        P("section", ("dp", "ctx"), None),
        P("section", None, None),
        P("section", None),
        P("section", None),
        P("section", None),
        P("section", None),
        P("section", None),
        P("section", ("dp", "ctx"), None),
    )
    return jax.shard_map(shards, mesh=mesh, in_specs=in_specs, out_specs=out_specs, check_vma=False)
```
